128 devices in a mesh: seg: 16 (over y, x), blk: 8 (over z, core).
Axes of the slice: x: 4, y: 4, z: 4, core: 2. Of those that a mesh axis runs over, the one named last changes fastest.
Arguments:
- tokens: bfloat16 [128, 512, 768], P('seg', 'blk'), may hold values from -6 to 6
- memory: bfloat16 [128, 20, 768], P('seg'), may hold values from -6 to 6
- mem_init: bfloat16 [20, 768], replicated, may hold values from -6 to 6
- reset_flags: int32 [128], P('seg'), may hold values 0 or 1
- doc_ids: int32 [128, 512], P('seg'), may hold values from 0 to 2, as said below
- w_qkv: bfloat16 [768, 2304], replicated, may hold values from -0.21875 to 0.21875
- b_query: bfloat16 [768], replicated, may hold values from -3 to 3
- b_value: bfloat16 [768], replicated, may hold values from -3 to 3
- w_out: bfloat16 [768, 768], replicated, may hold values from -3.5 to 3.5
- b_out: bfloat16 [768], replicated, may hold values from -2 to 2
- norm1_gain: bfloat16 [768], replicated, may hold values from 0.099609375 to 1.8984375
- norm1_bias: bfloat16 [768], replicated, may hold values from -2 to 2
- w_in: bfloat16 [768, 3072], replicated, may hold values from -0.21875 to 0.21875
- b_in: bfloat16 [3072], replicated, may hold values from -3 to 3
- w_down: bfloat16 [3072, 768], replicated, may hold values from -0.109375 to 0.109375
- b_down: bfloat16 [768], replicated, may hold values from -2 to 2
- norm2_gain: bfloat16 [768], replicated, may hold values from 0.099609375 to 1.8984375
- norm2_bias: bfloat16 [768], replicated, may hold values from -2 to 2
- out_cot: bfloat16 [128, 512, 768], P('seg', 'blk'), may hold values from -6 to 6
- mem_cot: bfloat16 [128, 20, 768], P('seg'), may hold values from -6 to 6
Outputs:
- output: bfloat16 [128, 512, 768], P('seg', 'blk')
- mem_output: bfloat16 [128, 20, 768], P('seg')
- grad_tokens: bfloat16 [128, 512, 768], P('seg', 'blk')
- grad_memory: bfloat16 [128, 20, 768], P('seg')
- grad_mem_init: float32 [20, 768], replicated
- grad_w_qkv: float32 [768, 2304], replicated
- grad_b_query: float32 [768], replicated
- grad_b_value: float32 [768], replicated
- grad_w_out: float32 [768, 768], replicated
- grad_b_out: float32 [768], replicated
- grad_norm1_gain: float32 [768], replicated
- grad_norm1_bias: float32 [768], replicated
- grad_w_in: float32 [768, 3072], replicated
- grad_b_in: float32 [3072], replicated
- grad_w_down: float32 [3072, 768], replicated
- grad_b_down: float32 [768], replicated
- grad_norm2_gain: float32 [768], replicated
- grad_norm2_bias: float32 [768], replicated
The draws below stay inside these ranges and needn't reach their ends.
Inputs may be any that keep to these rules, and one draw needn't show every extreme that they name: `doc_ids`: within a segment the numbers never fall and take the values 0, 1 and 2; document 1 starts before position 64 and ends at or after position 448.
All inputs are finite; a program needn't handle non-finite values. No bound on the sum of `reset_flags` on one device may be relied on, other than what follows from the above.
Results may differ from the reference program's by a relative error of at most 0.028.
Values may be sent and summed in bfloat16 or wider, within the bound.
No kernel may reach another device: no remote copies, remote signals or barrier semaphores. Data moves between devices by JAX's collectives and lax.ppermute only.
A program may use at most 256 MiB of HBM per device.

```python
import jax
import jax.numpy as jnp
from jax import lax

D = 768
HEADS = 12
HEAD_DIM = 64
FF = 3072
MEM = 20
SEG_LEN = 512
TOK_DEV = 64
SEGS = 128


def draw_doc_ids(key, part):
    key = jax.random.fold_in(key, 11)
    first_key, second_key = jax.random.split(key)
    first_cut = jax.random.randint(first_key, (SEGS, 1), 1, TOK_DEV)
    second_cut = jax.random.randint(second_key, (SEGS, 1), SEG_LEN - TOK_DEV + 1, SEG_LEN)
    places = jnp.arange(SEG_LEN, dtype=jnp.int32)[None, :]
    return ((places >= first_cut).astype(jnp.int32) + (places >= second_cut).astype(jnp.int32)).astype(jnp.int32)


def place_ends(values, own_key, least, top_value):
    longest = values.shape.index(max(values.shape))
    spots = []
    for shift in (0, 1):
        where = [jax.random.randint(jax.random.fold_in(own_key, axis), (), 0, length) for axis, length in enumerate(values.shape)]
        where[longest] = (where[longest] + shift) % values.shape[longest]
        spots.append(tuple(where))
    return values.at[spots[0]].set(least).at[spots[1]].set(top_value)


def steps_of(key, shape, cuts, low, top_value):
    factor_of, own = 1.0, jax.random.fold_in(key, 6)
    for position, shards_of in cuts:
        draws = jnp.exp(jax.random.uniform(jax.random.fold_in(own, position), (shards_of,), jnp.float32, low / len(cuts), top_value / len(cuts)))
        factor_of = factor_of * jnp.repeat(draws, shape[position] // shards_of).reshape([-1 if axis == position else 1 for axis in range(len(shape))])
    return factor_of


def gaussian(key, extent, deviation, reach, cuts=(), kind=jnp.bfloat16):
    array = deviation * jax.random.normal(key, extent, jnp.float32)
    if cuts:
        array = array * steps_of(key, extent, cuts, -0.22, 0.18)
    return jnp.clip(array, -reach, reach).astype(kind)


def setup_inputs(seed: int = 0) -> dict:
    key_list = jax.random.split(jax.random.key(seed), 21)
    tokens = gaussian(key_list[0], (SEGS, SEG_LEN, D), 1.0, 6.0, ((0, 16), (1, 8)))
    memory = gaussian(key_list[1], (SEGS, MEM, D), 1.0, 6.0, ((0, 16),))
    mem_init = gaussian(key_list[2], (MEM, D), 1.0, 6.0)
    reset_flags = place_ends((jax.random.randint(key_list[3], (SEGS,), 0, 4) < 1).astype(jnp.int32), jax.random.fold_in(key_list[3], 1), 0, 1)
    doc_ids = draw_doc_ids(jax.random.fold_in(key_list[20], 71), 0)
    w_qkv = gaussian(key_list[5], (D, 3 * D), D ** -0.5, 0.21875)
    b_query = gaussian(key_list[6], (D,), 0.5, 3.0)
    b_value = gaussian(key_list[7], (D,), 0.5, 3.0)
    w_out = gaussian(key_list[8], (D, D), (max(2, D * 2 // SEG_LEN)) ** -0.5, 3.5)
    b_out = gaussian(key_list[9], (D,), 0.3, 2.0)
    norm1_gain = jnp.clip(1.0 + 0.18 * jax.random.normal(key_list[10], (D,), jnp.float32), 0.099609375, 1.8984375).astype(jnp.bfloat16)
    norm1_bias = gaussian(key_list[11], (D,), 0.3, 2.0)
    w_in = gaussian(key_list[12], (D, FF), D ** -0.5, 0.21875)
    b_in = gaussian(key_list[13], (FF,), 0.5, 3.0)
    w_down = gaussian(key_list[14], (FF, D), FF ** -0.5, 0.109375)
    b_down = gaussian(key_list[15], (D,), 0.3, 2.0)
    norm2_gain = jnp.clip(1.0 + 0.18 * jax.random.normal(key_list[16], (D,), jnp.float32), 0.099609375, 1.8984375).astype(jnp.bfloat16)
    norm2_bias = gaussian(key_list[17], (D,), 0.3, 2.0)
    out_cot = gaussian(key_list[18], (SEGS, SEG_LEN, D), 1.0, 6.0, ((0, 16), (1, 8)))
    mem_cot = gaussian(key_list[19], (SEGS, MEM, D), 1.0, 6.0, ((0, 16),))
    return dict(tokens=tokens, memory=memory, mem_init=mem_init, reset_flags=reset_flags, doc_ids=doc_ids, w_qkv=w_qkv, b_query=b_query, b_value=b_value, w_out=w_out, b_out=b_out, norm1_gain=norm1_gain, norm1_bias=norm1_bias, w_in=w_in, b_in=b_in, w_down=w_down, b_down=b_down, norm2_gain=norm2_gain, norm2_bias=norm2_bias, out_cot=out_cot, mem_cot=mem_cot)


EPS = 1e-12
FLOOR = -1000000000.0

@jax.custom_vjp
def low(v):
    return lax.optimization_barrier(v.astype(jnp.bfloat16)).astype(jnp.float32)

@jax.custom_vjp
def low_back(v):
    return v

def low_keep(v):
    return (low(v), None)

def low_pass(kept, grad):
    return (grad,)

def back_keep(v):
    return (v, None)

def back_low(kept, grad):
    return (low(grad),)
low.defvjp(low_keep, low_pass)
low_back.defvjp(back_keep, back_low)

def normalize(value):
    centre = lax.optimization_barrier(jnp.mean(value, axis=-1, keepdims=True))
    centered = value - centre
    spread = lax.optimization_barrier(jnp.mean(centered * centered, axis=-1, keepdims=True))
    return centered * lax.rsqrt(spread + EPS)

def block_forward(all_rows, seg_docs, w_qkv, b_query, b_value, w_out, b_out, norm1_gain, norm1_bias, w_in, b_in, w_down, b_down, norm2_gain, norm2_bias):
    exact_mode = lax.Precision.HIGHEST
    row_count = all_rows.shape[0]
    score_scale = HEAD_DIM ** (-0.5)
    rows_low = low(all_rows)
    qkv_rows = low_back(jnp.dot(rows_low, w_qkv, precision=exact_mode))
    query_low = low(qkv_rows[:, :D] + b_query)
    key_low = low(qkv_rows[:, D:2 * D])
    value_low = low(qkv_rows[:, 2 * D:] + b_value)
    query_heads = query_low.reshape(row_count, HEADS, HEAD_DIM)
    key_heads = key_low.reshape(row_count, HEADS, HEAD_DIM)
    value_heads = value_low.reshape(row_count, HEADS, HEAD_DIM)
    scores = low_back(jnp.einsum('qhd,khd->hqk', query_heads, key_heads, precision=exact_mode) * score_scale)
    mem_marks = jnp.full((MEM,), -1, jnp.int32)
    query_docs = jnp.concatenate([mem_marks, seg_docs.astype(jnp.int32)])
    key_docs = jnp.concatenate([mem_marks - 1, seg_docs.astype(jnp.int32)])
    allowed = (query_docs[:, None] == key_docs[None, :]) | (query_docs[:, None] < 0) | (key_docs[None, :] < 0)
    probs_low = low(jax.nn.softmax(jnp.where(allowed[None], scores, FLOOR), axis=-1))
    attended = jnp.einsum('hqk,khd->qhd', probs_low, value_heads, precision=exact_mode).reshape(row_count, D)
    attended_low = low(low_back(attended))
    resid_one = all_rows + low_back(jnp.dot(attended_low, w_out, precision=exact_mode)) + b_out
    hidden_one = normalize(resid_one) * norm1_gain + norm1_bias
    hidden_low = low(hidden_one)
    inner = low_back(jnp.dot(hidden_low, w_in, precision=exact_mode)) + b_in
    activated_low = low(jax.nn.gelu(inner, approximate=False))
    resid_two = hidden_one + low_back(jnp.dot(activated_low, w_down, precision=exact_mode)) + b_down
    return normalize(resid_two) * norm2_gain + norm2_bias

def widen(value):
    return value.astype(jnp.float32)

def reference(tokens, memory, mem_init, reset_flags, doc_ids, w_qkv, b_query, b_value, w_out, b_out, norm1_gain, norm1_bias, w_in, b_in, w_down, b_down, norm2_gain, norm2_bias, out_cot, mem_cot):
    params = tuple((widen(p) for p in (mem_init, w_qkv, b_query, b_value, w_out, b_out, norm1_gain, norm1_bias, w_in, b_in, w_down, b_down, norm2_gain, norm2_bias)))

    def one_segment(carry, item):
        seg_tokens, seg_memory, seg_flag, seg_docs, cot_tokens, cot_memory = item

        def forward(tok_rows, mem_rows, *weights):
            start_rows = jnp.where(seg_flag == 1, weights[0], mem_rows)
            all_rows = jnp.concatenate([start_rows, tok_rows], axis=0)
            result = block_forward(all_rows, seg_docs, *weights[1:])
            return (result[MEM:], result[:MEM])
        outputs, backward = jax.vjp(forward, widen(seg_tokens), widen(seg_memory), *params)
        grads = backward((widen(cot_tokens), widen(cot_memory)))
        carry = tuple((total + grad for total, grad in zip(carry, grads[2:])))
        return (carry, (outputs[0].astype(jnp.bfloat16), outputs[1].astype(jnp.bfloat16), grads[0].astype(jnp.bfloat16), grads[1].astype(jnp.bfloat16)))
    start = tuple((jnp.zeros(p.shape, jnp.float32) for p in params))
    totals, per_seg = lax.scan(one_segment, start, (tokens, memory, reset_flags, doc_ids, out_cot, mem_cot))
    return (per_seg[0], per_seg[1], per_seg[2], per_seg[3], totals[0], totals[1], totals[2], totals[3], totals[4], totals[5], totals[6], totals[7], totals[8], totals[9], totals[10], totals[11], totals[12], totals[13])
```

```python
import jax
import jax.numpy as jnp
from jax import lax
from jax.sharding import Mesh, PartitionSpec as P

HEADS = 12

EPS = 1e-12
FLOOR = -1000000000.0

F32 = jnp.float32
BF16 = jnp.bfloat16
BLK = ("z", "core")
SEG = ("y", "x")
ALL = ("y", "x", "z", "core")


def norm_parts(value):
    centre = jnp.mean(value, axis=-1, keepdims=True)
    centered = value - centre
    spread = jnp.mean(centered * centered, axis=-1, keepdims=True)
    scale = lax.rsqrt(spread + EPS)
    return centered * scale, scale


def norm_back(grad, normal, scale):
    mean_grad = jnp.mean(grad, axis=-1, keepdims=True)
    mean_prod = jnp.mean(grad * normal, axis=-1, keepdims=True)
    return scale * (grad - mean_grad - normal * mean_prod)


def dot(left, right):
    return jnp.dot(left, right, preferred_element_type=F32)


def dot_nt(left, right):
    return lax.dot_general(left, right, (((1,), (1,)), ((), ())), preferred_element_type=F32)


def dot_tn(left, right):
    return lax.dot_general(left, right, (((0,), (0,)), ((), ())), preferred_element_type=F32)


def to_segments(value):
    return lax.all_to_all(value, BLK, 0, 1, tiled=True)[0]


def to_blocks(value, seg_count):
    parts = value.reshape(seg_count, value.shape[0] // seg_count, value.shape[1])
    return lax.all_to_all(parts, BLK, 0, 0, tiled=True)


def heads(value):
    return value.reshape(value.shape[0], HEADS, -1).transpose(1, 0, 2)


def unheads(value):
    return value.transpose(1, 0, 2).reshape(value.shape[1], -1)


def local(
    tokens,
    memory,
    mem_init,
    reset_flags,
    doc_ids,
    w_qkv,
    b_query,
    b_value,
    w_out,
    b_out,
    norm1_gain,
    norm1_bias,
    w_in,
    b_in,
    w_down,
    b_down,
    norm2_gain,
    norm2_bias,
    out_cot,
    mem_cot,
):
    seg_count, tok_count, width = tokens.shape
    mem_count = memory.shape[1]
    score_scale = (width // HEADS) ** (-0.5)
    place = lax.axis_index(BLK)
    pick = lambda value: lax.dynamic_index_in_dim(value, place, 0, keepdims=False)
    my_flag = pick(reset_flags) == 1
    my_docs = pick(doc_ids)
    mem_rows = jnp.where(my_flag, mem_init, pick(memory))
    rows = jnp.concatenate([to_segments(tokens), mem_rows], axis=0)
    cot = jnp.concatenate([to_segments(out_cot), pick(mem_cot)], axis=0).astype(F32)

    text_count = rows.shape[0] - mem_count
    qkv = dot(rows, w_qkv)
    query = heads((qkv[:, :width] + b_query.astype(F32)).astype(BF16))
    key = heads(qkv[:, width : 2 * width].astype(BF16))
    value = heads((qkv[:, 2 * width :] + b_value.astype(F32)).astype(BF16))
    query_docs = jnp.concatenate([my_docs, jnp.full((mem_count,), -1, jnp.int32)])
    allowed = (
        (query_docs[:, None] == query_docs[None, :])
        | (query_docs[:, None] < 0)
        | (query_docs[None, :] < 0)
    )[None]
    scores = jnp.einsum("hqd,hkd->hqk", query, key, preferred_element_type=F32) * score_scale
    masked = jnp.where(allowed, scores, FLOOR)
    top = jnp.max(masked, axis=-1, keepdims=True)
    raised = jnp.exp(masked - top)
    total = jnp.sum(raised, axis=-1, keepdims=True)
    probs = raised / total
    probs_low = probs.astype(BF16)
    attended = unheads(
        jnp.einsum("hqk,hkd->hqd", probs_low, value, preferred_element_type=F32).astype(BF16)
    )
    resid_one = rows.astype(F32) + dot(attended, w_out) + b_out.astype(F32)
    norm_one, scale_one = norm_parts(resid_one)
    hidden = norm_one * norm1_gain.astype(F32) + norm1_bias.astype(F32)
    hidden_low = hidden.astype(BF16)
    inner = dot(hidden_low, w_in) + b_in.astype(F32)
    phi = 0.5 * (1.0 + lax.erf(inner * (0.5**0.5)))
    activated = (inner * phi).astype(BF16)
    slope = phi + inner * jnp.exp(-0.5 * inner * inner) * 0.3989422804014327
    resid_two = hidden + dot(activated, w_down) + b_down.astype(F32)
    norm_two, scale_two = norm_parts(resid_two)
    result = (norm_two * norm2_gain.astype(F32) + norm2_bias.astype(F32)).astype(BF16)
    output = to_blocks(result[:text_count], seg_count)
    mem_output = lax.all_gather(result[text_count:], BLK, axis=0)

    grad_gain2 = jnp.sum(cot * norm_two, axis=0)
    grad_bias2 = jnp.sum(cot, axis=0)
    g_two = norm_back(cot * norm2_gain.astype(F32), norm_two, scale_two)
    grad_bdown = jnp.sum(g_two, axis=0)
    g_two_low = g_two.astype(BF16)
    grad_wdown = dot_tn(activated, g_two_low).astype(BF16)
    grad_wdown = lax.psum(grad_wdown, ALL)
    g_inner = dot_nt(g_two_low, w_down) * slope
    grad_bin = jnp.sum(g_inner, axis=0)
    g_inner_low = g_inner.astype(BF16)
    grad_win = dot_tn(hidden_low, g_inner_low).astype(BF16)
    grad_wdown, grad_win = lax.optimization_barrier((grad_wdown, grad_win))
    grad_win = lax.psum(grad_win, ALL)
    g_hidden = g_two + dot_nt(g_inner_low, w_in)
    grad_gain1 = jnp.sum(g_hidden * norm_one, axis=0)
    grad_bias1 = jnp.sum(g_hidden, axis=0)
    g_one = norm_back(g_hidden * norm1_gain.astype(F32), norm_one, scale_one)
    grad_bout = jnp.sum(g_one, axis=0)
    g_one_low = g_one.astype(BF16)
    grad_wout = dot_tn(attended, g_one_low).astype(BF16)
    g_att = heads(dot_nt(g_one_low, w_out).astype(BF16))
    g_probs = jnp.einsum("hqd,hkd->hqk", g_att, value, preferred_element_type=F32)
    delta = jnp.sum(probs * g_probs, axis=-1, keepdims=True)
    g_scores = (probs * (g_probs - delta)).astype(BF16)
    g_query = jnp.einsum("hqk,hkd->hqd", g_scores, key, preferred_element_type=F32) * score_scale
    g_key = jnp.einsum("hqk,hqd->hkd", g_scores, query, preferred_element_type=F32) * score_scale
    g_value = jnp.einsum("hqk,hqd->hkd", probs_low, g_att, preferred_element_type=F32)
    g_query, g_value = unheads(g_query), unheads(g_value)
    grad_bquery = jnp.sum(g_query, axis=0)
    grad_bvalue = jnp.sum(g_value, axis=0)
    g_qkv = jnp.concatenate(
        [g_query.astype(BF16), unheads(g_key).astype(BF16), g_value.astype(BF16)], axis=1
    )
    grad_wqkv = dot_tn(rows, g_qkv).astype(BF16)
    g_rows = g_one + dot_nt(g_qkv, w_qkv)
    grad_tokens = to_blocks(g_rows[:text_count].astype(BF16), seg_count)
    grad_mem = g_rows[text_count:]
    grad_memory = lax.all_gather(jnp.where(my_flag, 0.0, grad_mem).astype(BF16), BLK, axis=0)
    grad_init = jnp.where(my_flag, grad_mem, 0.0)
    small = jnp.concatenate(
        [
            grad_init.reshape(-1),
            grad_bquery,
            grad_bvalue,
            grad_bout,
            grad_gain1,
            grad_bias1,
            grad_bin,
            grad_bdown,
            grad_gain2,
            grad_bias2,
        ]
    )
    tail = jnp.concatenate([grad_wout, small.astype(BF16).reshape(-1, width)], axis=0)
    grad_win, grad_wqkv, tail = lax.optimization_barrier((grad_win, grad_wqkv, tail))
    grad_wqkv, tail = lax.psum((grad_wqkv, tail), ALL)
    grad_wout = tail[:width]
    small = tail[width:].astype(F32).reshape(-1)
    sizes = [mem_count * width] + [width] * 5 + [w_in.shape[1]] + [width] * 3
    pieces, start = [], 0
    for size in sizes:
        pieces.append(small[start : start + size])
        start += size
    return (
        output,
        mem_output,
        grad_tokens,
        grad_memory,
        pieces[0].reshape(mem_count, width),
        grad_wqkv.astype(F32),
        pieces[1],
        pieces[2],
        grad_wout.astype(F32),
        pieces[3],
        pieces[4],
        pieces[5],
        grad_win.astype(F32),
        pieces[6],
        grad_wdown.astype(F32),
        pieces[7],
        pieces[8],
        pieces[9],
    )


def solution(mesh):
    chips = Mesh(mesh.devices.reshape(4, 4, 4, 2), ALL)
    placed = (
        P(SEG, BLK, None),
        P(SEG, None, None),
        P(),
        P(SEG),
        P(SEG, None),
        *([P()] * 13),
        P(SEG, BLK, None),
        P(SEG, None, None),
    )
    return jax.shard_map(
        local,
        mesh=chips,
        in_specs=placed,
        out_specs=(
            P(SEG, BLK, None),
            P(SEG, None, None),
            P(SEG, BLK, None),
            P(SEG, None, None),
            *([P()] * 14),
        ),
        check_vma=False,
    )
```

```python
import jax
import jax.numpy as jnp
from jax import lax
from jax.experimental import pallas as pl
from jax.experimental.pallas import tpu as pltpu
from jax.sharding import Mesh, PartitionSpec as P

F32 = jnp.float32
BF16 = jnp.bfloat16
HEADS = 12
EPS = 1e-12
BAN = 2.0**30
VMEM_ASK = 60 * 1024 * 1024
BLK = ("z", "core")
SEG = ("y", "x")
ALL = ("y", "x", "z", "core")
XYZ = ("x", "y", "z")
CHIPS = 64
ROW_PAD = 12


def dot(left, right):
    return jnp.dot(left, right, preferred_element_type=F32)


def dot_nt(left, right):
    return lax.dot_general(left, right, (((1,), (1,)), ((), ())), preferred_element_type=F32)


def dot_tn(left, right):
    return lax.dot_general(left, right, (((0,), (0,)), ((), ())), preferred_element_type=F32)


def cost(micros):
    return pl.CostEstimate(flops=int(micros * 1e9), bytes_accessed=0, transcendentals=0)


def lanes_of(shape):
    return lax.broadcasted_iota(jnp.int32, shape, 1)


def split_three(value):
    high = value.astype(BF16)
    rest = value - high.astype(F32)
    middle = rest.astype(BF16)
    low = (rest - middle.astype(F32)).astype(BF16)
    return high, middle, low


def norm_parts(value):
    centre = jnp.mean(value, axis=-1, keepdims=True)
    centered = value - centre
    spread = jnp.mean(centered * centered, axis=-1, keepdims=True)
    scale = lax.rsqrt(spread + EPS)
    return centered * scale, scale


def norm_back(grad, normal, scale):
    mean_grad = jnp.mean(grad, axis=-1, keepdims=True)
    mean_prod = jnp.mean(grad * normal, axis=-1, keepdims=True)
    return scale * (grad - mean_grad - normal * mean_prod)


def attend_kernel(text, mem, w_q, w_k, w_v, lines, lines_all, mark_q, mark_k, w_out,
                  q_out, k_out, v_out, att_out, log_out, resid):
    step = pl.program_id(0)
    x = jnp.concatenate([text[...], mem[...]], axis=0)
    count = x.shape[0]
    query = (dot(x, w_q[...]) + lines[0:1, :]).astype(BF16)
    key = dot(x, w_k[...]).astype(BF16)
    value = (dot(x, w_v[...]) + lines[1:2, :]).astype(BF16)
    q_out[...] = query
    k_out[...] = key
    v_out[...] = value
    scaled = query * jnp.asarray(0.125, BF16)
    lane = lanes_of((count, 128))
    ones = (lane == 0).astype(BF16)
    mq, mk = mark_q[...], mark_k[...]
    pairs = []
    logs = jnp.zeros((count, 128), F32)
    for pair in range(2):
        span = slice(128 * pair, 128 * pair + 128)
        key_wide = jnp.concatenate([key[:, span], mk], axis=1)
        value_wide = jnp.concatenate([value[:, span], ones], axis=1)
        outs = []
        for side in range(2):
            mine = jnp.where(lane // 64 == side, scaled[:, span], jnp.asarray(0, BF16))
            scores = dot_nt(jnp.concatenate([mine, mq], axis=1), key_wide)
            top = jnp.max(scores, axis=-1, keepdims=True)
            raised = jnp.exp(scores - top).astype(BF16)
            summed = dot(raised, value_wide)
            total = summed[:, 128:129]
            outs.append(summed[:, :128] / total)
            logs = jnp.where(lane == 4 * step + 2 * pair + side, top + jnp.log(total), logs)
        pairs.append(jnp.where(lane < 64, outs[0], outs[1]).astype(BF16))
    attended = jnp.concatenate(pairs, axis=1)
    att_out[...] = attended

    @pl.when(step == 0)
    def _():
        log_out[...] = logs
        resid[...] = x.astype(F32) + lines_all[2:3, :]

    @pl.when(step > 0)
    def _():
        log_out[...] += logs

    resid[...] += dot(attended, w_out[...])


def attend(text, mem, w_qkv, lines, mark_q, mark_k, w_out):
    width = text.shape[1]
    count = text.shape[0] + mem.shape[0]
    whole = lambda shape: pl.BlockSpec(shape, lambda j: (0, 0))
    cols = lambda height, base: pl.BlockSpec((height, 256), lambda j: (0, base + j))
    low = jax.ShapeDtypeStruct((count, width), BF16)
    return pl.pallas_call(
        attend_kernel,
        grid=(3,),
        in_specs=[
            whole(text.shape),
            whole(mem.shape),
            cols(width, 0),
            cols(width, 3),
            cols(width, 6),
            cols(16, 0),
            whole((16, width)),
            whole((count, 128)),
            whole((count, 128)),
            pl.BlockSpec((256, width), lambda j: (j, 0)),
        ],
        out_specs=[
            cols(count, 0),
            cols(count, 0),
            cols(count, 0),
            cols(count, 0),
            whole((count, 128)),
            whole((count, width)),
        ],
        out_shape=[
            low,
            low,
            low,
            low,
            jax.ShapeDtypeStruct((count, 128), F32),
            jax.ShapeDtypeStruct((count, width), F32),
        ],
        compiler_params=pltpu.CompilerParams(vmem_limit_bytes=VMEM_ASK),
        cost_estimate=cost(15),
        name="attend",
    )(text, mem, w_qkv, w_qkv, w_qkv, lines, lines, mark_q, mark_k, w_out)


def pack_rows(out, value, split):
    blocks = out.shape[0]
    each = split // blocks
    for block in range(blocks):
        out[block, :each] = value[block * each : (block + 1) * each]
        out[block, each:] = value[split:]


def column_sum(value):
    return jnp.sum(value, axis=0, keepdims=True)


def feed_kernel(resid_one, lines, w_in, w_down, cot_text, cot_mem,
                slope_out, hidden_out, result_out, g_two, g_low_out, sums_out, grad_out, act_all):
    step = pl.program_id(0)
    half = pl.num_programs(0) // 2

    @pl.when(step == 0)
    def _():
        normal, _ = norm_parts(resid_one[...])
        hidden = normal * lines[3:4, :] + lines[4:5, :]
        hidden_out[...] = hidden.astype(BF16)
        g_two[...] = hidden + lines[5:6, :]

    @pl.when(step < half)
    def _():
        inner = dot(hidden_out[...], w_in[...]) + lines[pl.ds(8 + step, 1), :]
        phi = 0.5 * (1.0 + lax.erf(inner * (0.5**0.5)))
        act = (inner * phi).astype(BF16)
        act_all[step] = act
        slope = phi + inner * jnp.exp(-0.5 * inner * inner) * 0.3989422804014327
        slope_out[...] = slope.astype(BF16)
        g_two[...] += dot(act, w_down[...])

    @pl.when(step == half - 1)
    def _():
        normal, scale = norm_parts(g_two[...])
        result = normal * lines[6:7, :] + lines[7:8, :]
        pack_rows(result_out, result.astype(BF16), cot_text.shape[0])
        grad = jnp.concatenate([cot_text[...], cot_mem[...]], axis=0).astype(F32)
        sums_out[0:1, :] = column_sum(grad * normal)
        sums_out[1:2, :] = column_sum(grad)
        grad = norm_back(grad * lines[6:7, :], normal, scale)
        sums_out[2:3, :] = column_sum(grad)
        g_two[...] = grad
        g_low_out[...] = grad.astype(BF16)

    @pl.when(step >= half)
    def _():
        grad_out[...] = dot_tn(act_all[step - half], g_low_out[...]).astype(BF16)


def feed(resid_one, lines, w_in, w_down, cot_text, cot_mem, packed):
    count, width = resid_one.shape
    wide = w_in.shape[1]
    half = wide // width
    whole = lambda shape: pl.BlockSpec(shape, lambda j: (0, 0))
    early = lambda height: pl.BlockSpec((height, width), lambda j: (0, jnp.minimum(j, half - 1)))
    full = whole((count, width))
    return pl.pallas_call(
        feed_kernel,
        grid=(2 * half,),
        in_specs=[
            full,
            whole(lines.shape),
            early(width),
            pl.BlockSpec((width, width), lambda j: (jnp.minimum(j, half - 1), 0)),
            whole(cot_text.shape),
            whole(cot_mem.shape),
        ],
        out_specs=[
            early(count),
            full,
            pl.BlockSpec(packed, lambda j: (0, 0, 0)),
            full,
            full,
            whole((8, width)),
            pl.BlockSpec((width, width), lambda j: (jnp.maximum(j - half, 0), 0)),
        ],
        out_shape=[
            jax.ShapeDtypeStruct((count, wide), BF16),
            jax.ShapeDtypeStruct((count, width), BF16),
            jax.ShapeDtypeStruct(packed, BF16),
            jax.ShapeDtypeStruct((count, width), F32),
            jax.ShapeDtypeStruct((count, width), BF16),
            jax.ShapeDtypeStruct((8, width), F32),
            jax.ShapeDtypeStruct((wide, width), BF16),
        ],
        scratch_shapes=[pltpu.VMEM((half, count, width), BF16)],
        compiler_params=pltpu.CompilerParams(vmem_limit_bytes=VMEM_ASK),
        cost_estimate=cost(20),
        name="feed",
    )(resid_one, lines, w_in, w_down, cot_text, cot_mem)


def inner_back_kernel(g_low, slope, hidden, w_down, grad_out, inner_out, sums_out):
    g_inner = dot_nt(g_low[...], w_down[...]) * slope[...].astype(F32)
    sums_out[0:1, :] = column_sum(g_inner)
    g_inner_low = g_inner.astype(BF16)
    inner_out[...] = g_inner_low
    grad_out[0] = dot_tn(hidden[...], g_inner_low).astype(BF16)


def inner_back(g_low, slope, hidden, w_down):
    count, width = g_low.shape
    wide = slope.shape[1]
    half = wide // width
    full = pl.BlockSpec((count, width), lambda j: (0, 0))
    part = lambda height: pl.BlockSpec((height, width), lambda j: (0, j))
    return pl.pallas_call(
        inner_back_kernel,
        grid=(half,),
        in_specs=[full, part(count), full, pl.BlockSpec((width, width), lambda j: (j, 0))],
        out_specs=[
            pl.BlockSpec((1, width, width), lambda j: (j, 0, 0)),
            part(count),
            part(8),
        ],
        out_shape=[
            jax.ShapeDtypeStruct((half, width, width), BF16),
            jax.ShapeDtypeStruct((count, wide), BF16),
            jax.ShapeDtypeStruct((8, wide), F32),
        ],
        compiler_params=pltpu.CompilerParams(vmem_limit_bytes=VMEM_ASK),
        cost_estimate=cost(10),
        name="inner_back",
    )(g_low, slope, hidden, w_down)


def norm_one_back_kernel(g_two, g_inner, w_in, resid_one, lines, g_one, g_one_low, sums_out):
    step = pl.program_id(0)

    @pl.when(step == 0)
    def _():
        g_one[...] = g_two[...]

    g_one[...] += dot_nt(g_inner[...], w_in[...])

    @pl.when(step == pl.num_programs(0) - 1)
    def _():
        normal, scale = norm_parts(resid_one[...])
        g_hidden = g_one[...]
        sums_out[0:1, :] = column_sum(g_hidden * normal)
        sums_out[1:2, :] = column_sum(g_hidden)
        grad = norm_back(g_hidden * lines[3:4, :], normal, scale)
        sums_out[2:3, :] = column_sum(grad)
        g_one[...] = grad
        g_one_low[...] = grad.astype(BF16)


def norm_one_back(g_two, g_inner, w_in, resid_one, lines):
    count, width = g_two.shape
    half = w_in.shape[1] // width
    whole = lambda shape: pl.BlockSpec(shape, lambda j: (0, 0))
    part = lambda height: pl.BlockSpec((height, width), lambda j: (0, j))
    full = whole((count, width))
    return pl.pallas_call(
        norm_one_back_kernel,
        grid=(half,),
        in_specs=[full, part(count), part(width), full, whole(lines.shape)],
        out_specs=[full, full, whole((8, width))],
        out_shape=[
            jax.ShapeDtypeStruct((count, width), F32),
            jax.ShapeDtypeStruct((count, width), BF16),
            jax.ShapeDtypeStruct((8, width), F32),
        ],
        compiler_params=pltpu.CompilerParams(vmem_limit_bytes=VMEM_ASK),
        cost_estimate=cost(8),
        name="norm_one_back",
    )(g_two, g_inner, w_in, resid_one, lines)


def attend_back_kernel(text, mem, q, k, v, att, logs, mark_q, mark_k, g_one, g_low, w_out,
                       w_q, w_k, w_v, sums_two, sums_one, sums_in, scalars,
                       mine_out, theirs_out, packed_out, g_rows, sums):
    step = pl.program_id(0)
    core = scalars[0, 1]
    split = text.shape[0]
    count = split + mem.shape[0]
    width = text.shape[1]
    query, key, value, attended = q[...], k[...], v[...], att[...]

    def put(half, start, part):
        rows = pl.ds(pl.multiple_of(start, 16), part.shape[0])

        @pl.when(core == half)
        def _():
            mine_out[rows, :] = part

        @pl.when(core != half)
        def _():
            theirs_out[rows, :] = part

    blocks = width // 128
    grad_w_out = dot_tn(attended, g_low[...]).astype(BF16)
    for block in range(blocks):
        part = grad_w_out[:, 128 * block : 128 * block + 128]
        put(1, (blocks + block) * width + 256 * step, part)
    g_att = dot_nt(g_low[...], w_out[...])
    g_att_low = g_att.astype(BF16)
    scaled = query * jnp.asarray(0.125, BF16)
    product = g_att_low.astype(F32) * attended.astype(F32)
    lane = lanes_of((count, 128))
    none = jnp.asarray(0, BF16)
    thirds = ((lane >= 4) & (lane < 7)).astype(BF16)
    mq, mk = mark_q[...], mark_k[...] + thirds
    log_all = logs[...]

    def extra(column, base):
        high, middle, low = split_three(-column)
        wide = jnp.where(lane == 4, high, jnp.where(lane == 5, middle, low))
        return jnp.where((lane >= 4) & (lane < 7), wide, base)

    g_querys, g_keys, g_values = [], [], []
    for pair in range(2):
        span = slice(128 * pair, 128 * pair + 128)
        key_pair = key[:, span]
        key_wide = jnp.concatenate([key_pair, mk], axis=1)
        value_wide = jnp.concatenate([value[:, span], thirds], axis=1)
        key_turned = key_pair.astype(F32).T
        turned = lax.broadcasted_iota(jnp.int32, key_turned.shape, 0)
        g_query = g_key = g_value = None
        for side in range(2):
            own = lane // 64 == side
            mine = jnp.where(own, scaled[:, span], none)
            head = 4 * step + 2 * pair + side
            log_own = jnp.sum(jnp.where(lane == head, log_all, 0.0), axis=1, keepdims=True)
            query_wide = jnp.concatenate([mine, extra(log_own, mq)], axis=1)
            probs = jnp.exp(dot_nt(key_wide, query_wide))
            g_mine = jnp.where(own, g_att_low[:, span], none)
            delta = jnp.sum(jnp.where(own, product[:, span], 0.0), axis=1, keepdims=True)
            g_wide = jnp.concatenate([g_mine, extra(delta, jnp.zeros_like(mq))], axis=1)
            g_scores = (probs * dot_nt(value_wide, g_wide)).astype(BF16)
            part_v = dot(probs.astype(BF16), g_mine)
            part_k = dot(g_scores, mine)
            turned_own = jnp.where(turned // 64 == side, key_turned, 0.0).astype(BF16)
            part_q = dot(turned_own, g_scores)
            if side == 0:
                g_query, g_key, g_value = part_q, part_k, part_v
            else:
                g_query, g_key, g_value = g_query + part_q, g_key + part_k, g_value + part_v
        g_querys.append(g_query.T * 0.125)
        g_keys.append(g_key)
        g_values.append(g_value)
    g_query = jnp.concatenate(g_querys, axis=1)
    g_key = jnp.concatenate(g_keys, axis=1)
    g_value = jnp.concatenate(g_values, axis=1)
    columns = pl.ds(pl.multiple_of(256 * step, 256), 256)
    sums[0:1, columns] = column_sum(g_query)
    sums[1:2, columns] = column_sum(g_value)
    x = jnp.concatenate([text[...], mem[...]], axis=0)

    @pl.when(step == 0)
    def _():
        g_rows[...] = g_one[...]

    total = g_rows[...]
    for place, (grad, weight) in enumerate(((g_query, w_q), (g_key, w_k), (g_value, w_v))):
        low = grad.astype(BF16)
        grad_w = dot_tn(x, low).astype(BF16)
        for block in range(2):
            part = grad_w[:, 128 * block : 128 * block + 128]
            put(place // 2, ((place % 2) * blocks + 2 * step + block) * width, part)
        total += dot_nt(low, weight[...])
    g_rows[...] = total

    @pl.when(step == pl.num_programs(0) - 1)
    def _():
        reset = scalars[0, 0] == 1
        g_mem = total[split:]
        zero = jnp.zeros_like(g_mem)
        g_kept = jnp.where(reset, zero, g_mem)
        pack_rows(packed_out, jnp.concatenate([total[:split], g_kept], axis=0).astype(BF16), split)
        sums[2:5, :] = sums_one[0:3, :]
        sums[5:8, :] = sums_two[0:3, :]
        for place in range(4):
            sums[8 + place : 9 + place, :] = sums_in[0:1, place * width : (place + 1) * width]
        sums[12:16, :] = jnp.zeros((4, width), F32)
        small = [jnp.where(reset, g_mem, zero).astype(BF16), sums[...].astype(BF16)]
        small = jnp.concatenate(small, axis=0)
        base = 2 * blocks * width
        spare = mine_out.shape[0] - base
        empty = jnp.zeros((spare, 128), BF16)
        mine_out[base:, :] = empty
        theirs_out[base:, :] = empty
        for block in range(blocks):
            put(0, base + block * small.shape[0], small[:, 128 * block : 128 * block + 128])


def attend_back(text, mem, q, k, v, att, logs, mark_q, mark_k, g_one, g_low, w_out, w_qkv,
                sums_two, sums_one, sums_in, scalars, packed):
    width = text.shape[1]
    count = text.shape[0] + mem.shape[0]
    whole = lambda shape: pl.BlockSpec(shape, lambda j: (0, 0))
    cols = lambda height, base: pl.BlockSpec((height, 256), lambda j: (0, base + j))
    full = whole((count, width))
    mark = whole((count, 128))
    height = 2 * (width // 128) * width + 512
    return pl.pallas_call(
        attend_back_kernel,
        grid=(3,),
        in_specs=[
            whole(text.shape),
            whole(mem.shape),
            cols(count, 0),
            cols(count, 0),
            cols(count, 0),
            cols(count, 0),
            mark,
            mark,
            mark,
            full,
            full,
            pl.BlockSpec((256, width), lambda j: (j, 0)),
            cols(width, 0),
            cols(width, 3),
            cols(width, 6),
            whole(sums_two.shape),
            whole(sums_one.shape),
            whole(sums_in.shape),
            pl.BlockSpec(memory_space=pltpu.SMEM),
        ],
        out_specs=[
            whole((height, 128)),
            whole((height, 128)),
            pl.BlockSpec(packed, lambda j: (0, 0, 0)),
        ],
        out_shape=[
            jax.ShapeDtypeStruct((height, 128), BF16),
            jax.ShapeDtypeStruct((height, 128), BF16),
            jax.ShapeDtypeStruct(packed, BF16),
        ],
        scratch_shapes=[pltpu.VMEM((count, width), F32), pltpu.VMEM((16, width), F32)],
        compiler_params=pltpu.CompilerParams(vmem_limit_bytes=VMEM_ASK),
        cost_estimate=cost(25),
        name="attend_back",
    )(text, mem, q, k, v, att, logs, mark_q, mark_k, g_one, g_low, w_out, w_qkv, w_qkv, w_qkv,
      sums_two, sums_one, sums_in, scalars)


def widen_kernel(mine, got, scalars, qkv_out, out_out):
    group = pl.program_id(0)
    own = group // 2 == scalars[0, 1]
    width = out_out.shape[0]

    def fill(ref):
        for block in range(width // 128):
            rows = slice(block * width, (block + 1) * width)
            ref[:, 128 * block : 128 * block + 128] = jnp.where(
                own, mine[rows, :].astype(F32), got[rows, :].astype(F32)
            )

    @pl.when(group < 3)
    def _():
        fill(qkv_out)

    @pl.when(group == 3)
    def _():
        fill(out_out)


def widen(mine, got, scalars, width):
    tall = width // 128 * width
    half = pl.BlockSpec((tall, 128), lambda g: (g % 2, 0))
    return pl.pallas_call(
        widen_kernel,
        grid=(4,),
        in_specs=[half, half, pl.BlockSpec(memory_space=pltpu.SMEM)],
        out_specs=[
            pl.BlockSpec((width, width), lambda g: (0, jnp.minimum(g, 2))),
            pl.BlockSpec((width, width), lambda g: (0, 0)),
        ],
        out_shape=[
            jax.ShapeDtypeStruct((width, 3 * width), F32),
            jax.ShapeDtypeStruct((width, width), F32),
        ],
        compiler_params=pltpu.CompilerParams(vmem_limit_bytes=VMEM_ASK),
        cost_estimate=cost(6),
        name="widen",
    )(mine, got, scalars)


def core_swap(value):
    return lax.ppermute(value, "core", [(0, 1), (1, 0)])


def to_segments(value):
    return lax.all_to_all(value, BLK, 0, 1, tiled=True)[0]


def after(value, other):
    return lax.optimization_barrier((value, other))[0]


def doc_marks(docs, mem_count):
    kinds = (docs[:, None] == jnp.arange(3)[None]).astype(F32)
    rest = mem_count + ROW_PAD
    total = docs.shape[0] + rest
    spare = (jnp.arange(total) >= total - ROW_PAD).astype(F32)[:, None]
    query = jnp.concatenate([jnp.pad(kinds, ((0, rest), (0, 0))), jnp.ones((total, 1), F32)], 1)
    key = jnp.concatenate([jnp.pad(kinds - 1.0, ((0, rest), (0, 0))), -spare], 1) * BAN
    fill = ((0, 0), (0, 128 - query.shape[1]))
    return jnp.pad(query, fill).astype(BF16), jnp.pad(key, fill).astype(BF16)


def local(
    tokens,
    memory,
    mem_init,
    reset_flags,
    doc_ids,
    w_qkv,
    b_query,
    b_value,
    w_out,
    b_out,
    norm1_gain,
    norm1_bias,
    w_in,
    b_in,
    w_down,
    b_down,
    norm2_gain,
    norm2_bias,
    out_cot,
    mem_cot,
):
    seg_count, tok_count, width = tokens.shape
    mem_count = memory.shape[1]
    place = lax.axis_index(BLK)
    pick = lambda value: lax.dynamic_index_in_dim(value, place, 0, keepdims=False)
    fill = lambda value: jnp.pad(value, ((0, ROW_PAD), (0, 0)))
    packed = (seg_count, tok_count + mem_count + ROW_PAD, width)
    my_flag = pick(reset_flags)
    mark_q, mark_k = doc_marks(pick(doc_ids), mem_count)
    mem = fill(jnp.where(my_flag == 1, mem_init, pick(memory)))
    cot_mem = fill(pick(mem_cot))
    text = to_segments(tokens)
    cot_text = to_segments(after(out_cot, text))

    lines = jnp.concatenate(
        [b_query, b_value, b_out, norm1_gain, norm1_bias, b_down, norm2_gain, norm2_bias, b_in]
    )
    lines = jnp.pad(lines.astype(F32).reshape(-1, width), ((0, 4), (0, 0)))
    q, k, v, att, logs, resid = attend(text, mem, w_qkv, lines, mark_q, mark_k, w_out)
    slope, hidden, result, g_two, g_two_low, sums_two, grad_down = feed(
        resid, lines, w_in, w_down, cot_text, cot_mem, packed
    )
    grad_in, g_inner, sums_in = inner_back(g_two_low, slope, hidden, w_down)
    grad_down, grad_in = lax.psum((grad_down, grad_in), ALL)
    scalars = jnp.stack([my_flag, lax.axis_index("core")]).reshape(1, 2).astype(jnp.int32)
    small_count = mem_count + ROW_PAD + 16

    def attention_back(operands):
        result, g_two, g_inner, sums_two, sums_in = operands
        g_one, g_one_low, sums_one = norm_one_back(g_two, g_inner, w_in, resid, lines)
        mine, theirs, g_packed = attend_back(
            text,
            mem,
            q,
            k,
            v,
            att,
            logs,
            mark_q,
            mark_k,
            g_one,
            g_one_low,
            w_out,
            w_qkv,
            sums_two,
            sums_one,
            sums_in,
            scalars,
            packed,
        )
        both = jnp.concatenate([result, g_packed], axis=1)
        mine = (mine.astype(F32) + core_swap(theirs).astype(F32)).astype(BF16)
        parts = mine.reshape(CHIPS, -1, 128)
        parts = lax.all_to_all(parts, XYZ, 0, 0, tiled=True)
        part = jnp.sum(parts.astype(F32), axis=0).astype(BF16)
        parts = lax.all_to_all(
            jnp.broadcast_to(part[None], parts.shape), XYZ, 0, 0, tiled=True
        )
        mine = parts.reshape(mine.shape)
        both = lax.all_to_all(after(both, mine), BLK, 0, 0, tiled=True)
        got = core_swap(mine)
        grad_wqkv, grad_wout = widen(mine, got, scalars, width)
        blocks = width // 128
        small = jnp.where(scalars[0, 1] == 0, mine[-512:], got[-512:])
        small = small[: blocks * small_count].reshape(blocks, small_count, 128)
        small = small.astype(F32).transpose(1, 0, 2).reshape(small_count, width)
        pieces = []
        for base in (0, result.shape[1]):
            pieces.append(both[:, base : base + tok_count])
            pieces.append(both[:, base + tok_count : base + tok_count + mem_count])
        return grad_wqkv, grad_wout, small, *pieces

    def nothing(operands):
        text_zero = jnp.zeros(tokens.shape, BF16)
        mem_zero = jnp.zeros(memory.shape, BF16)
        return (
            jnp.zeros(w_qkv.shape, F32),
            jnp.zeros(w_out.shape, F32),
            jnp.zeros((small_count, width), F32),
            text_zero,
            mem_zero,
            text_zero,
            mem_zero,
        )

    grad_wqkv, grad_wout, small, output, mem_output, grad_tokens, grad_memory = lax.cond(
        reset_flags[0] >= 0, attention_back, nothing, (result, g_two, g_inner, sums_two, sums_in)
    )
    grad_bquery, grad_bvalue, grad_gain1, grad_bias1, grad_bout, grad_gain2, grad_bias2, grad_bdown = (
        small[mem_count + ROW_PAD + row] for row in range(8)
    )
    start = mem_count + ROW_PAD + 8
    grad_bin = small[start : start + w_in.shape[1] // width].reshape(-1)
    return (
        output,
        mem_output,
        grad_tokens,
        grad_memory,
        small[:mem_count],
        grad_wqkv,
        grad_bquery,
        grad_bvalue,
        grad_wout,
        grad_bout,
        grad_gain1,
        grad_bias1,
        jnp.concatenate(list(grad_in), axis=1).astype(F32),
        grad_bin,
        grad_down.astype(F32),
        grad_bdown,
        grad_gain2,
        grad_bias2,
    )


def solution(mesh):
    chips = Mesh(mesh.devices.reshape(4, 4, 4, 2), ALL)
    placed = (
        P(SEG, BLK, None),
        P(SEG, None, None),
        P(),
        P(SEG),
        P(SEG, None),
        *([P()] * 13),
        P(SEG, BLK, None),
        P(SEG, None, None),
    )
    return jax.shard_map(
        local,
        mesh=chips,
        in_specs=placed,
        out_specs=(
            P(SEG, BLK, None),
            P(SEG, None, None),
            P(SEG, BLK, None),
            P(SEG, None, None),
            *([P()] * 14),
        ),
        check_vma=False,
    )
```

```python
import jax
import jax.numpy as jnp
from jax import lax
from jax.experimental import pallas as pl
from jax.experimental.pallas import tpu as pltpu
from jax.sharding import Mesh, PartitionSpec as P

F32 = jnp.float32
BF16 = jnp.bfloat16
HEADS = 12
EPS = 1e-12
BAN = 2.0**30
VMEM_ASK = 60 * 1024 * 1024
BLK = ("z", "core")
SEG = ("y", "x")
ALL = ("y", "x", "z", "core")
XYZ = ("x", "y", "z")
CHIPS = 64
ROW_PAD = 12


def dot(left, right):
    return jnp.dot(left, right, preferred_element_type=F32)


def dot_nt(left, right):
    return lax.dot_general(left, right, (((1,), (1,)), ((), ())), preferred_element_type=F32)


def dot_tn(left, right):
    return lax.dot_general(left, right, (((0,), (0,)), ((), ())), preferred_element_type=F32)


def cost(micros):
    return pl.CostEstimate(flops=int(micros * 1e9), bytes_accessed=0, transcendentals=0)


def lanes_of(shape):
    return lax.broadcasted_iota(jnp.int32, shape, 1)


def split_three(value):
    high = value.astype(BF16)
    rest = value - high.astype(F32)
    middle = rest.astype(BF16)
    low = (rest - middle.astype(F32)).astype(BF16)
    return high, middle, low


def norm_parts(value):
    centre = jnp.mean(value, axis=-1, keepdims=True)
    centered = value - centre
    spread = jnp.mean(centered * centered, axis=-1, keepdims=True)
    scale = lax.rsqrt(spread + EPS)
    return centered * scale, scale


def norm_back(grad, normal, scale):
    mean_grad = jnp.mean(grad, axis=-1, keepdims=True)
    mean_prod = jnp.mean(grad * normal, axis=-1, keepdims=True)
    return scale * (grad - mean_grad - normal * mean_prod)


def pack_rows(out, value, split):
    blocks = out.shape[0]
    each = split // blocks
    for block in range(blocks):
        out[block, :each] = value[block * each : (block + 1) * each]
        out[block, each:] = value[split:]


def column_sum(value):
    return jnp.sum(value, axis=0, keepdims=True)


def attend_kernel(text, mem, w_q, w_k, w_v, lines, lines_all, mark_q, mark_k, w_out,
                  q_out, k_out, v_out, att_out, log_out, resid):
    step = pl.program_id(0)
    x = jnp.concatenate([text[...], mem[...]], axis=0)
    count = x.shape[0]
    query = (dot(x, w_q[...]) + lines[0:1, :]).astype(BF16)
    key = dot(x, w_k[...]).astype(BF16)
    value = (dot(x, w_v[...]) + lines[1:2, :]).astype(BF16)
    q_out[...] = query
    k_out[...] = key
    v_out[...] = value
    scaled = query * jnp.asarray(0.125, BF16)
    lane = lanes_of((count, 128))
    ones = (lane == 0).astype(BF16)
    mq, mk = mark_q[...], mark_k[...]
    pairs = []
    logs = jnp.zeros((count, 128), F32)
    for pair in range(2):
        span = slice(128 * pair, 128 * pair + 128)
        key_wide = jnp.concatenate([key[:, span], mk], axis=1)
        value_wide = jnp.concatenate([value[:, span], ones], axis=1)
        outs = []
        for side in range(2):
            mine = jnp.where(lane // 64 == side, scaled[:, span], jnp.asarray(0, BF16))
            scores = dot_nt(jnp.concatenate([mine, mq], axis=1), key_wide)
            top = jnp.max(scores, axis=-1, keepdims=True)
            raised = jnp.exp(scores - top).astype(BF16)
            summed = dot(raised, value_wide)
            total = summed[:, 128:129]
            outs.append(summed[:, :128] / total)
            logs = jnp.where(lane == 4 * step + 2 * pair + side, top + jnp.log(total), logs)
        pairs.append(jnp.where(lane < 64, outs[0], outs[1]).astype(BF16))
    attended = jnp.concatenate(pairs, axis=1)
    att_out[...] = attended

    @pl.when(step == 0)
    def _():
        log_out[...] = logs
        resid[...] = x.astype(F32) + lines_all[2:3, :]

    @pl.when(step > 0)
    def _():
        log_out[...] += logs

    resid[...] += dot(attended, w_out[...])


def attend(text, mem, w_qkv, lines, mark_q, mark_k, w_out):
    width = text.shape[1]
    count = text.shape[0] + mem.shape[0]
    whole = lambda shape: pl.BlockSpec(shape, lambda j: (0, 0))
    cols = lambda height, base: pl.BlockSpec((height, 256), lambda j: (0, base + j))
    low = jax.ShapeDtypeStruct((count, width), BF16)
    return pl.pallas_call(
        attend_kernel,
        grid=(3,),
        in_specs=[
            whole(text.shape),
            whole(mem.shape),
            cols(width, 0),
            cols(width, 3),
            cols(width, 6),
            cols(16, 0),
            whole((16, width)),
            whole((count, 128)),
            whole((count, 128)),
            pl.BlockSpec((256, width), lambda j: (j, 0)),
        ],
        out_specs=[
            cols(count, 0),
            cols(count, 0),
            cols(count, 0),
            cols(count, 0),
            whole((count, 128)),
            whole((count, width)),
        ],
        out_shape=[
            low,
            low,
            low,
            low,
            jax.ShapeDtypeStruct((count, 128), F32),
            jax.ShapeDtypeStruct((count, width), F32),
        ],
        compiler_params=pltpu.CompilerParams(vmem_limit_bytes=VMEM_ASK),
        cost_estimate=cost(15),
        name="attend",
    )(text, mem, w_qkv, w_qkv, w_qkv, lines, lines, mark_q, mark_k, w_out)


def feed_kernel(resid, lines, w_in, w_down, cot_text, cot_mem,
                result_out, g_two, inner_out, sums_out, sums_in_out, grad_down_out, grad_in_out,
                hidden_low, hidden_turned, g_low, act_all, slope_all):
    step = pl.program_id(0)
    down_at = act_all.shape[0]
    in_at = 2 * down_at

    @pl.when(step == 0)
    def _():
        normal, _ = norm_parts(resid[...])
        hidden = normal * lines[3:4, :] + lines[4:5, :]
        hidden_low[...] = hidden.astype(BF16)
        hidden_turned[...] = hidden.astype(BF16).T
        g_two[...] = hidden + lines[5:6, :]

    @pl.when(step < down_at)
    def _():
        inner = dot(hidden_low[...], w_in[...]) + lines[pl.ds(8 + step, 1), :]
        phi = 0.5 * (1.0 + lax.erf(inner * (0.5**0.5)))
        act = (inner * phi).astype(BF16)
        act_all[step] = act
        slope = phi + inner * jnp.exp(-0.5 * inner * inner) * 0.3989422804014327
        slope_all[step] = slope.astype(BF16)
        g_two[...] += dot(act, w_down[...])

    @pl.when(step == down_at - 1)
    def _():
        normal, scale = norm_parts(g_two[...])
        result = normal * lines[6:7, :] + lines[7:8, :]
        pack_rows(result_out, result.astype(BF16), cot_text.shape[0])
        grad = jnp.concatenate([cot_text[...], cot_mem[...]], axis=0).astype(F32)
        sums_out[0:1, :] = column_sum(grad * normal)
        sums_out[1:2, :] = column_sum(grad)
        grad = norm_back(grad * lines[6:7, :], normal, scale)
        sums_out[2:3, :] = column_sum(grad)
        g_two[...] = grad
        g_low[...] = grad.astype(BF16)

    @pl.when((step >= down_at) & (step < in_at))
    def _():
        grad_down_out[...] = dot_tn(act_all[step - down_at], g_low[...]).astype(BF16)

    @pl.when(step >= in_at)
    def _():
        g_inner = dot_nt(g_low[...], w_down[...]) * slope_all[step - in_at].astype(F32)
        sums_in_out[0:1, :] = column_sum(g_inner)
        g_inner_low = g_inner.astype(BF16)
        inner_out[...] = g_inner_low
        grad_in_out[0] = dot(hidden_turned[...], g_inner_low).astype(BF16)


def feed(resid, lines, w_in, w_down, cot_text, cot_mem, packed):
    count, width = resid.shape
    wide = w_in.shape[1]
    parts = wide // width
    in_at = 2 * parts
    whole = lambda shape: pl.BlockSpec(shape, lambda j: (0,) * len(shape))
    first_part = lambda j: jnp.minimum(j, parts - 1)
    last_part = lambda j: jnp.maximum(j - in_at, 0)
    down_part = lambda j: jnp.where(j < in_at, first_part(j), j - in_at)
    full = whole((count, width))
    high = jax.ShapeDtypeStruct((count, width), F32)
    return pl.pallas_call(
        feed_kernel,
        grid=(3 * parts,),
        in_specs=[
            full,
            whole(lines.shape),
            pl.BlockSpec((width, width), lambda j: (0, first_part(j))),
            pl.BlockSpec((width, width), lambda j: (down_part(j), 0)),
            whole(cot_text.shape),
            whole(cot_mem.shape),
        ],
        out_specs=[
            whole(packed),
            full,
            pl.BlockSpec((count, width), lambda j: (0, last_part(j))),
            whole((8, width)),
            pl.BlockSpec((8, width), lambda j: (0, last_part(j))),
            pl.BlockSpec((width, width), lambda j: (jnp.clip(j - parts, 0, parts - 1), 0)),
            pl.BlockSpec((1, width, width), lambda j: (last_part(j), 0, 0)),
        ],
        out_shape=[
            jax.ShapeDtypeStruct(packed, BF16),
            high,
            jax.ShapeDtypeStruct((count, wide), BF16),
            jax.ShapeDtypeStruct((8, width), F32),
            jax.ShapeDtypeStruct((8, wide), F32),
            jax.ShapeDtypeStruct((wide, width), BF16),
            jax.ShapeDtypeStruct((parts, width, width), BF16),
        ],
        scratch_shapes=[
            pltpu.VMEM((count, width), BF16),
            pltpu.VMEM((width, count), BF16),
            pltpu.VMEM((count, width), BF16),
            pltpu.VMEM((parts, count, width), BF16),
            pltpu.VMEM((parts, count, width), BF16),
        ],
        compiler_params=pltpu.CompilerParams(vmem_limit_bytes=VMEM_ASK),
        cost_estimate=cost(28),
        name="feed",
    )(resid, lines, w_in, w_down, cot_text, cot_mem)


def backward_kernel(g_two, g_inner, w_in, resid, lines, text, mem, q, k, v, att, logs, mark_q, mark_k,
                    w_out, w_q, w_k, w_v, sums_two, sums_in, scalars,
                    mine_out, theirs_out, packed_out, g_rows, g_low, rows_turned, sums):
    step = pl.program_id(0)
    parts = pl.num_programs(0) - 3

    @pl.when(step == 0)
    def _():
        x = jnp.concatenate([text[...], mem[...]], axis=0)
        rows_turned[...] = x.T
        g_rows[...] = g_two[...]

    @pl.when(step < parts)
    def _():
        g_rows[...] += dot_nt(g_inner[...], w_in[...])

    @pl.when(step == parts - 1)
    def _():
        normal, scale = norm_parts(resid[...])
        g_hidden = g_rows[...]
        sums[2:3, :] = column_sum(g_hidden * normal)
        sums[3:4, :] = column_sum(g_hidden)
        grad = norm_back(g_hidden * lines[3:4, :], normal, scale)
        sums[4:5, :] = column_sum(grad)
        g_rows[...] = grad
        g_low[...] = grad.astype(BF16)

    @pl.when(step >= parts)
    def _():
        attend_back_step(step - parts, text, mem, q, k, v, att, logs, mark_q, mark_k, g_low, w_out,
                         w_q, w_k, w_v, sums_two, sums_in, scalars,
                         mine_out, theirs_out, packed_out, g_rows, rows_turned, sums)


def attend_back_step(step, text, mem, q, k, v, att, logs, mark_q, mark_k, g_low, w_out,
                     w_q, w_k, w_v, sums_two, sums_in, scalars,
                     mine_out, theirs_out, packed_out, g_rows, rows_turned, sums):
    core = scalars[0, 1]
    split = text.shape[0]
    count = split + mem.shape[0]
    width = text.shape[1]
    query, key, value, attended = q[...], k[...], v[...], att[...]

    def put(half, start, part):
        rows = pl.ds(pl.multiple_of(start, 16), part.shape[0])

        @pl.when(core == half)
        def _():
            mine_out[rows, :] = part

        @pl.when(core != half)
        def _():
            theirs_out[rows, :] = part

    blocks = width // 128
    grad_w_out = dot_tn(attended, g_low[...]).astype(BF16)
    for block in range(blocks):
        part = grad_w_out[:, 128 * block : 128 * block + 128]
        put(1, (blocks + block) * width + 256 * step, part)
    g_att = dot_nt(g_low[...], w_out[...])
    g_att_low = g_att.astype(BF16)
    scaled = query * jnp.asarray(0.125, BF16)
    product = g_att_low.astype(F32) * attended.astype(F32)
    lane = lanes_of((count, 128))
    none = jnp.asarray(0, BF16)
    thirds = ((lane >= 4) & (lane < 7)).astype(BF16)
    mq, mk = mark_q[...], mark_k[...] + thirds
    log_all = logs[...]

    def extra(column, base):
        high, middle, low = split_three(-column)
        wide = jnp.where(lane == 4, high, jnp.where(lane == 5, middle, low))
        return jnp.where((lane >= 4) & (lane < 7), wide, base)

    g_querys, g_keys, g_values = [], [], []
    for pair in range(2):
        span = slice(128 * pair, 128 * pair + 128)
        key_pair = key[:, span]
        key_wide = jnp.concatenate([key_pair, mk], axis=1)
        value_wide = jnp.concatenate([value[:, span], thirds], axis=1)
        key_turned = key_pair.astype(F32).T
        turned = lax.broadcasted_iota(jnp.int32, key_turned.shape, 0)
        g_query = g_key = g_value = None
        for side in range(2):
            own = lane // 64 == side
            mine = jnp.where(own, scaled[:, span], none)
            head = 4 * step + 2 * pair + side
            log_own = jnp.sum(jnp.where(lane == head, log_all, 0.0), axis=1, keepdims=True)
            query_wide = jnp.concatenate([mine, extra(log_own, mq)], axis=1)
            probs = jnp.exp(dot_nt(key_wide, query_wide))
            g_mine = jnp.where(own, g_att_low[:, span], none)
            delta = jnp.sum(jnp.where(own, product[:, span], 0.0), axis=1, keepdims=True)
            g_wide = jnp.concatenate([g_mine, extra(delta, jnp.zeros_like(mq))], axis=1)
            g_scores = (probs * dot_nt(value_wide, g_wide)).astype(BF16)
            part_v = dot(probs.astype(BF16), g_mine)
            part_k = dot(g_scores, mine)
            turned_own = jnp.where(turned // 64 == side, key_turned, 0.0).astype(BF16)
            part_q = dot(turned_own, g_scores)
            if side == 0:
                g_query, g_key, g_value = part_q, part_k, part_v
            else:
                g_query, g_key, g_value = g_query + part_q, g_key + part_k, g_value + part_v
        g_querys.append(g_query.T * 0.125)
        g_keys.append(g_key)
        g_values.append(g_value)
    g_query = jnp.concatenate(g_querys, axis=1)
    g_key = jnp.concatenate(g_keys, axis=1)
    g_value = jnp.concatenate(g_values, axis=1)
    columns = pl.ds(pl.multiple_of(256 * step, 256), 256)
    sums[0:1, columns] = column_sum(g_query)
    sums[1:2, columns] = column_sum(g_value)
    total = g_rows[...]
    for place, (grad, weight) in enumerate(((g_query, w_q), (g_key, w_k), (g_value, w_v))):
        low = grad.astype(BF16)
        grad_w = dot(rows_turned[...], low).astype(BF16)
        for block in range(2):
            part = grad_w[:, 128 * block : 128 * block + 128]
            put(place // 2, ((place % 2) * blocks + 2 * step + block) * width, part)
        total += dot_nt(low, weight[...])
    g_rows[...] = total

    @pl.when(step == 2)
    def _():
        reset = scalars[0, 0] == 1
        g_mem = total[split:]
        zero = jnp.zeros_like(g_mem)
        g_kept = jnp.where(reset, zero, g_mem)
        pack_rows(packed_out, jnp.concatenate([total[:split], g_kept], axis=0).astype(BF16), split)
        sums[5:8, :] = sums_two[0:3, :]
        for place in range(4):
            sums[8 + place : 9 + place, :] = sums_in[0:1, place * width : (place + 1) * width]
        sums[12:16, :] = jnp.zeros((4, width), F32)
        small = [jnp.where(reset, g_mem, zero).astype(BF16), sums[...].astype(BF16)]
        small = jnp.concatenate(small, axis=0)
        base = 2 * blocks * width
        spare = mine_out.shape[0] - base
        empty = jnp.zeros((spare, 128), BF16)
        mine_out[base:, :] = empty
        theirs_out[base:, :] = empty
        for block in range(blocks):
            put(0, base + block * small.shape[0], small[:, 128 * block : 128 * block + 128])


def backward(g_two, g_inner, w_in, resid, lines, text, mem, q, k, v, att, logs, mark_q, mark_k,
             w_out, w_qkv, sums_two, sums_in, scalars, packed):
    width = text.shape[1]
    count = text.shape[0] + mem.shape[0]
    parts = w_in.shape[1] // width
    whole = lambda shape: pl.BlockSpec(shape, lambda j: (0,) * len(shape))
    early = lambda height: pl.BlockSpec((height, width), lambda j: (0, jnp.minimum(j, parts - 1)))
    quad = lambda j: jnp.maximum(j - parts, 0)
    cols = lambda height, base: pl.BlockSpec((height, 256), lambda j: (0, base + quad(j)))
    full = whole((count, width))
    mark = whole((count, 128))
    height = 2 * (width // 128) * width + 512
    half = jax.ShapeDtypeStruct((height, 128), BF16)
    return pl.pallas_call(
        backward_kernel,
        grid=(parts + 3,),
        in_specs=[
            full,
            early(count),
            early(width),
            full,
            whole(lines.shape),
            whole(text.shape),
            whole(mem.shape),
            cols(count, 0),
            cols(count, 0),
            cols(count, 0),
            cols(count, 0),
            mark,
            mark,
            mark,
            pl.BlockSpec((256, width), lambda j: (quad(j), 0)),
            cols(width, 0),
            cols(width, 3),
            cols(width, 6),
            whole(sums_two.shape),
            whole(sums_in.shape),
            pl.BlockSpec(memory_space=pltpu.SMEM),
        ],
        out_specs=[whole((height, 128)), whole((height, 128)), whole(packed)],
        out_shape=[half, half, jax.ShapeDtypeStruct(packed, BF16)],
        scratch_shapes=[
            pltpu.VMEM((count, width), F32),
            pltpu.VMEM((count, width), BF16),
            pltpu.VMEM((width, count), BF16),
            pltpu.VMEM((16, width), F32),
        ],
        compiler_params=pltpu.CompilerParams(vmem_limit_bytes=VMEM_ASK),
        cost_estimate=cost(33),
        name="backward",
    )(g_two, g_inner, w_in, resid, lines, text, mem, q, k, v, att, logs, mark_q, mark_k,
      w_out, w_qkv, w_qkv, w_qkv, sums_two, sums_in, scalars)


def widen_kernel(mine, got, scalars, qkv_out, out_out):
    group = pl.program_id(0)
    own = group // 2 == scalars[0, 1]
    width = out_out.shape[0]

    def fill(ref):
        for block in range(width // 128):
            rows = slice(block * width, (block + 1) * width)
            ref[:, 128 * block : 128 * block + 128] = jnp.where(
                own, mine[rows, :].astype(F32), got[rows, :].astype(F32)
            )

    @pl.when(group < 3)
    def _():
        fill(qkv_out)

    @pl.when(group == 3)
    def _():
        fill(out_out)


def widen(mine, got, scalars, width):
    tall = width // 128 * width
    half = pl.BlockSpec((tall, 128), lambda g: (g % 2, 0))
    return pl.pallas_call(
        widen_kernel,
        grid=(4,),
        in_specs=[half, half, pl.BlockSpec(memory_space=pltpu.SMEM)],
        out_specs=[
            pl.BlockSpec((width, width), lambda g: (0, jnp.minimum(g, 2))),
            pl.BlockSpec((width, width), lambda g: (0, 0)),
        ],
        out_shape=[
            jax.ShapeDtypeStruct((width, 3 * width), F32),
            jax.ShapeDtypeStruct((width, width), F32),
        ],
        compiler_params=pltpu.CompilerParams(vmem_limit_bytes=VMEM_ASK),
        cost_estimate=cost(6),
        name="widen",
    )(mine, got, scalars)


def widen_feed_kernel(down, inward, down_out, in_out):
    down_out[...] = down[...].astype(F32)
    in_out[...] = inward[0].astype(F32)


def widen_feed(down, inward):
    count, height, width = inward.shape
    cut = 2
    rows = height // cut
    return pl.pallas_call(
        widen_feed_kernel,
        grid=(count, cut),
        in_specs=[
            pl.BlockSpec((rows, width), lambda j, c: (j * cut + c, 0)),
            pl.BlockSpec((1, rows, width), lambda j, c: (j, c, 0)),
        ],
        out_specs=[
            pl.BlockSpec((rows, width), lambda j, c: (j * cut + c, 0)),
            pl.BlockSpec((rows, width), lambda j, c: (c, j)),
        ],
        out_shape=[
            jax.ShapeDtypeStruct(down.shape, F32),
            jax.ShapeDtypeStruct((height, count * width), F32),
        ],
        compiler_params=pltpu.CompilerParams(vmem_limit_bytes=VMEM_ASK),
        cost_estimate=cost(9),
        name="widen_feed",
    )(down, inward)


def ring_partner(place, way):
    return place ^ 1 if way == 0 else 3 - place


def ring_pairs(step):
    pairs = []
    for place in range(4):
        for core in range(2):
            other = ring_partner(place, (step + core) % 2)
            pairs.append((2 * place + core, 2 * other + core))
    return pairs


def ring_side(axis, step):
    place, core = lax.axis_index(axis), lax.axis_index("core")
    return jnp.where((step + core) % 2 == 0, (place + 1) // 2 % 2, place // 2)


def ring_swap(value, axis, step):
    return lax.ppermute(value, (axis, "core"), ring_pairs(step))


def core_swap(value):
    return lax.ppermute(value, "core", [(0, 1), (1, 0)])


def add_pair(pair):
    return (pair[0].astype(F32) + pair[1].astype(F32)).astype(BF16)


def half_of(pair, side):
    half = pair[0].shape[0] // 2
    return add_pair([lax.dynamic_slice_in_dim(part, side * half, half, 0) for part in pair])


def ring_halve(pair, axis, step):
    side = ring_side(axis, step)
    got = ring_swap(half_of(pair, 1 - side), axis, step)
    return half_of(pair, side), got


def ring_join(value, axis, step):
    got = ring_swap(value, axis, step)
    return jnp.where(
        ring_side(axis, step) == 0,
        jnp.concatenate([value, got], axis=0),
        jnp.concatenate([got, value], axis=0),
    )


def to_segments(value):
    return lax.all_to_all(value, BLK, 0, 1, tiled=True)[0]


def after(value, other):
    return lax.optimization_barrier((value, other))[0]


def doc_marks(docs, mem_count):
    kinds = (docs[:, None] == jnp.arange(3)[None]).astype(F32)
    rest = mem_count + ROW_PAD
    total = docs.shape[0] + rest
    spare = (jnp.arange(total) >= total - ROW_PAD).astype(F32)[:, None]
    query = jnp.concatenate([jnp.pad(kinds, ((0, rest), (0, 0))), jnp.ones((total, 1), F32)], 1)
    key = jnp.concatenate([jnp.pad(kinds - 1.0, ((0, rest), (0, 0))), -spare], 1) * BAN
    fill = ((0, 0), (0, 128 - query.shape[1]))
    return jnp.pad(query, fill).astype(BF16), jnp.pad(key, fill).astype(BF16)


def local(
    tokens,
    memory,
    mem_init,
    reset_flags,
    doc_ids,
    w_qkv,
    b_query,
    b_value,
    w_out,
    b_out,
    norm1_gain,
    norm1_bias,
    w_in,
    b_in,
    w_down,
    b_down,
    norm2_gain,
    norm2_bias,
    out_cot,
    mem_cot,
):
    seg_count, tok_count, width = tokens.shape
    mem_count = memory.shape[1]
    place = lax.axis_index(BLK)
    pick = lambda value: lax.dynamic_index_in_dim(value, place, 0, keepdims=False)
    fill = lambda value: jnp.pad(value, ((0, ROW_PAD), (0, 0)))
    packed = (seg_count, tok_count + mem_count + ROW_PAD, width)
    my_flag = pick(reset_flags)
    mark_q, mark_k = doc_marks(pick(doc_ids), mem_count)
    mem = fill(jnp.where(my_flag == 1, mem_init, pick(memory)))
    cot_mem = fill(pick(mem_cot))
    text = to_segments(tokens)
    cot_text = to_segments(after(out_cot, text))

    lines = jnp.concatenate(
        [b_query, b_value, b_out, norm1_gain, norm1_bias, b_down, norm2_gain, norm2_bias, b_in]
    )
    lines = jnp.pad(lines.astype(F32).reshape(-1, width), ((0, 4), (0, 0)))
    q, k, v, att, logs, resid = attend(text, mem, w_qkv, lines, mark_q, mark_k, w_out)
    result, g_two, g_inner, sums_two, sums_in, grad_down, grad_in = feed(
        resid, lines, w_in, w_down, cot_text, cot_mem, packed
    )
    grad_down, grad_in = lax.psum((grad_down, grad_in), ALL)
    scalars = jnp.stack([my_flag, lax.axis_index("core")]).reshape(1, 2).astype(jnp.int32)
    small_count = mem_count + ROW_PAD + 16

    def attention_back(operands):
        result, g_two, g_inner, sums_two, sums_in = operands
        mine, theirs, g_packed = backward(
            g_two,
            g_inner,
            w_in,
            resid,
            lines,
            text,
            mem,
            q,
            k,
            v,
            att,
            logs,
            mark_q,
            mark_k,
            w_out,
            w_qkv,
            sums_two,
            sums_in,
            scalars,
            packed,
        )
        both = jnp.concatenate([result, g_packed], axis=1)
        pair = (mine, core_swap(theirs))
        for step in (0, 1):
            pair = ring_halve(pair, "z", step)
        both = lax.all_to_all(after(both, pair[0]), BLK, 0, 0, tiled=True)
        for step in (0, 1):
            pair = ring_halve(pair, "x", step)
        for step in (0, 1):
            part = add_pair(pair)
            pair = (part, ring_swap(part, "y", step))
        mine = add_pair(pair)
        for step in (1, 0):
            mine = ring_join(mine, "x", step)
        mine = ring_join(after(mine, both), "z", 1)
        pieces = []
        for base in (0, result.shape[1]):
            pieces.append(both[:, base : base + tok_count])
            pieces.append(both[:, base + tok_count : base + tok_count + mem_count])
        mine = ring_join(mine, "z", 0)
        got = core_swap(mine)
        grad_wqkv, grad_wout = widen(mine, got, scalars, width)
        blocks = width // 128
        small = jnp.where(scalars[0, 1] == 0, mine[-512:], got[-512:])
        small = small[: blocks * small_count].reshape(blocks, small_count, 128)
        small = small.astype(F32).transpose(1, 0, 2).reshape(small_count, width)
        return grad_wqkv, grad_wout, small, *pieces

    def nothing(operands):
        text_zero = jnp.zeros(tokens.shape, BF16)
        mem_zero = jnp.zeros(memory.shape, BF16)
        return (
            jnp.zeros(w_qkv.shape, F32),
            jnp.zeros(w_out.shape, F32),
            jnp.zeros((small_count, width), F32),
            text_zero,
            mem_zero,
            text_zero,
            mem_zero,
        )

    grad_wqkv, grad_wout, small, output, mem_output, grad_tokens, grad_memory = lax.cond(
        reset_flags[0] >= 0, attention_back, nothing, (result, g_two, g_inner, sums_two, sums_in)
    )
    grad_down, grad_in = widen_feed(grad_down, grad_in)
    grad_bquery, grad_bvalue, grad_gain1, grad_bias1, grad_bout, grad_gain2, grad_bias2, grad_bdown = (
        small[mem_count + ROW_PAD + row] for row in range(8)
    )
    start = mem_count + ROW_PAD + 8
    grad_bin = small[start : start + w_in.shape[1] // width].reshape(-1)
    return (
        output,
        mem_output,
        grad_tokens,
        grad_memory,
        small[:mem_count],
        grad_wqkv,
        grad_bquery,
        grad_bvalue,
        grad_wout,
        grad_bout,
        grad_gain1,
        grad_bias1,
        grad_in,
        grad_bin,
        grad_down,
        grad_bdown,
        grad_gain2,
        grad_bias2,
    )


def solution(mesh):
    chips = Mesh(mesh.devices.reshape(4, 4, 4, 2), ALL)
    placed = (
        P(SEG, BLK, None),
        P(SEG, None, None),
        P(),
        P(SEG),
        P(SEG, None),
        *([P()] * 13),
        P(SEG, BLK, None),
        P(SEG, None, None),
    )
    return jax.shard_map(
        local,
        mesh=chips,
        in_specs=placed,
        out_specs=(
            P(SEG, BLK, None),
            P(SEG, None, None),
            P(SEG, BLK, None),
            P(SEG, None, None),
            *([P()] * 14),
        ),
        check_vma=False,
    )
```

```python
import jax
import jax.numpy as jnp
from jax import lax
from jax.experimental import pallas as pl
from jax.experimental.pallas import tpu as pltpu
from jax.sharding import Mesh, PartitionSpec as P

F32 = jnp.float32
BF16 = jnp.bfloat16
HEADS = 12
EPS = 1e-12
BAN = 2.0**30
VMEM_ASK = 60 * 1024 * 1024
BLK = ("z", "core")
SEG = ("y", "x")
ALL = ("y", "x", "z", "core")
XYZ = ("x", "y", "z")
CHIPS = 64
ROW_PAD = 12
SPARE_ROWS = 320
RING = ("z", "x", "y")


def dot(left, right):
    return jnp.dot(left, right, preferred_element_type=F32)


def dot_nt(left, right):
    return lax.dot_general(left, right, (((1,), (1,)), ((), ())), preferred_element_type=F32)


def dot_tn(left, right):
    return lax.dot_general(left, right, (((0,), (0,)), ((), ())), preferred_element_type=F32)


def cost(micros):
    return pl.CostEstimate(flops=int(micros * 1e9), bytes_accessed=0, transcendentals=0)


def lanes_of(shape):
    return lax.broadcasted_iota(jnp.int32, shape, 1)


def split_three(value):
    high = value.astype(BF16)
    rest = value - high.astype(F32)
    middle = rest.astype(BF16)
    low = (rest - middle.astype(F32)).astype(BF16)
    return high, middle, low


def norm_parts(value):
    centre = jnp.mean(value, axis=-1, keepdims=True)
    centered = value - centre
    spread = jnp.mean(centered * centered, axis=-1, keepdims=True)
    scale = lax.rsqrt(spread + EPS)
    return centered * scale, scale


def norm_back(grad, normal, scale):
    mean_grad = jnp.mean(grad, axis=-1, keepdims=True)
    mean_prod = jnp.mean(grad * normal, axis=-1, keepdims=True)
    return scale * (grad - mean_grad - normal * mean_prod)


def pack_rows(out, value, split, base=0):
    blocks = out.shape[0]
    each = split // blocks
    rest = value.shape[0] - split
    for block in range(blocks):
        out[block, base : base + each] = value[block * each : (block + 1) * each]
        out[block, base + each : base + each + rest] = value[split:]


def column_sum(value):
    return jnp.sum(value, axis=0, keepdims=True)


def attend_kernel(text, mem, w_q, w_k, w_v, lines, lines_all, mark_q, mark_k, w_out,
                  q_out, k_out, v_out, att_out, log_out, resid):
    step = pl.program_id(0)
    x = jnp.concatenate([text[...], mem[...]], axis=0)
    count = x.shape[0]
    query = (dot(x, w_q[...]) + lines[0:1, :]).astype(BF16)
    key = dot(x, w_k[...]).astype(BF16)
    value = (dot(x, w_v[...]) + lines[1:2, :]).astype(BF16)
    q_out[...] = query
    k_out[...] = key
    v_out[...] = value
    scaled = query * jnp.asarray(0.125, BF16)
    lane = lanes_of((count, 128))
    ones = (lane == 0).astype(BF16)
    mq, mk = mark_q[...], mark_k[...]
    pairs = []
    logs = jnp.zeros((count, 128), F32)
    for pair in range(2):
        span = slice(128 * pair, 128 * pair + 128)
        key_wide = jnp.concatenate([key[:, span], mk], axis=1)
        value_wide = jnp.concatenate([value[:, span], ones], axis=1)
        outs = []
        for side in range(2):
            mine = jnp.where(lane // 64 == side, scaled[:, span], jnp.asarray(0, BF16))
            scores = dot_nt(jnp.concatenate([mine, mq], axis=1), key_wide)
            top = jnp.max(scores, axis=-1, keepdims=True)
            raised = jnp.exp(scores - top).astype(BF16)
            summed = dot(raised, value_wide)
            total = summed[:, 128:129]
            outs.append(summed[:, :128] / total)
            logs = jnp.where(lane == 4 * step + 2 * pair + side, top + jnp.log(total), logs)
        pairs.append(jnp.where(lane < 64, outs[0], outs[1]).astype(BF16))
    attended = jnp.concatenate(pairs, axis=1)
    att_out[...] = attended

    @pl.when(step == 0)
    def _():
        log_out[...] = logs
        resid[...] = x.astype(F32) + lines_all[2:3, :]

    @pl.when(step > 0)
    def _():
        log_out[...] += logs

    resid[...] += dot(attended, w_out[...])


def attend(text, mem, w_qkv, lines, mark_q, mark_k, w_out):
    width = text.shape[1]
    count = text.shape[0] + mem.shape[0]
    whole = lambda shape: pl.BlockSpec(shape, lambda j: (0, 0))
    cols = lambda height, base: pl.BlockSpec((height, 256), lambda j: (0, base + j))
    low = jax.ShapeDtypeStruct((count, width), BF16)
    return pl.pallas_call(
        attend_kernel,
        grid=(3,),
        in_specs=[
            whole(text.shape),
            whole(mem.shape),
            cols(width, 0),
            cols(width, 3),
            cols(width, 6),
            cols(16, 0),
            whole((16, width)),
            whole((count, 128)),
            whole((count, 128)),
            pl.BlockSpec((256, width), lambda j: (j, 0)),
        ],
        out_specs=[
            cols(count, 0),
            cols(count, 0),
            cols(count, 0),
            cols(count, 0),
            whole((count, 128)),
            whole((count, width)),
        ],
        out_shape=[
            low,
            low,
            low,
            low,
            jax.ShapeDtypeStruct((count, 128), F32),
            jax.ShapeDtypeStruct((count, width), F32),
        ],
        compiler_params=pltpu.CompilerParams(vmem_limit_bytes=VMEM_ASK),
        cost_estimate=cost(15),
        name="attend",
    )(text, mem, w_qkv, w_qkv, w_qkv, lines, lines, mark_q, mark_k, w_out)


def feed_kernel(resid, lines, w_in, w_down, cot_text, cot_mem,
                result_out, g_two, inner_out, sums_out, sums_in_out, grad_down_out, grad_in_out,
                hidden_low, hidden_turned, g_low, act_all, slope_all):
    step = pl.program_id(0)
    half = pl.num_programs(0) // 2
    width = resid.shape[1]
    cuts = w_in.shape[1] // width

    @pl.when(step == 0)
    def _():
        normal, _ = norm_parts(resid[...])
        hidden = normal * lines[3:4, :] + lines[4:5, :]
        hidden_low[...] = hidden.astype(BF16)
        hidden_turned[...] = hidden.astype(BF16).T
        g_two[...] = hidden + lines[5:6, :]

    @pl.when(step < half)
    def _():
        total = g_two[...]
        for cut in range(cuts):
            span = slice(cut * width, (cut + 1) * width)
            part = step * cuts + cut
            inner = dot(hidden_low[...], w_in[:, span]) + lines[pl.ds(8 + part, 1), :]
            phi = 0.5 * (1.0 + lax.erf(inner * (0.5**0.5)))
            act = (inner * phi).astype(BF16)
            act_all[part] = act
            slope = phi + inner * jnp.exp(-0.5 * inner * inner) * 0.3989422804014327
            slope_all[part] = slope.astype(BF16)
            total += dot(act, w_down[span, :])
        g_two[...] = total

    @pl.when(step == half - 1)
    def _():
        normal, scale = norm_parts(g_two[...])
        result = normal * lines[6:7, :] + lines[7:8, :]
        pack_rows(result_out, result.astype(BF16), cot_text.shape[0])
        grad = jnp.concatenate([cot_text[...], cot_mem[...]], axis=0).astype(F32)
        sums_out[0:1, :] = column_sum(grad * normal)
        sums_out[1:2, :] = column_sum(grad)
        grad = norm_back(grad * lines[6:7, :], normal, scale)
        sums_out[2:3, :] = column_sum(grad)
        g_two[...] = grad
        g_low[...] = grad.astype(BF16)

    @pl.when(step >= half)
    def _():
        for cut in range(cuts):
            span = slice(cut * width, (cut + 1) * width)
            part = (step - half) * cuts + cut
            g_inner = dot_nt(g_low[...], w_down[span, :]) * slope_all[part].astype(F32)
            sums_in_out[0:1, span] = column_sum(g_inner)
            g_inner_low = g_inner.astype(BF16)
            inner_out[:, span] = g_inner_low
            grad_down_out[span, :] = dot_tn(act_all[part], g_low[...]).astype(BF16)
            grad_in_out[cut] = dot(hidden_turned[...], g_inner_low).astype(BF16)


def feed(resid, lines, w_in, w_down, cot_text, cot_mem, packed):
    count, width = resid.shape
    wide = w_in.shape[1]
    parts, cuts = wide // width, 2
    half = parts // cuts
    chunk = cuts * width
    whole = lambda shape: pl.BlockSpec(shape, lambda j: (0,) * len(shape))
    late = lambda j: jnp.maximum(j - half, 0)
    full = whole((count, width))
    high = jax.ShapeDtypeStruct((count, width), F32)
    return pl.pallas_call(
        feed_kernel,
        grid=(2 * half,),
        in_specs=[
            full,
            whole(lines.shape),
            pl.BlockSpec((width, chunk), lambda j: (0, jnp.minimum(j, half - 1))),
            pl.BlockSpec((chunk, width), lambda j: (j % half, 0)),
            whole(cot_text.shape),
            whole(cot_mem.shape),
        ],
        out_specs=[
            whole(packed),
            full,
            pl.BlockSpec((count, chunk), lambda j: (0, late(j))),
            whole((8, width)),
            pl.BlockSpec((8, chunk), lambda j: (0, late(j))),
            pl.BlockSpec((chunk, width), lambda j: (late(j), 0)),
            pl.BlockSpec((cuts, width, width), lambda j: (late(j), 0, 0)),
        ],
        out_shape=[
            jax.ShapeDtypeStruct(packed, BF16),
            high,
            jax.ShapeDtypeStruct((count, wide), BF16),
            jax.ShapeDtypeStruct((8, width), F32),
            jax.ShapeDtypeStruct((8, wide), F32),
            jax.ShapeDtypeStruct((wide, width), BF16),
            jax.ShapeDtypeStruct((parts, width, width), BF16),
        ],
        scratch_shapes=[
            pltpu.VMEM((count, width), BF16),
            pltpu.VMEM((width, count), BF16),
            pltpu.VMEM((count, width), BF16),
            pltpu.VMEM((parts, count, width), BF16),
            pltpu.VMEM((parts, count, width), BF16),
        ],
        compiler_params=pltpu.CompilerParams(vmem_limit_bytes=VMEM_ASK),
        cost_estimate=cost(28),
        name="feed",
    )(resid, lines, w_in, w_down, cot_text, cot_mem)


def backward_kernel(g_two, g_inner, w_in, resid, lines, text, mem, q, k, v, att, logs, mark_q, mark_k,
                    w_out, w_q, w_k, w_v, sums_two, sums_in, scalars, result,
                    mine_out, theirs_out, packed_out, g_rows, g_low, rows_turned, sums):
    step = pl.program_id(0)
    parts = pl.num_programs(0) - 3

    @pl.when(step == 0)
    def _():
        x = jnp.concatenate([text[...], mem[...]], axis=0)
        rows_turned[...] = x.T
        g_rows[...] = g_two[...]
        packed_out[:, : result.shape[1]] = result[...]

    @pl.when(step < parts)
    def _():
        g_rows[...] += dot_nt(g_inner[...], w_in[...])

    @pl.when(step == parts - 1)
    def _():
        normal, scale = norm_parts(resid[...])
        g_hidden = g_rows[...]
        sums[2:3, :] = column_sum(g_hidden * normal)
        sums[3:4, :] = column_sum(g_hidden)
        grad = norm_back(g_hidden * lines[3:4, :], normal, scale)
        sums[4:5, :] = column_sum(grad)
        g_rows[...] = grad
        g_low[...] = grad.astype(BF16)

    @pl.when(step >= parts)
    def _():
        attend_back_step(step - parts, text, mem, q, k, v, att, logs, mark_q, mark_k, g_low, w_out,
                         w_q, w_k, w_v, sums_two, sums_in, scalars,
                         mine_out, theirs_out, packed_out, g_rows, rows_turned, sums)


def attend_back_step(step, text, mem, q, k, v, att, logs, mark_q, mark_k, g_low, w_out,
                     w_q, w_k, w_v, sums_two, sums_in, scalars,
                     mine_out, theirs_out, packed_out, g_rows, rows_turned, sums):
    core = scalars[0, 1]
    split = text.shape[0]
    count = split + mem.shape[0]
    width = text.shape[1]
    query, key, value, attended = q[...], k[...], v[...], att[...]

    def put(half, start, part):
        rows = pl.ds(pl.multiple_of(start, 16), part.shape[0])

        @pl.when(core == half)
        def _():
            mine_out[rows, :] = part

        @pl.when(core != half)
        def _():
            theirs_out[rows, :] = part

    blocks = width // 128
    group_rows = mine_out.shape[0] // 2
    grad_w_out = dot_tn(attended, g_low[...]).astype(BF16)
    for block in range(blocks):
        part = grad_w_out[:, 128 * block : 128 * block + 128]
        put(1, group_rows + block * width + 256 * step, part)
    g_att = dot_nt(g_low[...], w_out[...])
    g_att_low = g_att.astype(BF16)
    scaled = query * jnp.asarray(0.125, BF16)
    product = g_att_low.astype(F32) * attended.astype(F32)
    lane = lanes_of((count, 128))
    none = jnp.asarray(0, BF16)
    thirds = ((lane >= 4) & (lane < 7)).astype(BF16)
    mq, mk = mark_q[...], mark_k[...] + thirds
    log_all = logs[...]

    def extra(column, base):
        high, middle, low = split_three(-column)
        wide = jnp.where(lane == 4, high, jnp.where(lane == 5, middle, low))
        return jnp.where((lane >= 4) & (lane < 7), wide, base)

    g_querys, g_keys, g_values = [], [], []
    for pair in range(2):
        span = slice(128 * pair, 128 * pair + 128)
        key_pair = key[:, span]
        key_wide = jnp.concatenate([key_pair, mk], axis=1)
        value_wide = jnp.concatenate([value[:, span], thirds], axis=1)
        key_turned = key_pair.astype(F32).T
        turned = lax.broadcasted_iota(jnp.int32, key_turned.shape, 0)
        g_query = g_key = g_value = None
        for side in range(2):
            own = lane // 64 == side
            mine = jnp.where(own, scaled[:, span], none)
            head = 4 * step + 2 * pair + side
            log_own = jnp.sum(jnp.where(lane == head, log_all, 0.0), axis=1, keepdims=True)
            query_wide = jnp.concatenate([mine, extra(log_own, mq)], axis=1)
            probs = jnp.exp(dot_nt(key_wide, query_wide))
            g_mine = jnp.where(own, g_att_low[:, span], none)
            delta = jnp.sum(jnp.where(own, product[:, span], 0.0), axis=1, keepdims=True)
            g_wide = jnp.concatenate([g_mine, extra(delta, jnp.zeros_like(mq))], axis=1)
            g_scores = (probs * dot_nt(value_wide, g_wide)).astype(BF16)
            part_v = dot(probs.astype(BF16), g_mine)
            part_k = dot(g_scores, mine)
            turned_own = jnp.where(turned // 64 == side, key_turned, 0.0).astype(BF16)
            part_q = dot(turned_own, g_scores)
            if side == 0:
                g_query, g_key, g_value = part_q, part_k, part_v
            else:
                g_query, g_key, g_value = g_query + part_q, g_key + part_k, g_value + part_v
        g_querys.append(g_query.T * 0.125)
        g_keys.append(g_key)
        g_values.append(g_value)
    g_query = jnp.concatenate(g_querys, axis=1)
    g_key = jnp.concatenate(g_keys, axis=1)
    g_value = jnp.concatenate(g_values, axis=1)
    columns = pl.ds(pl.multiple_of(256 * step, 256), 256)
    sums[0:1, columns] = column_sum(g_query)
    sums[1:2, columns] = column_sum(g_value)
    total = g_rows[...]
    for place, (grad, weight) in enumerate(((g_query, w_q), (g_key, w_k), (g_value, w_v))):
        low = grad.astype(BF16)
        grad_w = dot(rows_turned[...], low).astype(BF16)
        for block in range(2):
            part = grad_w[:, 128 * block : 128 * block + 128]
            put(place // 2, (place % 2) * group_rows + (2 * step + block) * width, part)
        total += dot_nt(low, weight[...])
    g_rows[...] = total

    @pl.when(step == 2)
    def _():
        reset = scalars[0, 0] == 1
        g_mem = total[split:]
        zero = jnp.zeros_like(g_mem)
        g_kept = jnp.where(reset, zero, g_mem)
        g_all = jnp.concatenate([total[:split], g_kept], axis=0).astype(BF16)
        pack_rows(packed_out, g_all, split, packed_out.shape[1] // 2)
        sums[5:8, :] = sums_two[0:3, :]
        for place in range(4):
            sums[8 + place : 9 + place, :] = sums_in[0:1, place * width : (place + 1) * width]
        sums[12:16, :] = jnp.zeros((4, width), F32)
        small = [jnp.where(reset, g_mem, zero).astype(BF16), sums[...].astype(BF16)]
        small = jnp.concatenate(small, axis=0)
        base = blocks * width
        empty = jnp.zeros((SPARE_ROWS, 128), BF16)
        for place in range(2):
            rows = slice(place * group_rows + base, (place + 1) * group_rows)
            mine_out[rows, :] = empty
            theirs_out[rows, :] = empty
        for place in range(2):
            for block in range(blocks):
                start = place * group_rows + base + block * small.shape[0]
                put(0, start, small[:, 128 * block : 128 * block + 128])


def backward(g_two, g_inner, w_in, resid, lines, text, mem, q, k, v, att, logs, mark_q, mark_k,
             w_out, w_qkv, sums_two, sums_in, scalars, result):
    width = text.shape[1]
    count = text.shape[0] + mem.shape[0]
    chunk = 2 * width
    parts = w_in.shape[1] // chunk
    whole = lambda shape: pl.BlockSpec(shape, lambda j: (0,) * len(shape))
    early = lambda height: pl.BlockSpec((height, chunk), lambda j: (0, jnp.minimum(j, parts - 1)))
    quad = lambda j: jnp.maximum(j - parts, 0)
    cols = lambda height, base: pl.BlockSpec((height, 256), lambda j: (0, base + quad(j)))
    full = whole((count, width))
    mark = whole((count, 128))
    height = 2 * (width // 128 * width + SPARE_ROWS)
    half = jax.ShapeDtypeStruct((height, 128), BF16)
    packed = (result.shape[0], 2 * result.shape[1], width)
    return pl.pallas_call(
        backward_kernel,
        grid=(parts + 3,),
        in_specs=[
            full,
            early(count),
            early(width),
            full,
            whole(lines.shape),
            whole(text.shape),
            whole(mem.shape),
            cols(count, 0),
            cols(count, 0),
            cols(count, 0),
            cols(count, 0),
            mark,
            mark,
            mark,
            pl.BlockSpec((256, width), lambda j: (quad(j), 0)),
            cols(width, 0),
            cols(width, 3),
            cols(width, 6),
            whole(sums_two.shape),
            whole(sums_in.shape),
            pl.BlockSpec(memory_space=pltpu.SMEM),
            whole(result.shape),
        ],
        out_specs=[whole((height, 128)), whole((height, 128)), whole(packed)],
        out_shape=[half, half, jax.ShapeDtypeStruct(packed, BF16)],
        scratch_shapes=[
            pltpu.VMEM((count, width), F32),
            pltpu.VMEM((count, width), BF16),
            pltpu.VMEM((width, count), BF16),
            pltpu.VMEM((16, width), F32),
        ],
        compiler_params=pltpu.CompilerParams(vmem_limit_bytes=VMEM_ASK),
        cost_estimate=cost(33),
        name="backward",
    )(g_two, g_inner, w_in, resid, lines, text, mem, q, k, v, att, logs, mark_q, mark_k,
      w_out, w_qkv, w_qkv, w_qkv, sums_two, sums_in, scalars, result)


def widen_kernel(first, second, groups, *refs):
    early = len(refs) == 5
    if early:
        qkv_out, out_out, small_out, wide, sems = refs
    else:
        qkv_out, out_out, wide, sems = refs[-4:]
    width = wide.shape[1]

    def copies(place):
        group = groups[0, place]
        columns = pl.ds(pl.multiple_of(jnp.minimum(group, 2) * width, width), width)
        to_qkv = pltpu.make_async_copy(wide.at[place], qkv_out.at[:, columns], sems.at[place])
        to_out = pltpu.make_async_copy(wide.at[place], out_out, sems.at[place])
        return group < 3, to_qkv, to_out

    for place, piece in enumerate((first, second)):
        for block in range(width // 128):
            rows = slice(block * width, (block + 1) * width)
            wide[place, :, 128 * block : 128 * block + 128] = piece[rows, :].astype(F32)
        in_qkv, to_qkv, to_out = copies(place)

        if early:

            @pl.when(groups[0, place] < 2)
            def _():
                height = small_out.shape[0]
                for block in range(width // 128):
                    start = width // 128 * width + block * height
                    part = piece[start : start + height, :].astype(F32)
                    small_out[:, 128 * block : 128 * block + 128] = part

        @pl.when(in_qkv)
        def _():
            to_qkv.start()

        @pl.when(jnp.logical_not(in_qkv))
        def _():
            to_out.start()

    for place in range(2):
        in_qkv, to_qkv, to_out = copies(place)

        @pl.when(in_qkv)
        def _():
            to_qkv.wait()

        @pl.when(jnp.logical_not(in_qkv))
        def _():
            to_out.wait()


def widen(first, second, groups, width, partly=()):
    vmem = pl.BlockSpec(memory_space=pltpu.VMEM)
    hbm = pl.BlockSpec(memory_space=pl.ANY)
    return pl.pallas_call(
        widen_kernel,
        in_specs=[vmem, vmem, pl.BlockSpec(memory_space=pltpu.SMEM)]
        + [hbm] * len(partly),
        out_specs=[hbm, hbm] + ([] if partly else [vmem]),
        out_shape=[
            jax.ShapeDtypeStruct((width, 3 * width), F32),
            jax.ShapeDtypeStruct((width, width), F32),
        ]
        + ([] if partly else [jax.ShapeDtypeStruct((48, width), F32)]),
        scratch_shapes=[pltpu.VMEM((2, width, width), F32), pltpu.SemaphoreType.DMA((2,))],
        input_output_aliases={3: 0, 4: 1} if partly else {},
        compiler_params=pltpu.CompilerParams(vmem_limit_bytes=VMEM_ASK),
        cost_estimate=cost(4),
        name="widen",
    )(first, second, groups, *partly)


def widen_feed_kernel(down, inward, down_out, in_out, low, high, in_sems, out_sems):
    count, width = inward.shape[0], inward.shape[2]
    low_rows = low.shape[1]
    cut = width // low_rows
    places = []
    for part in range(count):
        for piece in range(cut):
            rows = pl.ds(piece * low_rows, low_rows)
            tall = pl.ds(part * width + piece * low_rows, low_rows)
            columns = pl.ds(part * width, width)
            places.append((inward.at[part, rows], in_out.at[rows, columns]))
            places.append((down.at[tall], down_out.at[tall]))
    fetches, sends = [], []
    for place, (source, target) in enumerate(places):
        fetches.append(pltpu.make_async_copy(source, low.at[place], in_sems.at[place]))
        sends.append(pltpu.make_async_copy(high.at[place], target, out_sems.at[place]))
        fetches[-1].start()
    for place in range(len(places)):
        fetches[place].wait()
        high[place] = low[place].astype(F32)
        sends[place].start()
    for send in sends:
        send.wait()


def widen_feed(down, inward):
    count, height, width = inward.shape
    cut = 2
    blocks = 2 * count * cut
    hbm = pl.BlockSpec(memory_space=pl.ANY)
    return pl.pallas_call(
        widen_feed_kernel,
        in_specs=[hbm, hbm],
        out_specs=[hbm, hbm],
        out_shape=[
            jax.ShapeDtypeStruct(down.shape, F32),
            jax.ShapeDtypeStruct((height, count * width), F32),
        ],
        scratch_shapes=[
            pltpu.VMEM((blocks, height // cut, width), BF16),
            pltpu.VMEM((blocks, height // cut, width), F32),
            pltpu.SemaphoreType.DMA((blocks,)),
            pltpu.SemaphoreType.DMA((blocks,)),
        ],
        compiler_params=pltpu.CompilerParams(vmem_limit_bytes=VMEM_ASK),
        cost_estimate=cost(9),
        name="widen_feed",
    )(down, inward)


def ring_partner(place, way):
    return place ^ 1 if way == 0 else 3 - place


def ring_pairs(step):
    pairs = []
    for place in range(4):
        for core in range(2):
            other = ring_partner(place, (step + core) % 2)
            pairs.append((2 * place + core, 2 * other + core))
    return pairs


def ring_side(axis, step):
    place, core = lax.axis_index(axis), lax.axis_index("core")
    return jnp.where((step + core) % 2 == 0, (place + 1) // 2 % 2, place // 2)


def ring_swap(value, axis, step):
    return lax.ppermute(value, (axis, "core"), ring_pairs(step))


def core_swap(value):
    return lax.ppermute(value, "core", [(0, 1), (1, 0)])


def add_pair(pair):
    return (pair[0].astype(F32) + pair[1].astype(F32)).astype(BF16)


def half_of(pair, side):
    half = pair[0].shape[0] // 2
    return add_pair([lax.dynamic_slice_in_dim(part, side * half, half, 0) for part in pair])


def ring_halve(pair, axis, step):
    side = ring_side(axis, step)
    got = ring_swap(half_of(pair, 1 - side), axis, step)
    return half_of(pair, side), got


def ring_join(value, axis, step):
    got = ring_swap(value, axis, step)
    return jnp.where(
        ring_side(axis, step) == 0,
        jnp.concatenate([value, got], axis=0),
        jnp.concatenate([got, value], axis=0),
    )


def to_segments(value):
    return lax.all_to_all(value, BLK, 0, 1, tiled=True)[0]


def after(value, other):
    return lax.optimization_barrier((value, other))[0]


def doc_marks(docs, mem_count):
    kinds = (docs[:, None] == jnp.arange(3)[None]).astype(F32)
    rest = mem_count + ROW_PAD
    total = docs.shape[0] + rest
    spare = (jnp.arange(total) >= total - ROW_PAD).astype(F32)[:, None]
    query = jnp.concatenate([jnp.pad(kinds, ((0, rest), (0, 0))), jnp.ones((total, 1), F32)], 1)
    key = jnp.concatenate([jnp.pad(kinds - 1.0, ((0, rest), (0, 0))), -spare], 1) * BAN
    fill = ((0, 0), (0, 128 - query.shape[1]))
    return jnp.pad(query, fill).astype(BF16), jnp.pad(key, fill).astype(BF16)


def local(
    tokens,
    memory,
    mem_init,
    reset_flags,
    doc_ids,
    w_qkv,
    b_query,
    b_value,
    w_out,
    b_out,
    norm1_gain,
    norm1_bias,
    w_in,
    b_in,
    w_down,
    b_down,
    norm2_gain,
    norm2_bias,
    out_cot,
    mem_cot,
):
    seg_count, tok_count, width = tokens.shape
    mem_count = memory.shape[1]
    place = lax.axis_index(BLK)
    pick = lambda value: lax.dynamic_index_in_dim(value, place, 0, keepdims=False)
    fill = lambda value: jnp.pad(value, ((0, ROW_PAD), (0, 0)))
    packed = (seg_count, tok_count + mem_count + ROW_PAD, width)
    my_flag = pick(reset_flags)
    mark_q, mark_k = doc_marks(pick(doc_ids), mem_count)
    mem = fill(jnp.where(my_flag == 1, mem_init, pick(memory)))
    cot_mem = fill(pick(mem_cot))
    text = to_segments(tokens)
    cot_text = to_segments(after(out_cot, text))

    lines = jnp.concatenate(
        [b_query, b_value, b_out, norm1_gain, norm1_bias, b_down, norm2_gain, norm2_bias, b_in]
    )
    lines = jnp.pad(lines.astype(F32).reshape(-1, width), ((0, 4), (0, 0)))
    q, k, v, att, logs, resid = attend(text, mem, w_qkv, lines, mark_q, mark_k, w_out)
    result, g_two, g_inner, sums_two, sums_in, grad_down, grad_in = feed(
        resid, lines, w_in, w_down, cot_text, cot_mem, packed
    )
    grad_down, grad_in = lax.psum((grad_down, grad_in), ALL)
    scalars = jnp.stack([my_flag, lax.axis_index("core")]).reshape(1, 2).astype(jnp.int32)
    small_count = mem_count + ROW_PAD + 16

    def attention_back(operands):
        result, g_two, g_inner, sums_two, sums_in = operands
        mine, theirs, g_packed = backward(
            g_two,
            g_inner,
            w_in,
            resid,
            lines,
            text,
            mem,
            q,
            k,
            v,
            att,
            logs,
            mark_q,
            mark_k,
            w_out,
            w_qkv,
            sums_two,
            sums_in,
            scalars,
            result,
        )
        pair = (mine, core_swap(theirs))
        for step in (0, 1):
            pair = ring_halve(pair, RING[0], step)
        both = lax.all_to_all(after(g_packed, pair[0]), BLK, 0, 0, tiled=True)
        for step in (0, 1):
            pair = ring_halve(pair, RING[1], step)
        for step in (0, 1):
            part = add_pair(pair)
            pair = (part, ring_swap(part, RING[2], step))
        mine = add_pair(pair)
        for step in (1, 0):
            mine = ring_join(mine, RING[1], step)
        mine = ring_join(mine, RING[0], 1)
        pieces = []
        for base in (0, result.shape[1]):
            pieces.append(both[:, base : base + tok_count])
            pieces.append(both[:, base + tok_count : base + tok_count + mem_count])
        mine = after(mine, tuple(pieces))
        far, near = ring_swap(mine, RING[0], 0), core_swap(mine)
        core, height = lax.axis_index("core"), lax.axis_index(RING[0])
        sides = [(height + 1) // 2 % 2, height // 2]
        own = 2 * core + jnp.where(core == 0, sides[0], sides[1])
        other = 2 * (1 - core) + jnp.where(core == 0, sides[1], sides[0])
        groups = jnp.stack([own, other, own ^ 1, other ^ 1]).astype(jnp.int32).reshape(1, 4)
        *wide, small = widen(mine, near, groups[:, :2], width)
        start = small_count - 16
        vectors = [small[start + row] for row in range(8)]
        bin_rows = w_in.shape[1] // width
        vectors.append(small[start + 8 : start + 8 + bin_rows].reshape(-1))
        vectors.append(small[:mem_count])
        far, wide, vectors = lax.optimization_barrier((far, wide, vectors))
        wide = widen(far, core_swap(far), groups[:, 2:], width, wide)
        return *wide, *vectors, *pieces

    def nothing(operands):
        text_zero = jnp.zeros(tokens.shape, BF16)
        mem_zero = jnp.zeros(memory.shape, BF16)
        line = jnp.zeros((width,), F32)
        return (
            jnp.zeros(w_qkv.shape, F32),
            jnp.zeros(w_out.shape, F32),
            *[line] * 8,
            jnp.zeros(b_in.shape, F32),
            jnp.zeros(mem_init.shape, F32),
            text_zero,
            mem_zero,
            text_zero,
            mem_zero,
        )

    (
        grad_wqkv,
        grad_wout,
        grad_bquery,
        grad_bvalue,
        grad_gain1,
        grad_bias1,
        grad_bout,
        grad_gain2,
        grad_bias2,
        grad_bdown,
        grad_bin,
        grad_init,
        output,
        mem_output,
        grad_tokens,
        grad_memory,
    ) = lax.cond(
        reset_flags[0] >= 0, attention_back, nothing, (result, g_two, g_inner, sums_two, sums_in)
    )
    grad_down, grad_in = widen_feed(grad_down, grad_in)
    return (
        output,
        mem_output,
        grad_tokens,
        grad_memory,
        grad_init,
        grad_wqkv,
        grad_bquery,
        grad_bvalue,
        grad_wout,
        grad_bout,
        grad_gain1,
        grad_bias1,
        grad_in,
        grad_bin,
        grad_down,
        grad_bdown,
        grad_gain2,
        grad_bias2,
    )


def solution(mesh):
    chips = Mesh(mesh.devices.reshape(4, 4, 4, 2), ALL)
    placed = (
        P(SEG, BLK, None),
        P(SEG, None, None),
        P(),
        P(SEG),
        P(SEG, None),
        *([P()] * 13),
        P(SEG, BLK, None),
        P(SEG, None, None),
    )
    return jax.shard_map(
        local,
        mesh=chips,
        in_specs=placed,
        out_specs=(
            P(SEG, BLK, None),
            P(SEG, None, None),
            P(SEG, BLK, None),
            P(SEG, None, None),
            *([P()] * 14),
        ),
        check_vma=False,
    )
```

```python
import jax
import jax.numpy as jnp
from jax import lax
from jax.experimental import pallas as pl
from jax.experimental.pallas import tpu as pltpu
from jax.sharding import Mesh, PartitionSpec as P

F32 = jnp.float32
BF16 = jnp.bfloat16
HEADS = 12
EPS = 1e-12
BAN = 2.0**30
VMEM_ASK = 60 * 1024 * 1024
BLK = ("z", "core")
SEG = ("y", "x")
ALL = ("y", "x", "z", "core")
XYZ = ("x", "y", "z")
CHIPS = 64
ROW_PAD = 12
SPARE_ROWS = 256


def dot(left, right):
    return jnp.dot(left, right, preferred_element_type=F32)


def dot_nt(left, right):
    return lax.dot_general(left, right, (((1,), (1,)), ((), ())), preferred_element_type=F32)


def dot_tn(left, right):
    return lax.dot_general(left, right, (((0,), (0,)), ((), ())), preferred_element_type=F32)


def cost(micros):
    return pl.CostEstimate(flops=int(micros * 1e9), bytes_accessed=0, transcendentals=0)


def lanes_of(shape):
    return lax.broadcasted_iota(jnp.int32, shape, 1)


def split_three(value):
    high = value.astype(BF16)
    rest = value - high.astype(F32)
    middle = rest.astype(BF16)
    low = (rest - middle.astype(F32)).astype(BF16)
    return high, middle, low


def norm_parts(value):
    centre = jnp.mean(value, axis=-1, keepdims=True)
    centered = value - centre
    spread = jnp.mean(centered * centered, axis=-1, keepdims=True)
    scale = lax.rsqrt(spread + EPS)
    return centered * scale, scale


def norm_back(grad, normal, scale):
    mean_grad = jnp.mean(grad, axis=-1, keepdims=True)
    mean_prod = jnp.mean(grad * normal, axis=-1, keepdims=True)
    return scale * (grad - mean_grad - normal * mean_prod)


def pack_rows(out, value, split, base=0):
    blocks = out.shape[0]
    each = split // blocks
    rest = value.shape[0] - split
    for block in range(blocks):
        out[block, base : base + each] = value[block * each : (block + 1) * each]
        out[block, base + each : base + each + rest] = value[split:]


def column_sum(value):
    return jnp.sum(value, axis=0, keepdims=True)


def attend_kernel(text, mem, w_q, w_k, w_v, lines, lines_all, mark_q, mark_k, w_out,
                  q_out, k_out, v_out, att_out, log_out, resid):
    step = pl.program_id(0)
    x = jnp.concatenate([text[...], mem[...]], axis=0)
    count = x.shape[0]
    query = (dot(x, w_q[...]) + lines[0:1, :]).astype(BF16)
    key = dot(x, w_k[...]).astype(BF16)
    value = (dot(x, w_v[...]) + lines[1:2, :]).astype(BF16)
    q_out[...] = query
    k_out[...] = key
    v_out[...] = value
    scaled = query * jnp.asarray(0.125, BF16)
    lane = lanes_of((count, 128))
    ones = (lane == 0).astype(BF16)
    mq, mk = mark_q[...], mark_k[...]
    pairs = []
    logs = jnp.zeros((count, 128), F32)
    for pair in range(2):
        span = slice(128 * pair, 128 * pair + 128)
        key_wide = jnp.concatenate([key[:, span], mk], axis=1)
        value_wide = jnp.concatenate([value[:, span], ones], axis=1)
        outs = []
        for side in range(2):
            mine = jnp.where(lane // 64 == side, scaled[:, span], jnp.asarray(0, BF16))
            scores = dot_nt(jnp.concatenate([mine, mq], axis=1), key_wide)
            top = jnp.max(scores, axis=-1, keepdims=True)
            raised = jnp.exp(scores - top).astype(BF16)
            summed = dot(raised, value_wide)
            total = summed[:, 128:129]
            outs.append(summed[:, :128] / total)
            logs = jnp.where(lane == 4 * step + 2 * pair + side, top + jnp.log(total), logs)
        pairs.append(jnp.where(lane < 64, outs[0], outs[1]).astype(BF16))
    attended = jnp.concatenate(pairs, axis=1)
    att_out[...] = attended

    @pl.when(step == 0)
    def _():
        log_out[...] = logs
        resid[...] = x.astype(F32) + lines_all[2:3, :]

    @pl.when(step > 0)
    def _():
        log_out[...] += logs

    resid[...] += dot(attended, w_out[...])


def attend(text, mem, w_qkv, lines, mark_q, mark_k, w_out):
    width = text.shape[1]
    count = text.shape[0] + mem.shape[0]
    whole = lambda shape: pl.BlockSpec(shape, lambda j: (0, 0))
    cols = lambda height, base: pl.BlockSpec((height, 256), lambda j: (0, base + j))
    low = jax.ShapeDtypeStruct((count, width), BF16)
    return pl.pallas_call(
        attend_kernel,
        grid=(3,),
        in_specs=[
            whole(text.shape),
            whole(mem.shape),
            cols(width, 0),
            cols(width, 3),
            cols(width, 6),
            cols(16, 0),
            whole((16, width)),
            whole((count, 128)),
            whole((count, 128)),
            pl.BlockSpec((256, width), lambda j: (j, 0)),
        ],
        out_specs=[
            cols(count, 0),
            cols(count, 0),
            cols(count, 0),
            cols(count, 0),
            whole((count, 128)),
            whole((count, width)),
        ],
        out_shape=[
            low,
            low,
            low,
            low,
            jax.ShapeDtypeStruct((count, 128), F32),
            jax.ShapeDtypeStruct((count, width), F32),
        ],
        compiler_params=pltpu.CompilerParams(vmem_limit_bytes=VMEM_ASK),
        cost_estimate=cost(15),
        name="attend",
    )(text, mem, w_qkv, w_qkv, w_qkv, lines, lines, mark_q, mark_k, w_out)


def feed_kernel(resid, lines, w_in, w_down, cot_text, cot_mem,
                result_out, g_two, inner_out, sums_out, sums_in_out, grad_down_out, grad_in_out,
                hidden_low, hidden_turned, g_low, act_all, slope_all):
    step = pl.program_id(0)
    half = pl.num_programs(0) // 2
    width = resid.shape[1]
    cuts = w_in.shape[1] // width

    @pl.when(step == 0)
    def _():
        normal, _ = norm_parts(resid[...])
        hidden = normal * lines[3:4, :] + lines[4:5, :]
        hidden_low[...] = hidden.astype(BF16)
        hidden_turned[...] = hidden.astype(BF16).T
        g_two[...] = hidden + lines[5:6, :]

    @pl.when(step < half)
    def _():
        total = g_two[...]
        for cut in range(cuts):
            span = slice(cut * width, (cut + 1) * width)
            part = step * cuts + cut
            inner = dot(hidden_low[...], w_in[:, span]) + lines[pl.ds(8 + part, 1), :]
            phi = 0.5 * (1.0 + lax.erf(inner * (0.5**0.5)))
            act = (inner * phi).astype(BF16)
            act_all[part] = act
            slope = phi + inner * jnp.exp(-0.5 * inner * inner) * 0.3989422804014327
            slope_all[part] = slope.astype(BF16)
            total += dot(act, w_down[span, :])
        g_two[...] = total

    @pl.when(step == half - 1)
    def _():
        normal, scale = norm_parts(g_two[...])
        result = normal * lines[6:7, :] + lines[7:8, :]
        pack_rows(result_out, result.astype(BF16), cot_text.shape[0])
        grad = jnp.concatenate([cot_text[...], cot_mem[...]], axis=0).astype(F32)
        sums_out[0:1, :] = column_sum(grad * normal)
        sums_out[1:2, :] = column_sum(grad)
        grad = norm_back(grad * lines[6:7, :], normal, scale)
        sums_out[2:3, :] = column_sum(grad)
        g_two[...] = grad
        g_low[...] = grad.astype(BF16)

    @pl.when(step >= half)
    def _():
        for cut in range(cuts):
            span = slice(cut * width, (cut + 1) * width)
            part = (step - half) * cuts + cut
            g_inner = dot_nt(g_low[...], w_down[span, :]) * slope_all[part].astype(F32)
            sums_in_out[0:1, span] = column_sum(g_inner)
            g_inner_low = g_inner.astype(BF16)
            inner_out[:, span] = g_inner_low
            grad_down_out[span, :] = dot_tn(act_all[part], g_low[...]).astype(BF16)
            grad_in_out[cut] = dot(hidden_turned[...], g_inner_low).astype(BF16)


def feed(resid, lines, w_in, w_down, cot_text, cot_mem, packed):
    count, width = resid.shape
    wide = w_in.shape[1]
    parts, cuts = wide // width, 2
    half = parts // cuts
    chunk = cuts * width
    whole = lambda shape: pl.BlockSpec(shape, lambda j: (0,) * len(shape))
    late = lambda j: jnp.maximum(j - half, 0)
    full = whole((count, width))
    high = jax.ShapeDtypeStruct((count, width), F32)
    return pl.pallas_call(
        feed_kernel,
        grid=(2 * half,),
        in_specs=[
            full,
            whole(lines.shape),
            pl.BlockSpec((width, chunk), lambda j: (0, jnp.minimum(j, half - 1))),
            pl.BlockSpec((chunk, width), lambda j: (j % half, 0)),
            whole(cot_text.shape),
            whole(cot_mem.shape),
        ],
        out_specs=[
            whole(packed),
            full,
            pl.BlockSpec((count, chunk), lambda j: (0, late(j))),
            whole((8, width)),
            pl.BlockSpec((8, chunk), lambda j: (0, late(j))),
            pl.BlockSpec((chunk, width), lambda j: (late(j), 0)),
            pl.BlockSpec((cuts, width, width), lambda j: (late(j), 0, 0)),
        ],
        out_shape=[
            jax.ShapeDtypeStruct(packed, BF16),
            high,
            jax.ShapeDtypeStruct((count, wide), BF16),
            jax.ShapeDtypeStruct((8, width), F32),
            jax.ShapeDtypeStruct((8, wide), F32),
            jax.ShapeDtypeStruct((wide, width), BF16),
            jax.ShapeDtypeStruct((parts, width, width), BF16),
        ],
        scratch_shapes=[
            pltpu.VMEM((count, width), BF16),
            pltpu.VMEM((width, count), BF16),
            pltpu.VMEM((count, width), BF16),
            pltpu.VMEM((parts, count, width), BF16),
            pltpu.VMEM((parts, count, width), BF16),
        ],
        compiler_params=pltpu.CompilerParams(vmem_limit_bytes=VMEM_ASK),
        cost_estimate=cost(28),
        name="feed",
    )(resid, lines, w_in, w_down, cot_text, cot_mem)


def backward_kernel(g_two, g_inner, w_in, resid, lines, text, mem, q, k, v, att, logs, mark_q, mark_k,
                    w_out, w_q, w_k, w_v, sums_two, sums_in, scalars, result,
                    mine_out, theirs_out, packed_out, g_rows, g_low, rows_turned, sums):
    step = pl.program_id(0)
    parts = pl.num_programs(0) - 3

    @pl.when(step == 0)
    def _():
        x = jnp.concatenate([text[...], mem[...]], axis=0)
        rows_turned[...] = x.T
        g_rows[...] = g_two[...]
        packed_out[:, : result.shape[1]] = result[...]

    @pl.when(step < parts)
    def _():
        g_rows[...] += dot_nt(g_inner[...], w_in[...])

    @pl.when(step == parts - 1)
    def _():
        normal, scale = norm_parts(resid[...])
        g_hidden = g_rows[...]
        first = sums.shape[0] - 12
        sums[first + 2 : first + 3, :] = column_sum(g_hidden * normal)
        sums[first + 3 : first + 4, :] = column_sum(g_hidden)
        grad = norm_back(g_hidden * lines[3:4, :], normal, scale)
        sums[first + 4 : first + 5, :] = column_sum(grad)
        g_rows[...] = grad
        g_low[...] = grad.astype(BF16)

    @pl.when(step >= parts)
    def _():
        attend_back_step(step - parts, text, mem, q, k, v, att, logs, mark_q, mark_k, g_low, w_out,
                         w_q, w_k, w_v, sums_two, sums_in, scalars,
                         mine_out, theirs_out, packed_out, g_rows, rows_turned, sums)


def attend_back_step(step, text, mem, q, k, v, att, logs, mark_q, mark_k, g_low, w_out,
                     w_q, w_k, w_v, sums_two, sums_in, scalars,
                     mine_out, theirs_out, packed_out, g_rows, rows_turned, sums):
    core = scalars[0, 1]
    split = text.shape[0]
    count = split + mem.shape[0]
    width = text.shape[1]
    query, key, value, attended = q[...], k[...], v[...], att[...]

    def put(half, start, part):
        rows = pl.ds(pl.multiple_of(start, 16), part.shape[0])

        @pl.when(core == half)
        def _():
            mine_out[rows, :] = part

        @pl.when(core != half)
        def _():
            theirs_out[rows, :] = part

    blocks = width // 128
    group_rows = mine_out.shape[0] // 2
    piece_rows = group_rows // 2

    def start_of(group, block):
        piece = block // (blocks // 2)
        return group * group_rows + piece * piece_rows + block % (blocks // 2) * width

    grad_w_out = dot_tn(attended, g_low[...]).astype(BF16)
    for block in range(blocks):
        part = grad_w_out[:, 128 * block : 128 * block + 128]
        put(1, start_of(1, block) + 256 * step, part)
    g_att = dot_nt(g_low[...], w_out[...])
    g_att_low = g_att.astype(BF16)
    scaled = query * jnp.asarray(0.125, BF16)
    product = g_att_low.astype(F32) * attended.astype(F32)
    lane = lanes_of((count, 128))
    none = jnp.asarray(0, BF16)
    thirds = ((lane >= 4) & (lane < 7)).astype(BF16)
    mq, mk = mark_q[...], mark_k[...] + thirds
    log_all = logs[...]

    def extra(column, base):
        high, middle, low = split_three(-column)
        wide = jnp.where(lane == 4, high, jnp.where(lane == 5, middle, low))
        return jnp.where((lane >= 4) & (lane < 7), wide, base)

    g_querys, g_keys, g_values = [], [], []
    for pair in range(2):
        span = slice(128 * pair, 128 * pair + 128)
        key_pair = key[:, span]
        key_wide = jnp.concatenate([key_pair, mk], axis=1)
        value_wide = jnp.concatenate([value[:, span], thirds], axis=1)
        key_turned = key_pair.astype(F32).T
        turned = lax.broadcasted_iota(jnp.int32, key_turned.shape, 0)
        g_query = g_key = g_value = None
        for side in range(2):
            own = lane // 64 == side
            mine = jnp.where(own, scaled[:, span], none)
            head = 4 * step + 2 * pair + side
            log_own = jnp.sum(jnp.where(lane == head, log_all, 0.0), axis=1, keepdims=True)
            query_wide = jnp.concatenate([mine, extra(log_own, mq)], axis=1)
            probs = jnp.exp(dot_nt(key_wide, query_wide))
            g_mine = jnp.where(own, g_att_low[:, span], none)
            delta = jnp.sum(jnp.where(own, product[:, span], 0.0), axis=1, keepdims=True)
            g_wide = jnp.concatenate([g_mine, extra(delta, jnp.zeros_like(mq))], axis=1)
            g_scores = (probs * dot_nt(value_wide, g_wide)).astype(BF16)
            part_v = dot(probs.astype(BF16), g_mine)
            part_k = dot(g_scores, mine)
            turned_own = jnp.where(turned // 64 == side, key_turned, 0.0).astype(BF16)
            part_q = dot(turned_own, g_scores)
            if side == 0:
                g_query, g_key, g_value = part_q, part_k, part_v
            else:
                g_query, g_key, g_value = g_query + part_q, g_key + part_k, g_value + part_v
        g_querys.append(g_query.T * 0.125)
        g_keys.append(g_key)
        g_values.append(g_value)
    g_query = jnp.concatenate(g_querys, axis=1)
    g_key = jnp.concatenate(g_keys, axis=1)
    g_value = jnp.concatenate(g_values, axis=1)
    columns = pl.ds(pl.multiple_of(256 * step, 256), 256)
    first = sums.shape[0] - 12
    sums[first : first + 1, columns] = column_sum(g_query)
    sums[first + 1 : first + 2, columns] = column_sum(g_value)
    total = g_rows[...]
    for place, (grad, weight) in enumerate(((g_query, w_q), (g_key, w_k), (g_value, w_v))):
        low = grad.astype(BF16)
        grad_w = dot(rows_turned[...], low).astype(BF16)
        for block in range(2):
            part = grad_w[:, 128 * block : 128 * block + 128]
            put(place // 2, start_of(place % 2, 2 * step + block), part)
        total += dot_nt(low, weight[...])
    g_rows[...] = total

    @pl.when(step == 2)
    def _():
        reset = scalars[0, 0] == 1
        g_mem = total[split:]
        zero = jnp.zeros_like(g_mem)
        g_kept = jnp.where(reset, zero, g_mem)
        g_all = jnp.concatenate([total[:split], g_kept], axis=0).astype(BF16)
        pack_rows(packed_out, g_all, split, packed_out.shape[1] // 2)
        first = sums.shape[0] - 12
        sums[first + 5 : first + 8, :] = sums_two[0:3, :]
        for place in range(4):
            sums[first + 8 + place : first + 9 + place, :] = sums_in[0:1, place * width : (place + 1) * width]
        mem_count = sums.shape[0] - 12
        sums[0:mem_count, :] = jnp.where(reset, g_mem, zero)[0:mem_count]
        small = sums[...].astype(BF16)
        base = blocks // 2 * width
        empty = jnp.zeros((SPARE_ROWS, 128), BF16)
        for place in range(4):
            rows = slice(place * piece_rows + base, (place + 1) * piece_rows)
            mine_out[rows, :] = empty
            theirs_out[rows, :] = empty
        for place in range(2):
            for block in range(blocks):
                start = place * piece_rows + base + block * small.shape[0]
                put(0, start, small[:, 128 * block : 128 * block + 128])


def backward(g_two, g_inner, w_in, resid, lines, text, mem, q, k, v, att, logs, mark_q, mark_k,
             w_out, w_qkv, sums_two, sums_in, scalars, result):
    width = text.shape[1]
    count = text.shape[0] + mem.shape[0]
    chunk = 2 * width
    parts = w_in.shape[1] // chunk
    whole = lambda shape: pl.BlockSpec(shape, lambda j: (0,) * len(shape))
    early = lambda height: pl.BlockSpec((height, chunk), lambda j: (0, jnp.minimum(j, parts - 1)))
    quad = lambda j: jnp.maximum(j - parts, 0)
    cols = lambda height, base: pl.BlockSpec((height, 256), lambda j: (0, base + quad(j)))
    full = whole((count, width))
    mark = whole((count, 128))
    height = 2 * (width // 128 * width + 2 * SPARE_ROWS)
    half = jax.ShapeDtypeStruct((height, 128), BF16)
    packed = (result.shape[0], 2 * result.shape[1], width)
    return pl.pallas_call(
        backward_kernel,
        grid=(parts + 3,),
        in_specs=[
            full,
            early(count),
            early(width),
            full,
            whole(lines.shape),
            whole(text.shape),
            whole(mem.shape),
            cols(count, 0),
            cols(count, 0),
            cols(count, 0),
            cols(count, 0),
            mark,
            mark,
            mark,
            pl.BlockSpec((256, width), lambda j: (quad(j), 0)),
            cols(width, 0),
            cols(width, 3),
            cols(width, 6),
            whole(sums_two.shape),
            whole(sums_in.shape),
            pl.BlockSpec(memory_space=pltpu.SMEM),
            whole(result.shape),
        ],
        out_specs=[whole((height, 128)), whole((height, 128)), whole(packed)],
        out_shape=[half, half, jax.ShapeDtypeStruct(packed, BF16)],
        scratch_shapes=[
            pltpu.VMEM((count, width), F32),
            pltpu.VMEM((count, width), BF16),
            pltpu.VMEM((width, count), BF16),
            pltpu.VMEM((count - text.shape[0] - ROW_PAD + 12, width), F32),
        ],
        compiler_params=pltpu.CompilerParams(vmem_limit_bytes=VMEM_ASK),
        cost_estimate=cost(33),
        name="backward",
    )(g_two, g_inner, w_in, resid, lines, text, mem, q, k, v, att, logs, mark_q, mark_k,
      w_out, w_qkv, w_qkv, w_qkv, sums_two, sums_in, scalars, result)


def widen_kernel(*refs):
    pieces, codes = refs[:4], refs[4]
    early = len(refs) == 10
    if early:
        qkv_out, out_out, small_out, wide, sems = refs[5:]
    else:
        qkv_out, out_out, wide, sems = refs[-4:]
    width = wide.shape[1]
    part = wide.shape[2]
    blocks = part // 128

    def copies(place):
        code = codes[0, place]
        in_qkv = code < 6
        spot = jnp.where(in_qkv, code, code - 6)
        columns = pl.ds(pl.multiple_of(spot * part, part), part)
        to_qkv = pltpu.make_async_copy(wide.at[place], qkv_out.at[:, columns], sems.at[place])
        to_out = pltpu.make_async_copy(wide.at[place], out_out.at[:, columns], sems.at[place])
        return in_qkv, to_qkv, to_out

    for place, piece in enumerate(pieces):
        for block in range(blocks):
            rows = slice(block * width, (block + 1) * width)
            wide[place, :, 128 * block : 128 * block + 128] = piece[rows, :].astype(F32)
        in_qkv, to_qkv, to_out = copies(place)

        if early:

            @pl.when(codes[0, place] < 2)
            def _():
                height = small_out.shape[0]
                for block in range(2 * blocks):
                    start = blocks * width + block * height
                    rows = piece[start : start + height, :].astype(F32)
                    small_out[:, 128 * block : 128 * block + 128] = rows

        @pl.when(in_qkv)
        def _():
            to_qkv.start()

        @pl.when(jnp.logical_not(in_qkv))
        def _():
            to_out.start()

    for place in range(4):
        in_qkv, to_qkv, to_out = copies(place)

        @pl.when(in_qkv)
        def _():
            to_qkv.wait()

        @pl.when(jnp.logical_not(in_qkv))
        def _():
            to_out.wait()


def widen(pieces, codes, width, small_count, partly=()):
    vmem = pl.BlockSpec(memory_space=pltpu.VMEM)
    hbm = pl.BlockSpec(memory_space=pl.ANY)
    return pl.pallas_call(
        widen_kernel,
        in_specs=[vmem] * 4 + [pl.BlockSpec(memory_space=pltpu.SMEM)] + [hbm] * len(partly),
        out_specs=[hbm, hbm] + ([] if partly else [vmem]),
        out_shape=[
            jax.ShapeDtypeStruct((width, 3 * width), F32),
            jax.ShapeDtypeStruct((width, width), F32),
        ]
        + ([] if partly else [jax.ShapeDtypeStruct((small_count, width), F32)]),
        scratch_shapes=[pltpu.VMEM((4, width, width // 2), F32), pltpu.SemaphoreType.DMA((4,))],
        input_output_aliases={5: 0, 6: 1} if partly else {},
        compiler_params=pltpu.CompilerParams(vmem_limit_bytes=VMEM_ASK),
        cost_estimate=cost(4),
        name="widen",
    )(*pieces, codes, *partly)


def widen_feed_kernel(down, inward, down_out, in_out, low, high, in_sems, out_sems):
    count, width = inward.shape[0], inward.shape[2]
    low_rows = low.shape[1]
    cut = width // low_rows
    places = []
    for part in range(count):
        for piece in range(cut):
            rows = pl.ds(piece * low_rows, low_rows)
            tall = pl.ds(part * width + piece * low_rows, low_rows)
            columns = pl.ds(part * width, width)
            places.append((inward.at[part, rows], in_out.at[rows, columns]))
            places.append((down.at[tall], down_out.at[tall]))
    fetches, sends = [], []
    for place, (source, target) in enumerate(places):
        fetches.append(pltpu.make_async_copy(source, low.at[place], in_sems.at[place]))
        sends.append(pltpu.make_async_copy(high.at[place], target, out_sems.at[place]))
        fetches[-1].start()
    for place in range(len(places)):
        fetches[place].wait()
        high[place] = low[place].astype(F32)
        sends[place].start()
    for send in sends:
        send.wait()


def widen_feed(down, inward):
    count, height, width = inward.shape
    cut = 2
    blocks = 2 * count * cut
    hbm = pl.BlockSpec(memory_space=pl.ANY)
    return pl.pallas_call(
        widen_feed_kernel,
        in_specs=[hbm, hbm],
        out_specs=[hbm, hbm],
        out_shape=[
            jax.ShapeDtypeStruct(down.shape, F32),
            jax.ShapeDtypeStruct((height, count * width), F32),
        ],
        scratch_shapes=[
            pltpu.VMEM((blocks, height // cut, width), BF16),
            pltpu.VMEM((blocks, height // cut, width), F32),
            pltpu.SemaphoreType.DMA((blocks,)),
            pltpu.SemaphoreType.DMA((blocks,)),
        ],
        compiler_params=pltpu.CompilerParams(vmem_limit_bytes=VMEM_ASK),
        cost_estimate=cost(9),
        name="widen_feed",
    )(down, inward)


def ring_partner(place, way):
    return place ^ 1 if way == 0 else 3 - place


def ring_pairs(step):
    pairs = []
    for place in range(4):
        for core in range(2):
            other = ring_partner(place, (step + core) % 2)
            pairs.append((2 * place + core, 2 * other + core))
    return pairs


def side_of(place, core, step):
    return jnp.where((step + core) % 2 == 0, (place + 1) // 2 % 2, place // 2)


def ring_side(axis, step):
    return side_of(lax.axis_index(axis), lax.axis_index("core"), step)


def ring_swap(value, axis, step):
    return lax.ppermute(value, (axis, "core"), ring_pairs(step))


def core_swap(value):
    return lax.ppermute(value, "core", [(0, 1), (1, 0)])


def add_pair(pair):
    return (pair[0].astype(F32) + pair[1].astype(F32)).astype(BF16)


def half_of(pair, side, start=0, rows=None):
    rows = pair[0].shape[-2] if rows is None else rows
    axis = pair[0].ndim - 2
    place = start + side * (rows // 2)
    return add_pair([lax.dynamic_slice_in_dim(part, place, rows // 2, axis) for part in pair])


def ring_halve(pair, axis, step, start=0, rows=None):
    side = ring_side(axis, step)
    got = ring_swap(half_of(pair, 1 - side, start, rows), axis, step)
    return half_of(pair, side, start, rows), got


def ring_join(value, axis, step):
    got = ring_swap(value, axis, step)
    return jnp.where(
        ring_side(axis, step) == 0,
        jnp.concatenate([value, got], axis=-2),
        jnp.concatenate([got, value], axis=-2),
    )


def to_segments(value):
    return lax.all_to_all(value, BLK, 0, 1, tiled=True)[0]


def after(value, other):
    return lax.optimization_barrier((value, other))[0]


def doc_marks(docs, mem_count):
    kinds = (docs[:, None] == jnp.arange(3)[None]).astype(F32)
    rest = mem_count + ROW_PAD
    total = docs.shape[0] + rest
    spare = (jnp.arange(total) >= total - ROW_PAD).astype(F32)[:, None]
    query = jnp.concatenate([jnp.pad(kinds, ((0, rest), (0, 0))), jnp.ones((total, 1), F32)], 1)
    key = jnp.concatenate([jnp.pad(kinds - 1.0, ((0, rest), (0, 0))), -spare], 1) * BAN
    fill = ((0, 0), (0, 128 - query.shape[1]))
    return jnp.pad(query, fill).astype(BF16), jnp.pad(key, fill).astype(BF16)


def local(
    tokens,
    memory,
    mem_init,
    reset_flags,
    doc_ids,
    w_qkv,
    b_query,
    b_value,
    w_out,
    b_out,
    norm1_gain,
    norm1_bias,
    w_in,
    b_in,
    w_down,
    b_down,
    norm2_gain,
    norm2_bias,
    out_cot,
    mem_cot,
):
    seg_count, tok_count, width = tokens.shape
    mem_count = memory.shape[1]
    place = lax.axis_index(BLK)
    pick = lambda value: lax.dynamic_index_in_dim(value, place, 0, keepdims=False)
    fill = lambda value: jnp.pad(value, ((0, ROW_PAD), (0, 0)))
    packed = (seg_count, tok_count + mem_count + ROW_PAD, width)
    my_flag = pick(reset_flags)
    mark_q, mark_k = doc_marks(pick(doc_ids), mem_count)
    mem = fill(jnp.where(my_flag == 1, mem_init, pick(memory)))
    cot_mem = fill(pick(mem_cot))
    text = to_segments(tokens)
    cot_text = to_segments(after(out_cot, text))

    lines = jnp.concatenate(
        [b_query, b_value, b_out, norm1_gain, norm1_bias, b_down, norm2_gain, norm2_bias, b_in]
    )
    lines = jnp.pad(lines.astype(F32).reshape(-1, width), ((0, 4), (0, 0)))
    q, k, v, att, logs, resid = attend(text, mem, w_qkv, lines, mark_q, mark_k, w_out)
    result, g_two, g_inner, sums_two, sums_in, grad_down, grad_in = feed(
        resid, lines, w_in, w_down, cot_text, cot_mem, packed
    )
    grad_down, grad_in = lax.psum((grad_down, grad_in), ALL)
    scalars = jnp.stack([my_flag, lax.axis_index("core")]).reshape(1, 2).astype(jnp.int32)
    small_count = mem_count + 12

    def attention_back(operands):
        result, g_two, g_inner, sums_two, sums_in = operands
        mine, theirs, g_packed = backward(
            g_two,
            g_inner,
            w_in,
            resid,
            lines,
            text,
            mem,
            q,
            k,
            v,
            att,
            logs,
            mark_q,
            mark_k,
            w_out,
            w_qkv,
            sums_two,
            sums_in,
            scalars,
            result,
        )
        pair = (mine, core_swap(theirs))
        rows = mine.shape[0] // 2
        over_z = ring_halve(pair, "z", 0, 0, rows)
        over_x = ring_halve(pair, "x", 0, rows, rows)
        over_z = ring_halve(over_z, "z", 1)
        over_x = ring_halve(over_x, "x", 1)
        both = lax.all_to_all(after(g_packed, over_z[0]), BLK, 0, 0, tiled=True)
        side = ring_side("y", 0)
        got = ring_swap(jnp.stack([half_of(over_z, 1 - side), half_of(over_x, 1 - side)]), "y", 0)
        pair = (jnp.stack([half_of(over_z, side), half_of(over_x, side)]), got)
        pair = ring_halve(pair, "y", 1)
        over_z, over_x = add_pair([part[0] for part in pair]), add_pair([part[1] for part in pair])
        for step in (0, 1):
            got_z, got_x = ring_swap(over_z, "x", step), ring_swap(over_x, "z", step)
            over_z, over_x = add_pair((over_z, got_z)), add_pair((over_x, got_x))
        joined = after(jnp.stack([over_z, over_x]), both)
        for step in (1, 0):
            joined = ring_join(joined, "y", step)
        over_z = ring_join(joined[0], "z", 1)
        over_x = ring_join(joined[1], "x", 1)
        pieces = []
        for base in (0, result.shape[1]):
            pieces.append(both[:, base : base + tok_count])
            pieces.append(both[:, base + tok_count : base + tok_count + mem_count])
        over_z, over_x = after((over_z, over_x), tuple(pieces))
        far = [ring_swap(over_z, "z", 0), ring_swap(over_x, "x", 0)]
        near = [core_swap(over_z), core_swap(over_x)]
        core = lax.axis_index("core")
        codes = []
        for where in (core, 1 - core):
            for group, axis in enumerate(("z", "x")):
                codes.append(4 * where + 2 * group + side_of(lax.axis_index(axis), where, 0))
        codes = jnp.stack(codes).astype(jnp.int32).reshape(1, 4)
        *wide, small = widen([over_z, over_x, *near], codes, width, small_count)
        start = mem_count
        vectors = [small[start + row] for row in range(8)]
        bin_rows = w_in.shape[1] // width
        vectors.append(small[start + 8 : start + 8 + bin_rows].reshape(-1))
        vectors.append(small[:mem_count])
        far, wide, vectors = lax.optimization_barrier((far, wide, vectors))
        far = [*far, core_swap(far[0]), core_swap(far[1])]
        wide = widen(far, codes ^ 1, width, small_count, wide)
        return *wide, *vectors, *pieces

    def nothing(operands):
        text_zero = jnp.zeros(tokens.shape, BF16)
        mem_zero = jnp.zeros(memory.shape, BF16)
        line = jnp.zeros((width,), F32)
        return (
            jnp.zeros(w_qkv.shape, F32),
            jnp.zeros(w_out.shape, F32),
            *[line] * 8,
            jnp.zeros(b_in.shape, F32),
            jnp.zeros(mem_init.shape, F32),
            text_zero,
            mem_zero,
            text_zero,
            mem_zero,
        )

    (
        grad_wqkv,
        grad_wout,
        grad_bquery,
        grad_bvalue,
        grad_gain1,
        grad_bias1,
        grad_bout,
        grad_gain2,
        grad_bias2,
        grad_bdown,
        grad_bin,
        grad_init,
        output,
        mem_output,
        grad_tokens,
        grad_memory,
    ) = lax.cond(
        reset_flags[0] >= 0, attention_back, nothing, (result, g_two, g_inner, sums_two, sums_in)
    )
    grad_down, grad_in = widen_feed(grad_down, grad_in)
    return (
        output,
        mem_output,
        grad_tokens,
        grad_memory,
        grad_init,
        grad_wqkv,
        grad_bquery,
        grad_bvalue,
        grad_wout,
        grad_bout,
        grad_gain1,
        grad_bias1,
        grad_in,
        grad_bin,
        grad_down,
        grad_bdown,
        grad_gain2,
        grad_bias2,
    )


def solution(mesh):
    chips = Mesh(mesh.devices.reshape(4, 4, 4, 2), ALL)
    placed = (
        P(SEG, BLK, None),
        P(SEG, None, None),
        P(),
        P(SEG),
        P(SEG, None),
        *([P()] * 13),
        P(SEG, BLK, None),
        P(SEG, None, None),
    )
    return jax.shard_map(
        local,
        mesh=chips,
        in_specs=placed,
        out_specs=(
            P(SEG, BLK, None),
            P(SEG, None, None),
            P(SEG, BLK, None),
            P(SEG, None, None),
            *([P()] * 14),
        ),
        check_vma=False,
    )
```

```python
import jax
import jax.numpy as jnp
from jax import lax
from jax.experimental import pallas as pl
from jax.experimental.pallas import tpu as pltpu
from jax.sharding import Mesh, PartitionSpec as P

F32 = jnp.float32
BF16 = jnp.bfloat16
HEADS = 12
EPS = 1e-12
BAN = 2.0**30
VMEM_ASK = 60 * 1024 * 1024
BLK = ("z", "core")
SEG = ("y", "x")
ALL = ("y", "x", "z", "core")
XYZ = ("x", "y", "z")
CHIPS = 64
ROW_PAD = 12
SPARE_ROWS = 256


def dot(left, right):
    return jnp.dot(left, right, preferred_element_type=F32)


def dot_nt(left, right):
    return lax.dot_general(left, right, (((1,), (1,)), ((), ())), preferred_element_type=F32)


def dot_tn(left, right):
    return lax.dot_general(left, right, (((0,), (0,)), ((), ())), preferred_element_type=F32)


def cost(micros):
    return pl.CostEstimate(flops=int(micros * 1e9), bytes_accessed=0, transcendentals=0)


def lanes_of(shape):
    return lax.broadcasted_iota(jnp.int32, shape, 1)


def split_three(value):
    high = value.astype(BF16)
    rest = value - high.astype(F32)
    middle = rest.astype(BF16)
    low = (rest - middle.astype(F32)).astype(BF16)
    return high, middle, low


def norm_parts(value):
    centre = jnp.mean(value, axis=-1, keepdims=True)
    centered = value - centre
    spread = jnp.mean(centered * centered, axis=-1, keepdims=True)
    scale = lax.rsqrt(spread + EPS)
    return centered * scale, scale


def norm_back(grad, normal, scale):
    mean_grad = jnp.mean(grad, axis=-1, keepdims=True)
    mean_prod = jnp.mean(grad * normal, axis=-1, keepdims=True)
    return scale * (grad - mean_grad - normal * mean_prod)


def pack_rows(out, value, split, base=0):
    blocks = out.shape[0]
    each = split // blocks
    rest = value.shape[0] - split
    for block in range(blocks):
        out[block, base : base + each] = value[block * each : (block + 1) * each]
        out[block, base + each : base + each + rest] = value[split:]


def column_sum(value):
    return jnp.sum(value, axis=0, keepdims=True)


def attend_kernel(text, mem, w_q, w_k, w_v, lines, lines_all, mark_q, mark_k, w_out,
                  q_out, k_out, v_out, att_out, log_out, resid):
    step = pl.program_id(0)
    x = jnp.concatenate([text[...], mem[...]], axis=0)
    count = x.shape[0]
    query = (dot(x, w_q[...]) + lines[0:1, :]).astype(BF16)
    key = dot(x, w_k[...]).astype(BF16)
    value = (dot(x, w_v[...]) + lines[1:2, :]).astype(BF16)
    q_out[...] = query
    k_out[...] = key
    v_out[...] = value
    scaled = query * jnp.asarray(0.125, BF16)
    lane = lanes_of((count, 128))
    ones = (lane == 0).astype(BF16)
    mq, mk = mark_q[...], mark_k[...]
    logs = jnp.zeros((count, 128), F32)
    scores = []
    for head in range(4):
        span = slice(128 * (head // 2), 128 * (head // 2) + 128)
        mine = jnp.where(lane // 64 == head % 2, scaled[:, span], jnp.asarray(0, BF16))
        key_wide = jnp.concatenate([key[:, span], mk], axis=1)
        scores.append(dot_nt(jnp.concatenate([mine, mq], axis=1), key_wide))
    outs = []
    for head in range(4):
        span = slice(128 * (head // 2), 128 * (head // 2) + 128)
        value_wide = jnp.concatenate([value[:, span], ones], axis=1)
        top = jnp.max(scores[head], axis=-1, keepdims=True)
        raised = jnp.exp(scores[head] - top).astype(BF16)
        summed = dot(raised, value_wide)
        total = summed[:, 128:129]
        outs.append(summed[:, :128] / total)
        logs = jnp.where(lane == 4 * step + head, top + jnp.log(total), logs)
    pairs = [jnp.where(lane < 64, outs[0], outs[1]), jnp.where(lane < 64, outs[2], outs[3])]
    pairs = [pair.astype(BF16) for pair in pairs]
    attended = jnp.concatenate(pairs, axis=1)
    att_out[...] = attended

    @pl.when(step == 0)
    def _():
        log_out[...] = logs
        resid[...] = x.astype(F32) + lines_all[2:3, :]

    @pl.when(step > 0)
    def _():
        log_out[...] += logs

    resid[...] += dot(attended, w_out[...])


def attend(text, mem, w_qkv, lines, mark_q, mark_k, w_out):
    width = text.shape[1]
    count = text.shape[0] + mem.shape[0]
    whole = lambda shape: pl.BlockSpec(shape, lambda j: (0, 0))
    cols = lambda height, base: pl.BlockSpec((height, 256), lambda j: (0, base + j))
    low = jax.ShapeDtypeStruct((count, width), BF16)
    return pl.pallas_call(
        attend_kernel,
        grid=(3,),
        in_specs=[
            whole(text.shape),
            whole(mem.shape),
            cols(width, 0),
            cols(width, 3),
            cols(width, 6),
            cols(16, 0),
            whole((16, width)),
            whole((count, 128)),
            whole((count, 128)),
            pl.BlockSpec((256, width), lambda j: (j, 0)),
        ],
        out_specs=[
            cols(count, 0),
            cols(count, 0),
            cols(count, 0),
            cols(count, 0),
            whole((count, 128)),
            whole((count, width)),
        ],
        out_shape=[
            low,
            low,
            low,
            low,
            jax.ShapeDtypeStruct((count, 128), F32),
            jax.ShapeDtypeStruct((count, width), F32),
        ],
        compiler_params=pltpu.CompilerParams(vmem_limit_bytes=VMEM_ASK),
        cost_estimate=cost(15),
        name="attend",
    )(text, mem, w_qkv, w_qkv, w_qkv, lines, lines, mark_q, mark_k, w_out)


def feed_kernel(resid, lines, w_in, w_down, cot_text, cot_mem,
                result_out, g_two, inner_out, sums_out, sums_in_out, grad_down_out, grad_in_out,
                hidden_low, hidden_turned, g_low, act_all, slope_all):
    step = pl.program_id(0)
    half = pl.num_programs(0) // 2
    width = resid.shape[1]
    cuts = w_in.shape[1] // width

    @pl.when(step == 0)
    def _():
        normal, _ = norm_parts(resid[...])
        hidden = normal * lines[3:4, :] + lines[4:5, :]
        hidden_low[...] = hidden.astype(BF16)
        hidden_turned[...] = hidden.astype(BF16).T
        g_two[...] = hidden + lines[5:6, :]

    @pl.when(step < half)
    def _():
        spans = [slice(cut * width, (cut + 1) * width) for cut in range(cuts)]
        inners = [
            dot(hidden_low[...], w_in[:, spans[cut]]) + lines[pl.ds(8 + step * cuts + cut, 1), :]
            for cut in range(cuts)
        ]
        total = g_two[...]
        for cut, inner in enumerate(inners):
            part = step * cuts + cut
            phi = 0.5 * (1.0 + lax.erf(inner * (0.5**0.5)))
            act = (inner * phi).astype(BF16)
            act_all[part] = act
            slope = phi + inner * jnp.exp(-0.5 * inner * inner) * 0.3989422804014327
            slope_all[part] = slope.astype(BF16)
            total += dot(act, w_down[spans[cut], :])
        g_two[...] = total

    @pl.when(step == half - 1)
    def _():
        normal, scale = norm_parts(g_two[...])
        result = normal * lines[6:7, :] + lines[7:8, :]
        pack_rows(result_out, result.astype(BF16), cot_text.shape[0])
        grad = jnp.concatenate([cot_text[...], cot_mem[...]], axis=0).astype(F32)
        sums_out[0:1, :] = column_sum(grad * normal)
        sums_out[1:2, :] = column_sum(grad)
        grad = norm_back(grad * lines[6:7, :], normal, scale)
        sums_out[2:3, :] = column_sum(grad)
        g_two[...] = grad
        g_low[...] = grad.astype(BF16)

    @pl.when(step >= half)
    def _():
        spans = [slice(cut * width, (cut + 1) * width) for cut in range(cuts)]
        g_acts = [dot_nt(g_low[...], w_down[span, :]) for span in spans]
        for cut, span in enumerate(spans):
            part = (step - half) * cuts + cut
            grad_down_out[span, :] = dot_tn(act_all[part], g_low[...]).astype(BF16)
            g_inner = g_acts[cut] * slope_all[part].astype(F32)
            sums_in_out[0:1, span] = column_sum(g_inner)
            g_inner_low = g_inner.astype(BF16)
            inner_out[:, span] = g_inner_low
            grad_in_out[cut] = dot(hidden_turned[...], g_inner_low).astype(BF16)


def feed(resid, lines, w_in, w_down, cot_text, cot_mem, packed):
    count, width = resid.shape
    wide = w_in.shape[1]
    parts, cuts = wide // width, 2
    half = parts // cuts
    chunk = cuts * width
    whole = lambda shape: pl.BlockSpec(shape, lambda j: (0,) * len(shape))
    late = lambda j: jnp.maximum(j - half, 0)
    full = whole((count, width))
    high = jax.ShapeDtypeStruct((count, width), F32)
    return pl.pallas_call(
        feed_kernel,
        grid=(2 * half,),
        in_specs=[
            full,
            whole(lines.shape),
            pl.BlockSpec((width, chunk), lambda j: (0, jnp.minimum(j, half - 1))),
            pl.BlockSpec((chunk, width), lambda j: (j % half, 0)),
            whole(cot_text.shape),
            whole(cot_mem.shape),
        ],
        out_specs=[
            whole(packed),
            full,
            pl.BlockSpec((count, chunk), lambda j: (0, late(j))),
            whole((8, width)),
            pl.BlockSpec((8, chunk), lambda j: (0, late(j))),
            pl.BlockSpec((chunk, width), lambda j: (late(j), 0)),
            pl.BlockSpec((cuts, width, width), lambda j: (late(j), 0, 0)),
        ],
        out_shape=[
            jax.ShapeDtypeStruct(packed, BF16),
            high,
            jax.ShapeDtypeStruct((count, wide), BF16),
            jax.ShapeDtypeStruct((8, width), F32),
            jax.ShapeDtypeStruct((8, wide), F32),
            jax.ShapeDtypeStruct((wide, width), BF16),
            jax.ShapeDtypeStruct((parts, width, width), BF16),
        ],
        scratch_shapes=[
            pltpu.VMEM((count, width), BF16),
            pltpu.VMEM((width, count), BF16),
            pltpu.VMEM((count, width), BF16),
            pltpu.VMEM((parts, count, width), BF16),
            pltpu.VMEM((parts, count, width), BF16),
        ],
        compiler_params=pltpu.CompilerParams(vmem_limit_bytes=VMEM_ASK),
        cost_estimate=cost(28),
        name="feed",
    )(resid, lines, w_in, w_down, cot_text, cot_mem)


def backward_kernel(g_two, g_inner, w_in, resid, lines, text, mem, q, k, v, att, logs, mark_q, mark_k,
                    w_out, w_q, w_k, w_v, sums_two, sums_in, scalars, result,
                    mine_out, theirs_out, packed_out, g_rows, g_low, rows_turned, sums,
                    grads, sems):
    step = pl.program_id(0)
    parts = pl.num_programs(0) - 3

    @pl.when(step == 0)
    def _():
        x = jnp.concatenate([text[...], mem[...]], axis=0)
        rows_turned[...] = x.T
        g_rows[...] = g_two[...]
        packed_out[:, : result.shape[1]] = result[...]

    @pl.when(step < parts)
    def _():
        g_rows[...] += dot_nt(g_inner[...], w_in[...])

    @pl.when(step == parts - 1)
    def _():
        normal, scale = norm_parts(resid[...])
        g_hidden = g_rows[...]
        first = sums.shape[0] - 12
        sums[first + 2 : first + 3, :] = column_sum(g_hidden * normal)
        sums[first + 3 : first + 4, :] = column_sum(g_hidden)
        grad = norm_back(g_hidden * lines[3:4, :], normal, scale)
        sums[first + 4 : first + 5, :] = column_sum(grad)
        g_rows[...] = grad
        g_low[...] = grad.astype(BF16)

    @pl.when(step >= parts)
    def _():
        attend_back_step(step - parts, text, mem, q, k, v, att, logs, mark_q, mark_k, g_low, w_out,
                         w_q, w_k, w_v, sums_two, sums_in, scalars,
                         mine_out, theirs_out, packed_out, g_rows, rows_turned, sums,
                         grads, sems)


def attend_back_step(step, text, mem, q, k, v, att, logs, mark_q, mark_k, g_low, w_out,
                     w_q, w_k, w_v, sums_two, sums_in, scalars,
                     mine_out, theirs_out, packed_out, g_rows, rows_turned, sums,
                         grads, sems):
    core = scalars[0, 1]
    split = text.shape[0]
    count = split + mem.shape[0]
    width = text.shape[1]
    query, key, value, attended = q[...], k[...], v[...], att[...]

    def put(half, start, part):
        rows = pl.ds(pl.multiple_of(start, 16), part.shape[0])
        grads[jnp.where(core == half, 0, 1), rows, :] = part

    blocks = width // 128
    group_rows = grads.shape[1] // 2
    piece_rows = group_rows // 2

    def start_of(group, block):
        piece = block // (blocks // 2)
        return group * group_rows + piece * piece_rows + block % (blocks // 2) * width

    grad_w_out = dot_tn(attended, g_low[...]).astype(BF16)
    for block in range(blocks):
        part = grad_w_out[:, 128 * block : 128 * block + 128]
        put(1, start_of(1, block) + 256 * step, part)
    g_att = dot_nt(g_low[...], w_out[...])
    g_att_low = g_att.astype(BF16)
    scaled = query * jnp.asarray(0.125, BF16)
    product = g_att_low.astype(F32) * attended.astype(F32)
    lane = lanes_of((count, 128))
    none = jnp.asarray(0, BF16)
    thirds = ((lane >= 4) & (lane < 7)).astype(BF16)
    mq, mk = mark_q[...], mark_k[...] + thirds
    log_all = logs[...]

    def extra(column, base):
        high, middle, low = split_three(-column)
        wide = jnp.where(lane == 4, high, jnp.where(lane == 5, middle, low))
        return jnp.where((lane >= 4) & (lane < 7), wide, base)

    g_querys, g_keys, g_values = [], [], []
    for pair in range(2):
        span = slice(128 * pair, 128 * pair + 128)
        key_pair = key[:, span]
        key_wide = jnp.concatenate([key_pair, mk], axis=1)
        value_wide = jnp.concatenate([value[:, span], thirds], axis=1)
        key_turned = key_pair.astype(F32).T
        turned = lax.broadcasted_iota(jnp.int32, key_turned.shape, 0)
        g_query = g_key = g_value = None
        for side in range(2):
            own = lane // 64 == side
            mine = jnp.where(own, scaled[:, span], none)
            head = 4 * step + 2 * pair + side
            log_own = jnp.sum(jnp.where(lane == head, log_all, 0.0), axis=1, keepdims=True)
            query_wide = jnp.concatenate([mine, extra(log_own, mq)], axis=1)
            probs = jnp.exp(dot_nt(key_wide, query_wide))
            g_mine = jnp.where(own, g_att_low[:, span], none)
            delta = jnp.sum(jnp.where(own, product[:, span], 0.0), axis=1, keepdims=True)
            g_wide = jnp.concatenate([g_mine, extra(delta, jnp.zeros_like(mq))], axis=1)
            g_scores = (probs * dot_nt(value_wide, g_wide)).astype(BF16)
            part_v = dot(probs.astype(BF16), g_mine)
            part_k = dot(g_scores, mine)
            turned_own = jnp.where(turned // 64 == side, key_turned, 0.0).astype(BF16)
            part_q = dot(turned_own, g_scores)
            if side == 0:
                g_query, g_key, g_value = part_q, part_k, part_v
            else:
                g_query, g_key, g_value = g_query + part_q, g_key + part_k, g_value + part_v
        g_querys.append(g_query.T * 0.125)
        g_keys.append(g_key)
        g_values.append(g_value)
    g_query = jnp.concatenate(g_querys, axis=1)
    g_key = jnp.concatenate(g_keys, axis=1)
    g_value = jnp.concatenate(g_values, axis=1)
    columns = pl.ds(pl.multiple_of(256 * step, 256), 256)
    first = sums.shape[0] - 12
    sums[first : first + 1, columns] = column_sum(g_query)
    sums[first + 1 : first + 2, columns] = column_sum(g_value)
    total = g_rows[...]
    for place, (grad, weight) in enumerate(((g_query, w_q), (g_key, w_k), (g_value, w_v))):
        low = grad.astype(BF16)
        grad_w = dot(rows_turned[...], low).astype(BF16)
        for block in range(2):
            part = grad_w[:, 128 * block : 128 * block + 128]
            put(place // 2, start_of(place % 2, 2 * step + block), part)
        total += dot_nt(low, weight[...])
    g_rows[...] = total

    @pl.when(step == 2)
    def _():
        reset = scalars[0, 0] == 1
        g_mem = total[split:]
        zero = jnp.zeros_like(g_mem)
        g_kept = jnp.where(reset, zero, g_mem)
        g_all = jnp.concatenate([total[:split], g_kept], axis=0).astype(BF16)
        pack_rows(packed_out, g_all, split, packed_out.shape[1] // 2)
        first = sums.shape[0] - 12
        sums[first + 5 : first + 8, :] = sums_two[0:3, :]
        for place in range(4):
            sums[first + 8 + place : first + 9 + place, :] = sums_in[0:1, place * width : (place + 1) * width]
        mem_count = sums.shape[0] - 12
        sums[0:mem_count, :] = jnp.where(reset, g_mem, zero)[0:mem_count]
        small = sums[...].astype(BF16)
        base = blocks // 2 * width
        empty = jnp.zeros((SPARE_ROWS, 128), BF16)
        for place in range(4):
            rows = slice(place * piece_rows + base, (place + 1) * piece_rows)
            grads[0, rows, :] = empty
            grads[1, rows, :] = empty
        for place in range(2):
            for block in range(blocks):
                start = place * piece_rows + base + block * small.shape[0]
                put(0, start, small[:, 128 * block : 128 * block + 128])
        theirs = pltpu.make_async_copy(grads.at[1], theirs_out, sems.at[1])
        mine = pltpu.make_async_copy(grads.at[0], mine_out, sems.at[0])
        theirs.start()
        mine.start()
        theirs.wait()
        mine.wait()


def backward(g_two, g_inner, w_in, resid, lines, text, mem, q, k, v, att, logs, mark_q, mark_k,
             w_out, w_qkv, sums_two, sums_in, scalars, result):
    width = text.shape[1]
    count = text.shape[0] + mem.shape[0]
    chunk = 2 * width
    parts = w_in.shape[1] // chunk
    whole = lambda shape: pl.BlockSpec(shape, lambda j: (0,) * len(shape))
    early = lambda height: pl.BlockSpec((height, chunk), lambda j: (0, jnp.minimum(j, parts - 1)))
    quad = lambda j: jnp.maximum(j - parts, 0)
    cols = lambda height, base: pl.BlockSpec((height, 256), lambda j: (0, base + quad(j)))
    full = whole((count, width))
    mark = whole((count, 128))
    height = 2 * (width // 128 * width + 2 * SPARE_ROWS)
    half = jax.ShapeDtypeStruct((height, 128), BF16)
    packed = (result.shape[0], 2 * result.shape[1], width)
    return pl.pallas_call(
        backward_kernel,
        grid=(parts + 3,),
        in_specs=[
            full,
            early(count),
            early(width),
            full,
            whole(lines.shape),
            whole(text.shape),
            whole(mem.shape),
            cols(count, 0),
            cols(count, 0),
            cols(count, 0),
            cols(count, 0),
            mark,
            mark,
            mark,
            pl.BlockSpec((256, width), lambda j: (quad(j), 0)),
            cols(width, 0),
            cols(width, 3),
            cols(width, 6),
            whole(sums_two.shape),
            whole(sums_in.shape),
            pl.BlockSpec(memory_space=pltpu.SMEM),
            whole(result.shape),
        ],
        out_specs=[pl.BlockSpec(memory_space=pl.ANY)] * 2 + [whole(packed)],
        out_shape=[half, half, jax.ShapeDtypeStruct(packed, BF16)],
        scratch_shapes=[
            pltpu.VMEM((count, width), F32),
            pltpu.VMEM((count, width), BF16),
            pltpu.VMEM((width, count), BF16),
            pltpu.VMEM((count - text.shape[0] - ROW_PAD + 12, width), F32),
            pltpu.VMEM((2, height, 128), BF16),
            pltpu.SemaphoreType.DMA((2,)),
        ],
        compiler_params=pltpu.CompilerParams(vmem_limit_bytes=VMEM_ASK),
        cost_estimate=cost(33),
        name="backward",
    )(g_two, g_inner, w_in, resid, lines, text, mem, q, k, v, att, logs, mark_q, mark_k,
      w_out, w_qkv, w_qkv, w_qkv, sums_two, sums_in, scalars, result)


def widen_kernel(*refs):
    pieces, codes = refs[:4], refs[4]
    early = len(refs) == 10
    if early:
        qkv_out, out_out, small_out, wide, sems = refs[5:]
    else:
        qkv_out, out_out, wide, sems = refs[-4:]
    width = wide.shape[1]
    part = wide.shape[2]
    blocks = part // 128

    def copies(place):
        code = codes[0, place]
        in_qkv = code < 6
        spot = jnp.where(in_qkv, code, code - 6)
        columns = pl.ds(pl.multiple_of(spot * part, part), part)
        to_qkv = pltpu.make_async_copy(wide.at[place], qkv_out.at[:, columns], sems.at[place])
        to_out = pltpu.make_async_copy(wide.at[place], out_out.at[:, columns], sems.at[place])
        return in_qkv, to_qkv, to_out

    for place, piece in enumerate(pieces):
        for block in range(blocks):
            rows = slice(block * width, (block + 1) * width)
            wide[place, :, 128 * block : 128 * block + 128] = piece[rows, :].astype(F32)
        in_qkv, to_qkv, to_out = copies(place)

        if early:

            @pl.when(codes[0, place] < 2)
            def _():
                height = small_out.shape[0]
                for block in range(2 * blocks):
                    start = blocks * width + block * height
                    rows = piece[start : start + height, :].astype(F32)
                    small_out[:, 128 * block : 128 * block + 128] = rows

        @pl.when(in_qkv)
        def _():
            to_qkv.start()

        @pl.when(jnp.logical_not(in_qkv))
        def _():
            to_out.start()

    for place in range(4):
        in_qkv, to_qkv, to_out = copies(place)

        @pl.when(in_qkv)
        def _():
            to_qkv.wait()

        @pl.when(jnp.logical_not(in_qkv))
        def _():
            to_out.wait()


def widen(pieces, codes, width, small_count, partly=()):
    vmem = pl.BlockSpec(memory_space=pltpu.VMEM)
    hbm = pl.BlockSpec(memory_space=pl.ANY)
    return pl.pallas_call(
        widen_kernel,
        in_specs=[vmem] * 4 + [pl.BlockSpec(memory_space=pltpu.SMEM)] + [hbm] * len(partly),
        out_specs=[hbm, hbm] + ([] if partly else [vmem]),
        out_shape=[
            jax.ShapeDtypeStruct((width, 3 * width), F32),
            jax.ShapeDtypeStruct((width, width), F32),
        ]
        + ([] if partly else [jax.ShapeDtypeStruct((small_count, width), F32)]),
        scratch_shapes=[pltpu.VMEM((4, width, width // 2), F32), pltpu.SemaphoreType.DMA((4,))],
        input_output_aliases={5: 0, 6: 1} if partly else {},
        compiler_params=pltpu.CompilerParams(vmem_limit_bytes=VMEM_ASK),
        cost_estimate=cost(4),
        name="widen",
    )(*pieces, codes, *partly)


def widen_feed_kernel(down, inward, down_out, in_out, low, high, in_sems, out_sems):
    count, width = inward.shape[0], inward.shape[2]
    low_rows = low.shape[1]
    cut = width // low_rows
    places = []
    for part in range(count):
        for piece in range(cut):
            rows = pl.ds(piece * low_rows, low_rows)
            tall = pl.ds(part * width + piece * low_rows, low_rows)
            columns = pl.ds(part * width, width)
            places.append((inward.at[part, rows], in_out.at[rows, columns]))
            places.append((down.at[tall], down_out.at[tall]))
    fetches, sends = [], []
    for place, (source, target) in enumerate(places):
        fetches.append(pltpu.make_async_copy(source, low.at[place], in_sems.at[place]))
        sends.append(pltpu.make_async_copy(high.at[place], target, out_sems.at[place]))
        fetches[-1].start()
    for place in range(len(places)):
        fetches[place].wait()
        high[place] = low[place].astype(F32)
        sends[place].start()
    for send in sends:
        send.wait()


def widen_feed(down, inward):
    count, height, width = inward.shape
    cut = 2
    blocks = 2 * count * cut
    hbm = pl.BlockSpec(memory_space=pl.ANY)
    return pl.pallas_call(
        widen_feed_kernel,
        in_specs=[hbm, hbm],
        out_specs=[hbm, hbm],
        out_shape=[
            jax.ShapeDtypeStruct(down.shape, F32),
            jax.ShapeDtypeStruct((height, count * width), F32),
        ],
        scratch_shapes=[
            pltpu.VMEM((blocks, height // cut, width), BF16),
            pltpu.VMEM((blocks, height // cut, width), F32),
            pltpu.SemaphoreType.DMA((blocks,)),
            pltpu.SemaphoreType.DMA((blocks,)),
        ],
        compiler_params=pltpu.CompilerParams(vmem_limit_bytes=VMEM_ASK),
        cost_estimate=cost(9),
        name="widen_feed",
    )(down, inward)


def ring_partner(place, way):
    return place ^ 1 if way == 0 else 3 - place


def ring_pairs(step):
    pairs = []
    for place in range(4):
        for core in range(2):
            other = ring_partner(place, (step + core) % 2)
            pairs.append((2 * place + core, 2 * other + core))
    return pairs


def side_of(place, core, step):
    return jnp.where((step + core) % 2 == 0, (place + 1) // 2 % 2, place // 2)


def ring_side(axis, step):
    return side_of(lax.axis_index(axis), lax.axis_index("core"), step)


def ring_swap(value, axis, step):
    return lax.ppermute(value, (axis, "core"), ring_pairs(step))


def core_swap(value):
    return lax.ppermute(value, "core", [(0, 1), (1, 0)])


def add_pair(pair):
    return (pair[0].astype(F32) + pair[1].astype(F32)).astype(BF16)


def half_of(pair, side, start=0, rows=None):
    rows = pair[0].shape[-2] if rows is None else rows
    axis = pair[0].ndim - 2
    place = start + side * (rows // 2)
    return add_pair([lax.dynamic_slice_in_dim(part, place, rows // 2, axis) for part in pair])


def ring_halve(pair, axis, step, start=0, rows=None):
    side = ring_side(axis, step)
    got = ring_swap(half_of(pair, 1 - side, start, rows), axis, step)
    return half_of(pair, side, start, rows), got


def ring_join(value, axis, step):
    got = ring_swap(value, axis, step)
    return jnp.where(
        ring_side(axis, step) == 0,
        jnp.concatenate([value, got], axis=-2),
        jnp.concatenate([got, value], axis=-2),
    )


def to_segments(value):
    return lax.all_to_all(value, BLK, 0, 1, tiled=True)[0]


def after(value, other):
    return lax.optimization_barrier((value, other))[0]


def doc_marks(docs, mem_count):
    kinds = (docs[:, None] == jnp.arange(3)[None]).astype(F32)
    rest = mem_count + ROW_PAD
    total = docs.shape[0] + rest
    spare = (jnp.arange(total) >= total - ROW_PAD).astype(F32)[:, None]
    query = jnp.concatenate([jnp.pad(kinds, ((0, rest), (0, 0))), jnp.ones((total, 1), F32)], 1)
    key = jnp.concatenate([jnp.pad(kinds - 1.0, ((0, rest), (0, 0))), -spare], 1) * BAN
    fill = ((0, 0), (0, 128 - query.shape[1]))
    return jnp.pad(query, fill).astype(BF16), jnp.pad(key, fill).astype(BF16)


def local(
    tokens,
    memory,
    mem_init,
    reset_flags,
    doc_ids,
    w_qkv,
    b_query,
    b_value,
    w_out,
    b_out,
    norm1_gain,
    norm1_bias,
    w_in,
    b_in,
    w_down,
    b_down,
    norm2_gain,
    norm2_bias,
    out_cot,
    mem_cot,
):
    seg_count, tok_count, width = tokens.shape
    mem_count = memory.shape[1]
    place = lax.axis_index(BLK)
    pick = lambda value: lax.dynamic_index_in_dim(value, place, 0, keepdims=False)
    fill = lambda value: jnp.pad(value, ((0, ROW_PAD), (0, 0)))
    packed = (seg_count, tok_count + mem_count + ROW_PAD, width)
    my_flag = pick(reset_flags)
    mark_q, mark_k = doc_marks(pick(doc_ids), mem_count)
    mem = fill(jnp.where(my_flag == 1, mem_init, pick(memory)))
    cot_mem = fill(pick(mem_cot))
    text = to_segments(tokens)
    cot_text = to_segments(after(out_cot, text))

    lines = jnp.concatenate(
        [b_query, b_value, b_out, norm1_gain, norm1_bias, b_down, norm2_gain, norm2_bias, b_in]
    )
    lines = jnp.pad(lines.astype(F32).reshape(-1, width), ((0, 4), (0, 0)))
    q, k, v, att, logs, resid = attend(text, mem, w_qkv, lines, mark_q, mark_k, w_out)
    result, g_two, g_inner, sums_two, sums_in, grad_down, grad_in = feed(
        resid, lines, w_in, w_down, cot_text, cot_mem, packed
    )
    grad_down, grad_in = lax.psum((grad_down, grad_in), ALL)
    scalars = jnp.stack([my_flag, lax.axis_index("core")]).reshape(1, 2).astype(jnp.int32)
    small_count = mem_count + 12

    def attention_back(operands):
        result, g_two, g_inner, sums_two, sums_in = operands
        mine, theirs, g_packed = backward(
            g_two,
            g_inner,
            w_in,
            resid,
            lines,
            text,
            mem,
            q,
            k,
            v,
            att,
            logs,
            mark_q,
            mark_k,
            w_out,
            w_qkv,
            sums_two,
            sums_in,
            scalars,
            result,
        )
        pair = (mine, core_swap(theirs))
        rows = mine.shape[0] // 2
        over_z = ring_halve(pair, "z", 0, 0, rows)
        over_x = ring_halve(pair, "x", 0, rows, rows)
        over_z = ring_halve(over_z, "z", 1)
        over_x = ring_halve(over_x, "x", 1)
        both = lax.all_to_all(after(g_packed, over_z[0]), BLK, 0, 0, tiled=True)
        side = ring_side("y", 0)
        got = ring_swap(jnp.stack([half_of(over_z, 1 - side), half_of(over_x, 1 - side)]), "y", 0)
        pair = (jnp.stack([half_of(over_z, side), half_of(over_x, side)]), got)
        pair = ring_halve(pair, "y", 1)
        over_z, over_x = add_pair([part[0] for part in pair]), add_pair([part[1] for part in pair])
        for step in (0, 1):
            got_z, got_x = ring_swap(over_z, "x", step), ring_swap(over_x, "z", step)
            over_z, over_x = add_pair((over_z, got_z)), add_pair((over_x, got_x))
        joined = after(jnp.stack([over_z, over_x]), both)
        for step in (1, 0):
            joined = ring_join(joined, "y", step)
        over_z = ring_join(joined[0], "z", 1)
        over_x = ring_join(joined[1], "x", 1)
        pieces = []
        for base in (0, result.shape[1]):
            pieces.append(both[:, base : base + tok_count])
            pieces.append(both[:, base + tok_count : base + tok_count + mem_count])
        over_z, over_x = after((over_z, over_x), tuple(pieces))
        far = [ring_swap(over_z, "z", 0), ring_swap(over_x, "x", 0)]
        near = [core_swap(over_z), core_swap(over_x)]
        core = lax.axis_index("core")
        codes = []
        for where in (core, 1 - core):
            for group, axis in enumerate(("z", "x")):
                codes.append(4 * where + 2 * group + side_of(lax.axis_index(axis), where, 0))
        codes = jnp.stack(codes).astype(jnp.int32).reshape(1, 4)
        *wide, small = widen([over_z, over_x, *near], codes, width, small_count)
        start = mem_count
        vectors = [small[start + row] for row in range(8)]
        bin_rows = w_in.shape[1] // width
        vectors.append(small[start + 8 : start + 8 + bin_rows].reshape(-1))
        vectors.append(small[:mem_count])
        far, wide, vectors = lax.optimization_barrier((far, wide, vectors))
        far = [*far, core_swap(far[0]), core_swap(far[1])]
        wide = widen(far, codes ^ 1, width, small_count, wide)
        return *wide, *vectors, *pieces

    def nothing(operands):
        text_zero = jnp.zeros(tokens.shape, BF16)
        mem_zero = jnp.zeros(memory.shape, BF16)
        line = jnp.zeros((width,), F32)
        return (
            jnp.zeros(w_qkv.shape, F32),
            jnp.zeros(w_out.shape, F32),
            *[line] * 8,
            jnp.zeros(b_in.shape, F32),
            jnp.zeros(mem_init.shape, F32),
            text_zero,
            mem_zero,
            text_zero,
            mem_zero,
        )

    (
        grad_wqkv,
        grad_wout,
        grad_bquery,
        grad_bvalue,
        grad_gain1,
        grad_bias1,
        grad_bout,
        grad_gain2,
        grad_bias2,
        grad_bdown,
        grad_bin,
        grad_init,
        output,
        mem_output,
        grad_tokens,
        grad_memory,
    ) = lax.cond(
        reset_flags[0] >= 0, attention_back, nothing, (result, g_two, g_inner, sums_two, sums_in)
    )
    grad_down, grad_in = widen_feed(grad_down, grad_in)
    return (
        output,
        mem_output,
        grad_tokens,
        grad_memory,
        grad_init,
        grad_wqkv,
        grad_bquery,
        grad_bvalue,
        grad_wout,
        grad_bout,
        grad_gain1,
        grad_bias1,
        grad_in,
        grad_bin,
        grad_down,
        grad_bdown,
        grad_gain2,
        grad_bias2,
    )


def solution(mesh):
    chips = Mesh(mesh.devices.reshape(4, 4, 4, 2), ALL)
    placed = (
        P(SEG, BLK, None),
        P(SEG, None, None),
        P(),
        P(SEG),
        P(SEG, None),
        *([P()] * 13),
        P(SEG, BLK, None),
        P(SEG, None, None),
    )
    return jax.shard_map(
        local,
        mesh=chips,
        in_specs=placed,
        out_specs=(
            P(SEG, BLK, None),
            P(SEG, None, None),
            P(SEG, BLK, None),
            P(SEG, None, None),
            *([P()] * 14),
        ),
        check_vma=False,
    )
```

```python
import jax
import jax.numpy as jnp
from jax import lax
from jax.experimental import pallas as pl
from jax.experimental.pallas import tpu as pltpu
from jax.sharding import Mesh, PartitionSpec as P

F32 = jnp.float32
BF16 = jnp.bfloat16
HEADS = 12
EPS = 1e-12
BAN = 2.0**30
VMEM_ASK = 60 * 1024 * 1024
BLK = ("z", "core")
SEG = ("y", "x")
ALL = ("y", "x", "z", "core")
XYZ = ("x", "y", "z")
CHIPS = 64
ROW_PAD = 12
SPARE_ROWS = 256


def dot(left, right):
    return jnp.dot(left, right, preferred_element_type=F32)


def dot_nt(left, right):
    return lax.dot_general(left, right, (((1,), (1,)), ((), ())), preferred_element_type=F32)


def dot_tn(left, right):
    return lax.dot_general(left, right, (((0,), (0,)), ((), ())), preferred_element_type=F32)


def cost(micros):
    return pl.CostEstimate(flops=int(micros * 1e9), bytes_accessed=0, transcendentals=0)


def lanes_of(shape):
    return lax.broadcasted_iota(jnp.int32, shape, 1)


def split_three(value):
    high = value.astype(BF16)
    rest = value - high.astype(F32)
    middle = rest.astype(BF16)
    low = (rest - middle.astype(F32)).astype(BF16)
    return high, middle, low


def norm_parts(value):
    centre = jnp.mean(value, axis=-1, keepdims=True)
    centered = value - centre
    spread = jnp.mean(centered * centered, axis=-1, keepdims=True)
    scale = lax.rsqrt(spread + EPS)
    return centered * scale, scale


def norm_back(grad, normal, scale):
    mean_grad = jnp.mean(grad, axis=-1, keepdims=True)
    mean_prod = jnp.mean(grad * normal, axis=-1, keepdims=True)
    return scale * (grad - mean_grad - normal * mean_prod)


def pack_rows(out, value, split, base=0):
    blocks = out.shape[0]
    each = split // blocks
    rest = value.shape[0] - split
    for block in range(blocks):
        out[block, base : base + each] = value[block * each : (block + 1) * each]
        out[block, base + each : base + each + rest] = value[split:]


def column_sum(value):
    return jnp.sum(value, axis=0, keepdims=True)


def attend_kernel(text, mem, w_q, w_k, w_v, lines, lines_all, mark_q, mark_k, w_out,
                  q_out, k_out, v_out, att_out, log_out, resid):
    step = pl.program_id(0)
    x = jnp.concatenate([text[...], mem[...]], axis=0)
    count = x.shape[0]
    query = (dot(x, w_q[...]) + lines[0:1, :]).astype(BF16)
    key = dot(x, w_k[...]).astype(BF16)
    value = (dot(x, w_v[...]) + lines[1:2, :]).astype(BF16)
    q_out[...] = query
    k_out[...] = key
    v_out[...] = value
    scaled = query * jnp.asarray(0.125, BF16)
    lane = lanes_of((count, 128))
    ones = (lane == 0).astype(BF16)
    mq, mk = mark_q[...], mark_k[...]
    logs = jnp.zeros((count, 128), F32)
    scores = []
    for head in range(4):
        span = slice(128 * (head // 2), 128 * (head // 2) + 128)
        mine = jnp.where(lane // 64 == head % 2, scaled[:, span], jnp.asarray(0, BF16))
        key_wide = jnp.concatenate([key[:, span], mk], axis=1)
        scores.append(dot_nt(jnp.concatenate([mine, mq], axis=1), key_wide))
    outs = []
    for head in range(4):
        span = slice(128 * (head // 2), 128 * (head // 2) + 128)
        value_wide = jnp.concatenate([value[:, span], ones], axis=1)
        top = jnp.max(scores[head], axis=-1, keepdims=True)
        raised = jnp.exp(scores[head] - top).astype(BF16)
        summed = dot(raised, value_wide)
        total = summed[:, 128:129]
        outs.append(summed[:, :128] / total)
        logs = jnp.where(lane == 4 * step + head, top + jnp.log(total), logs)
    pairs = [jnp.where(lane < 64, outs[0], outs[1]), jnp.where(lane < 64, outs[2], outs[3])]
    pairs = [pair.astype(BF16) for pair in pairs]
    attended = jnp.concatenate(pairs, axis=1)
    att_out[...] = attended

    @pl.when(step == 0)
    def _():
        log_out[...] = logs
        resid[...] = x.astype(F32) + lines_all[2:3, :]

    @pl.when(step > 0)
    def _():
        log_out[...] += logs

    resid[...] += dot(attended, w_out[...])


def attend(text, mem, w_qkv, lines, mark_q, mark_k, w_out):
    width = text.shape[1]
    count = text.shape[0] + mem.shape[0]
    whole = lambda shape: pl.BlockSpec(shape, lambda j: (0, 0))
    cols = lambda height, base: pl.BlockSpec((height, 256), lambda j: (0, base + j))
    low = jax.ShapeDtypeStruct((count, width), BF16)
    return pl.pallas_call(
        attend_kernel,
        grid=(3,),
        in_specs=[
            whole(text.shape),
            whole(mem.shape),
            cols(width, 0),
            cols(width, 3),
            cols(width, 6),
            cols(16, 0),
            whole((16, width)),
            whole((count, 128)),
            whole((count, 128)),
            pl.BlockSpec((256, width), lambda j: (j, 0)),
        ],
        out_specs=[
            cols(count, 0),
            cols(count, 0),
            cols(count, 0),
            cols(count, 0),
            whole((count, 128)),
            whole((count, width)),
        ],
        out_shape=[
            low,
            low,
            low,
            low,
            jax.ShapeDtypeStruct((count, 128), F32),
            jax.ShapeDtypeStruct((count, width), F32),
        ],
        compiler_params=pltpu.CompilerParams(vmem_limit_bytes=VMEM_ASK),
        cost_estimate=cost(15),
        name="attend",
    )(text, mem, w_qkv, w_qkv, w_qkv, lines, lines, mark_q, mark_k, w_out)


def feed_kernel(resid, lines, w_in, w_down, cot_text, cot_mem,
                result_out, g_two, inner_out, sums_out, sums_in_out, grad_down_out, grad_in_out,
                hidden_low, hidden_turned, g_low, act_all, slope_all):
    step = pl.program_id(0)
    half = pl.num_programs(0) // 2
    width = resid.shape[1]
    cuts = w_in.shape[1] // width

    @pl.when(step == 0)
    def _():
        normal, _ = norm_parts(resid[...])
        hidden = normal * lines[3:4, :] + lines[4:5, :]
        hidden_low[...] = hidden.astype(BF16)
        hidden_turned[...] = hidden.astype(BF16).T
        g_two[...] = hidden + lines[5:6, :]

    @pl.when(step < half)
    def _():
        spans = [slice(cut * width, (cut + 1) * width) for cut in range(cuts)]
        inners = [
            dot(hidden_low[...], w_in[:, spans[cut]]) + lines[pl.ds(8 + step * cuts + cut, 1), :]
            for cut in range(cuts)
        ]
        total = g_two[...]
        for cut, inner in enumerate(inners):
            part = step * cuts + cut
            phi = 0.5 * (1.0 + lax.erf(inner * (0.5**0.5)))
            act = (inner * phi).astype(BF16)
            act_all[part] = act
            slope = phi + inner * jnp.exp(-0.5 * inner * inner) * 0.3989422804014327
            slope_all[part] = slope.astype(BF16)
            total += dot(act, w_down[spans[cut], :])
        g_two[...] = total

    @pl.when(step == half - 1)
    def _():
        normal, scale = norm_parts(g_two[...])
        result = normal * lines[6:7, :] + lines[7:8, :]
        pack_rows(result_out, result.astype(BF16), cot_text.shape[0])
        grad = jnp.concatenate([cot_text[...], cot_mem[...]], axis=0).astype(F32)
        sums_out[0:1, :] = column_sum(grad * normal)
        sums_out[1:2, :] = column_sum(grad)
        grad = norm_back(grad * lines[6:7, :], normal, scale)
        sums_out[2:3, :] = column_sum(grad)
        g_two[...] = grad
        g_low[...] = grad.astype(BF16)

    @pl.when(step >= half)
    def _():
        spans = [slice(cut * width, (cut + 1) * width) for cut in range(cuts)]
        g_acts = [dot_nt(g_low[...], w_down[span, :]) for span in spans]
        for cut, span in enumerate(spans):
            part = (step - half) * cuts + cut
            grad_down_out[span, :] = dot_tn(act_all[part], g_low[...]).astype(BF16)
            g_inner = g_acts[cut] * slope_all[part].astype(F32)
            sums_in_out[0:1, span] = column_sum(g_inner)
            g_inner_low = g_inner.astype(BF16)
            inner_out[:, span] = g_inner_low
            grad_in_out[cut] = dot(hidden_turned[...], g_inner_low).astype(BF16)


def feed(resid, lines, w_in, w_down, cot_text, cot_mem, packed):
    count, width = resid.shape
    wide = w_in.shape[1]
    parts, cuts = wide // width, 2
    half = parts // cuts
    chunk = cuts * width
    whole = lambda shape: pl.BlockSpec(shape, lambda j: (0,) * len(shape))
    late = lambda j: jnp.maximum(j - half, 0)
    full = whole((count, width))
    high = jax.ShapeDtypeStruct((count, width), F32)
    return pl.pallas_call(
        feed_kernel,
        grid=(2 * half,),
        in_specs=[
            full,
            whole(lines.shape),
            pl.BlockSpec((width, chunk), lambda j: (0, jnp.minimum(j, half - 1))),
            pl.BlockSpec((chunk, width), lambda j: (j % half, 0)),
            whole(cot_text.shape),
            whole(cot_mem.shape),
        ],
        out_specs=[
            whole(packed),
            full,
            pl.BlockSpec((count, chunk), lambda j: (0, late(j))),
            whole((8, width)),
            pl.BlockSpec((8, chunk), lambda j: (0, late(j))),
            pl.BlockSpec((chunk, width), lambda j: (late(j), 0)),
            pl.BlockSpec((cuts, width, width), lambda j: (late(j), 0, 0)),
        ],
        out_shape=[
            jax.ShapeDtypeStruct(packed, BF16),
            high,
            jax.ShapeDtypeStruct((count, wide), BF16),
            jax.ShapeDtypeStruct((8, width), F32),
            jax.ShapeDtypeStruct((8, wide), F32),
            jax.ShapeDtypeStruct((wide, width), BF16),
            jax.ShapeDtypeStruct((parts, width, width), BF16),
        ],
        scratch_shapes=[
            pltpu.VMEM((count, width), BF16),
            pltpu.VMEM((width, count), BF16),
            pltpu.VMEM((count, width), BF16),
            pltpu.VMEM((parts, count, width), BF16),
            pltpu.VMEM((parts, count, width), BF16),
        ],
        compiler_params=pltpu.CompilerParams(vmem_limit_bytes=VMEM_ASK),
        cost_estimate=cost(28),
        name="feed",
    )(resid, lines, w_in, w_down, cot_text, cot_mem)


def backward_kernel(g_two, g_inner, w_in, resid, lines, text, mem, q, k, v, att, logs, mark_q, mark_k,
                    w_out, w_q, w_k, w_v, sums_two, sums_in, scalars, result,
                    mine_out, theirs_out, packed_out, g_rows, g_low, rows_turned, sums,
                    grads, sems):
    step = pl.program_id(0)
    parts = pl.num_programs(0) - 3

    @pl.when(step == 0)
    def _():
        x = jnp.concatenate([text[...], mem[...]], axis=0)
        rows_turned[...] = x.T
        g_rows[...] = g_two[...]
        packed_out[:, : result.shape[1]] = result[...]

    @pl.when(step < parts)
    def _():
        g_rows[...] += dot_nt(g_inner[...], w_in[...])

    @pl.when(step == parts - 1)
    def _():
        normal, scale = norm_parts(resid[...])
        g_hidden = g_rows[...]
        first = sums.shape[0] - 12
        sums[first + 2 : first + 3, :] = column_sum(g_hidden * normal)
        sums[first + 3 : first + 4, :] = column_sum(g_hidden)
        grad = norm_back(g_hidden * lines[3:4, :], normal, scale)
        sums[first + 4 : first + 5, :] = column_sum(grad)
        g_rows[...] = grad
        g_low[...] = grad.astype(BF16)

    @pl.when(step >= parts)
    def _():
        attend_back_step(step - parts, text, mem, q, k, v, att, logs, mark_q, mark_k, g_low, w_out,
                         w_q, w_k, w_v, sums_two, sums_in, scalars,
                         mine_out, theirs_out, packed_out, g_rows, rows_turned, sums,
                         grads, sems)


def attend_back_step(step, text, mem, q, k, v, att, logs, mark_q, mark_k, g_low, w_out,
                     w_q, w_k, w_v, sums_two, sums_in, scalars,
                     mine_out, theirs_out, packed_out, g_rows, rows_turned, sums,
                         grads, sems):
    core = scalars[0, 1]
    split = text.shape[0]
    count = split + mem.shape[0]
    width = text.shape[1]
    query, key, value, attended = q[...], k[...], v[...], att[...]

    def put(half, start, part):
        rows = pl.ds(pl.multiple_of(start, 16), part.shape[0])
        grads[jnp.where(core == half, 0, 1), rows, :] = part

    blocks = width // 128
    group_rows = grads.shape[1] // 2
    piece_rows = group_rows // 2

    def start_of(group, block):
        piece = block // (blocks // 2)
        return group * group_rows + piece * piece_rows + block % (blocks // 2) * width

    grad_w_out = dot_tn(attended, g_low[...]).astype(BF16)
    for block in range(blocks):
        part = grad_w_out[:, 128 * block : 128 * block + 128]
        put(1, start_of(1, block) + 256 * step, part)
    g_att = dot_nt(g_low[...], w_out[...])
    g_att_low = g_att.astype(BF16)
    scaled = query * jnp.asarray(0.125, BF16)
    product = g_att_low.astype(F32) * attended.astype(F32)
    lane = lanes_of((count, 128))
    none = jnp.asarray(0, BF16)
    thirds = ((lane >= 4) & (lane < 7)).astype(BF16)
    mq, mk = mark_q[...], mark_k[...] + thirds
    log_all = logs[...]

    def extra(column, base):
        high, middle, low = split_three(-column)
        wide = jnp.where(lane == 4, high, jnp.where(lane == 5, middle, low))
        return jnp.where((lane >= 4) & (lane < 7), wide, base)

    g_querys, g_keys, g_values = [], [], []
    for pair in range(2):
        span = slice(128 * pair, 128 * pair + 128)
        key_pair = key[:, span]
        key_wide = jnp.concatenate([key_pair, mk], axis=1)
        value_wide = jnp.concatenate([value[:, span], thirds], axis=1)
        key_turned = key_pair.astype(F32).T
        turned = lax.broadcasted_iota(jnp.int32, key_turned.shape, 0)
        g_query = g_key = g_value = None
        for side in range(2):
            own = lane // 64 == side
            mine = jnp.where(own, scaled[:, span], none)
            head = 4 * step + 2 * pair + side
            log_own = jnp.sum(jnp.where(lane == head, log_all, 0.0), axis=1, keepdims=True)
            query_wide = jnp.concatenate([mine, extra(log_own, mq)], axis=1)
            probs = jnp.exp(dot_nt(key_wide, query_wide))
            g_mine = jnp.where(own, g_att_low[:, span], none)
            delta = jnp.sum(jnp.where(own, product[:, span], 0.0), axis=1, keepdims=True)
            g_wide = jnp.concatenate([g_mine, extra(delta, jnp.zeros_like(mq))], axis=1)
            g_scores = (probs * dot_nt(value_wide, g_wide)).astype(BF16)
            part_v = dot(probs.astype(BF16), g_mine)
            part_k = dot(g_scores, mine)
            turned_own = jnp.where(turned // 64 == side, key_turned, 0.0).astype(BF16)
            part_q = dot(turned_own, g_scores)
            if side == 0:
                g_query, g_key, g_value = part_q, part_k, part_v
            else:
                g_query, g_key, g_value = g_query + part_q, g_key + part_k, g_value + part_v
        g_querys.append(g_query.T * 0.125)
        g_keys.append(g_key)
        g_values.append(g_value)
    g_query = jnp.concatenate(g_querys, axis=1)
    g_key = jnp.concatenate(g_keys, axis=1)
    g_value = jnp.concatenate(g_values, axis=1)
    columns = pl.ds(pl.multiple_of(256 * step, 256), 256)
    first = sums.shape[0] - 12
    sums[first : first + 1, columns] = column_sum(g_query)
    sums[first + 1 : first + 2, columns] = column_sum(g_value)
    total = g_rows[...]
    for place, (grad, weight) in enumerate(((g_query, w_q), (g_key, w_k), (g_value, w_v))):
        low = grad.astype(BF16)
        grad_w = dot(rows_turned[...], low).astype(BF16)
        for block in range(2):
            part = grad_w[:, 128 * block : 128 * block + 128]
            put(place // 2, start_of(place % 2, 2 * step + block), part)
        total += dot_nt(low, weight[...])
    g_rows[...] = total

    @pl.when(step == 2)
    def _():
        reset = scalars[0, 0] == 1
        g_mem = total[split:]
        zero = jnp.zeros_like(g_mem)
        g_kept = jnp.where(reset, zero, g_mem)
        g_all = jnp.concatenate([total[:split], g_kept], axis=0).astype(BF16)
        pack_rows(packed_out, g_all, split, packed_out.shape[1] // 2)
        first = sums.shape[0] - 12
        sums[first + 5 : first + 8, :] = sums_two[0:3, :]
        for place in range(4):
            sums[first + 8 + place : first + 9 + place, :] = sums_in[0:1, place * width : (place + 1) * width]
        mem_count = sums.shape[0] - 12
        sums[0:mem_count, :] = jnp.where(reset, g_mem, zero)[0:mem_count]
        small = sums[...].astype(BF16)
        base = blocks // 2 * width
        empty = jnp.zeros((SPARE_ROWS, 128), BF16)
        for place in range(4):
            rows = slice(place * piece_rows + base, (place + 1) * piece_rows)
            grads[0, rows, :] = empty
            grads[1, rows, :] = empty
        for place in range(2):
            for block in range(blocks):
                start = place * piece_rows + base + block * small.shape[0]
                put(0, start, small[:, 128 * block : 128 * block + 128])
        theirs = pltpu.make_async_copy(grads.at[1], theirs_out, sems.at[1])
        mine = pltpu.make_async_copy(grads.at[0], mine_out, sems.at[0])
        theirs.start()
        mine.start()
        theirs.wait()
        mine.wait()


def backward(g_two, g_inner, w_in, resid, lines, text, mem, q, k, v, att, logs, mark_q, mark_k,
             w_out, w_qkv, sums_two, sums_in, scalars, result):
    width = text.shape[1]
    count = text.shape[0] + mem.shape[0]
    chunk = 2 * width
    parts = w_in.shape[1] // chunk
    whole = lambda shape: pl.BlockSpec(shape, lambda j: (0,) * len(shape))
    early = lambda height: pl.BlockSpec((height, chunk), lambda j: (0, jnp.minimum(j, parts - 1)))
    quad = lambda j: jnp.maximum(j - parts, 0)
    cols = lambda height, base: pl.BlockSpec((height, 256), lambda j: (0, base + quad(j)))
    full = whole((count, width))
    mark = whole((count, 128))
    height = 2 * (width // 128 * width + 2 * SPARE_ROWS)
    half = jax.ShapeDtypeStruct((height, 128), BF16)
    packed = (result.shape[0], 2 * result.shape[1], width)
    return pl.pallas_call(
        backward_kernel,
        grid=(parts + 3,),
        in_specs=[
            full,
            early(count),
            early(width),
            full,
            whole(lines.shape),
            whole(text.shape),
            whole(mem.shape),
            cols(count, 0),
            cols(count, 0),
            cols(count, 0),
            cols(count, 0),
            mark,
            mark,
            mark,
            pl.BlockSpec((256, width), lambda j: (quad(j), 0)),
            cols(width, 0),
            cols(width, 3),
            cols(width, 6),
            whole(sums_two.shape),
            whole(sums_in.shape),
            pl.BlockSpec(memory_space=pltpu.SMEM),
            whole(result.shape),
        ],
        out_specs=[pl.BlockSpec(memory_space=pl.ANY)] * 2 + [whole(packed)],
        out_shape=[half, half, jax.ShapeDtypeStruct(packed, BF16)],
        scratch_shapes=[
            pltpu.VMEM((count, width), F32),
            pltpu.VMEM((count, width), BF16),
            pltpu.VMEM((width, count), BF16),
            pltpu.VMEM((count - text.shape[0] - ROW_PAD + 12, width), F32),
            pltpu.VMEM((2, height, 128), BF16),
            pltpu.SemaphoreType.DMA((2,)),
        ],
        compiler_params=pltpu.CompilerParams(vmem_limit_bytes=VMEM_ASK),
        cost_estimate=cost(33),
        name="backward",
    )(g_two, g_inner, w_in, resid, lines, text, mem, q, k, v, att, logs, mark_q, mark_k,
      w_out, w_qkv, w_qkv, w_qkv, sums_two, sums_in, scalars, result)


def widen_kernel(*refs):
    pieces, codes = refs[:4], refs[4]
    early = len(refs) == 10
    if early:
        qkv_out, out_out, small_out, wide, sems = refs[5:]
    else:
        qkv_out, out_out, wide, sems = refs[-4:]
    width = wide.shape[1]
    part = wide.shape[2]
    blocks = part // 128

    def copies(place):
        code = codes[0, place]
        in_qkv = code < 6
        columns = pl.ds(pl.multiple_of(jnp.minimum(code, 5) * part, part), part)
        to_qkv = pltpu.make_async_copy(wide.at[place], qkv_out.at[:, columns], sems.at[place])
        columns = pl.ds(pl.multiple_of(jnp.maximum(code - 6, 0) * part, part), part)
        to_out = pltpu.make_async_copy(wide.at[place], out_out.at[:, columns], sems.at[place])
        return in_qkv, to_qkv, to_out

    for place, piece in enumerate(pieces):
        for block in range(blocks):
            rows = slice(block * width, (block + 1) * width)
            wide[place, :, 128 * block : 128 * block + 128] = piece[rows, :].astype(F32)
        in_qkv, to_qkv, to_out = copies(place)

        if early:

            @pl.when(codes[0, place] < 2)
            def _():
                height = small_out.shape[0]
                for block in range(2 * blocks):
                    start = blocks * width + block * height
                    rows = piece[start : start + height, :].astype(F32)
                    small_out[:, 128 * block : 128 * block + 128] = rows

        @pl.when(in_qkv)
        def _():
            to_qkv.start()

        @pl.when(jnp.logical_not(in_qkv))
        def _():
            to_out.start()

    for place in range(4):
        in_qkv, to_qkv, to_out = copies(place)

        @pl.when(in_qkv)
        def _():
            to_qkv.wait()

        @pl.when(jnp.logical_not(in_qkv))
        def _():
            to_out.wait()


def widen(pieces, codes, width, small_count, partly=()):
    vmem = pl.BlockSpec(memory_space=pltpu.VMEM)
    hbm = pl.BlockSpec(memory_space=pl.ANY)
    return pl.pallas_call(
        widen_kernel,
        in_specs=[vmem] * 4 + [pl.BlockSpec(memory_space=pltpu.SMEM)] + [hbm] * len(partly),
        out_specs=[hbm, hbm] + ([] if partly else [vmem]),
        out_shape=[
            jax.ShapeDtypeStruct((width, 3 * width), F32),
            jax.ShapeDtypeStruct((width, width), F32),
        ]
        + ([] if partly else [jax.ShapeDtypeStruct((small_count, width), F32)]),
        scratch_shapes=[pltpu.VMEM((4, width, width // 2), F32), pltpu.SemaphoreType.DMA((4,))],
        input_output_aliases={5: 0, 6: 1} if partly else {},
        compiler_params=pltpu.CompilerParams(vmem_limit_bytes=VMEM_ASK),
        cost_estimate=cost(4),
        name="widen",
    )(*pieces, codes, *partly)


def widen_feed_kernel(down, inward, down_out, in_out, low, high, in_sems, out_sems):
    count, width = inward.shape[0], inward.shape[2]
    low_rows = low.shape[1]
    cut = width // low_rows
    places = []
    for part in range(count):
        for piece in range(cut):
            rows = pl.ds(piece * low_rows, low_rows)
            tall = pl.ds(part * width + piece * low_rows, low_rows)
            columns = pl.ds(part * width, width)
            places.append((inward.at[part, rows], in_out.at[rows, columns]))
            places.append((down.at[tall], down_out.at[tall]))
    fetches, sends = [], []
    for place, (source, target) in enumerate(places):
        fetches.append(pltpu.make_async_copy(source, low.at[place], in_sems.at[place]))
        sends.append(pltpu.make_async_copy(high.at[place], target, out_sems.at[place]))
        fetches[-1].start()
    for place in range(len(places)):
        fetches[place].wait()
        high[place] = low[place].astype(F32)
        sends[place].start()
    for send in sends:
        send.wait()


def widen_feed(down, inward):
    count, height, width = inward.shape
    cut = 2
    blocks = 2 * count * cut
    hbm = pl.BlockSpec(memory_space=pl.ANY)
    return pl.pallas_call(
        widen_feed_kernel,
        in_specs=[hbm, hbm],
        out_specs=[hbm, hbm],
        out_shape=[
            jax.ShapeDtypeStruct(down.shape, F32),
            jax.ShapeDtypeStruct((height, count * width), F32),
        ],
        scratch_shapes=[
            pltpu.VMEM((blocks, height // cut, width), BF16),
            pltpu.VMEM((blocks, height // cut, width), F32),
            pltpu.SemaphoreType.DMA((blocks,)),
            pltpu.SemaphoreType.DMA((blocks,)),
        ],
        compiler_params=pltpu.CompilerParams(vmem_limit_bytes=VMEM_ASK),
        cost_estimate=cost(9),
        name="widen_feed",
    )(down, inward)


def ring_partner(place, way):
    return place ^ 1 if way == 0 else 3 - place


def ring_pairs(step):
    pairs = []
    for place in range(4):
        for core in range(2):
            other = ring_partner(place, (step + core) % 2)
            pairs.append((2 * place + core, 2 * other + core))
    return pairs


def side_of(place, core, step):
    return jnp.where((step + core) % 2 == 0, (place + 1) // 2 % 2, place // 2)


def ring_side(axis, step):
    return side_of(lax.axis_index(axis), lax.axis_index("core"), step)


def ring_swap(value, axis, step):
    return lax.ppermute(value, (axis, "core"), ring_pairs(step))


def core_swap(value):
    return lax.ppermute(value, "core", [(0, 1), (1, 0)])


def add_pair(pair):
    return (pair[0].astype(F32) + pair[1].astype(F32)).astype(BF16)


def half_of(pair, side, start=0, rows=None):
    rows = pair[0].shape[-2] if rows is None else rows
    axis = pair[0].ndim - 2
    place = start + side * (rows // 2)
    return add_pair([lax.dynamic_slice_in_dim(part, place, rows // 2, axis) for part in pair])


def ring_halve(pair, axis, step, start=0, rows=None):
    side = ring_side(axis, step)
    got = ring_swap(half_of(pair, 1 - side, start, rows), axis, step)
    return half_of(pair, side, start, rows), got


def ring_join(value, axis, step):
    got = ring_swap(value, axis, step)
    return jnp.where(
        ring_side(axis, step) == 0,
        jnp.concatenate([value, got], axis=-2),
        jnp.concatenate([got, value], axis=-2),
    )


def to_segments(value):
    return lax.all_to_all(value, BLK, 0, 1, tiled=True)[0]


def after(value, other):
    return lax.optimization_barrier((value, other))[0]


def doc_marks(docs, mem_count):
    kinds = (docs[:, None] == jnp.arange(3)[None]).astype(F32)
    rest = mem_count + ROW_PAD
    total = docs.shape[0] + rest
    spare = (jnp.arange(total) >= total - ROW_PAD).astype(F32)[:, None]
    query = jnp.concatenate([jnp.pad(kinds, ((0, rest), (0, 0))), jnp.ones((total, 1), F32)], 1)
    key = jnp.concatenate([jnp.pad(kinds - 1.0, ((0, rest), (0, 0))), -spare], 1) * BAN
    fill = ((0, 0), (0, 128 - query.shape[1]))
    return jnp.pad(query, fill).astype(BF16), jnp.pad(key, fill).astype(BF16)


def local(
    tokens,
    memory,
    mem_init,
    reset_flags,
    doc_ids,
    w_qkv,
    b_query,
    b_value,
    w_out,
    b_out,
    norm1_gain,
    norm1_bias,
    w_in,
    b_in,
    w_down,
    b_down,
    norm2_gain,
    norm2_bias,
    out_cot,
    mem_cot,
):
    seg_count, tok_count, width = tokens.shape
    mem_count = memory.shape[1]
    place = lax.axis_index(BLK)
    pick = lambda value: lax.dynamic_index_in_dim(value, place, 0, keepdims=False)
    fill = lambda value: jnp.pad(value, ((0, ROW_PAD), (0, 0)))
    packed = (seg_count, tok_count + mem_count + ROW_PAD, width)
    my_flag = pick(reset_flags)
    mark_q, mark_k = doc_marks(pick(doc_ids), mem_count)
    mem = fill(jnp.where(my_flag == 1, mem_init, pick(memory)))
    cot_mem = fill(pick(mem_cot))
    text = to_segments(tokens)
    cot_text = to_segments(after(out_cot, text))

    lines = jnp.concatenate(
        [b_query, b_value, b_out, norm1_gain, norm1_bias, b_down, norm2_gain, norm2_bias, b_in]
    )
    lines = jnp.pad(lines.astype(F32).reshape(-1, width), ((0, 4), (0, 0)))
    q, k, v, att, logs, resid = attend(text, mem, w_qkv, lines, mark_q, mark_k, w_out)
    result, g_two, g_inner, sums_two, sums_in, grad_down, grad_in = feed(
        resid, lines, w_in, w_down, cot_text, cot_mem, packed
    )
    grad_down, grad_in = lax.psum((grad_down, grad_in), ALL)
    scalars = jnp.stack([my_flag, lax.axis_index("core")]).reshape(1, 2).astype(jnp.int32)
    small_count = mem_count + 12

    def attention_back(operands):
        result, g_two, g_inner, sums_two, sums_in = operands
        mine, theirs, g_packed = backward(
            g_two,
            g_inner,
            w_in,
            resid,
            lines,
            text,
            mem,
            q,
            k,
            v,
            att,
            logs,
            mark_q,
            mark_k,
            w_out,
            w_qkv,
            sums_two,
            sums_in,
            scalars,
            result,
        )
        pair = (mine, core_swap(theirs))
        rows = mine.shape[0] // 2
        over_z = ring_halve(pair, "z", 0, 0, rows)
        over_x = ring_halve(pair, "x", 0, rows, rows)
        over_z = ring_halve(over_z, "z", 1)
        over_x = ring_halve(over_x, "x", 1)
        both = lax.all_to_all(after(g_packed, over_z[0]), BLK, 0, 0, tiled=True)
        side = ring_side("y", 0)
        got = ring_swap(jnp.stack([half_of(over_z, 1 - side), half_of(over_x, 1 - side)]), "y", 0)
        pair = (jnp.stack([half_of(over_z, side), half_of(over_x, side)]), got)
        pair = ring_halve(pair, "y", 1)
        over_z, over_x = add_pair([part[0] for part in pair]), add_pair([part[1] for part in pair])
        for step in (0, 1):
            got_z, got_x = ring_swap(over_z, "x", step), ring_swap(over_x, "z", step)
            over_z, over_x = add_pair((over_z, got_z)), add_pair((over_x, got_x))
        joined = after(jnp.stack([over_z, over_x]), both)
        for step in (1, 0):
            joined = ring_join(joined, "y", step)
        over_z = ring_join(joined[0], "z", 1)
        over_x = ring_join(joined[1], "x", 1)
        pieces = []
        for base in (0, result.shape[1]):
            pieces.append(both[:, base : base + tok_count])
            pieces.append(both[:, base + tok_count : base + tok_count + mem_count])
        over_z, over_x = after((over_z, over_x), tuple(pieces))
        far = [ring_swap(over_z, "z", 0), ring_swap(over_x, "x", 0)]
        near = [core_swap(over_z), core_swap(over_x)]
        core = lax.axis_index("core")
        codes = []
        for where in (core, 1 - core):
            for group, axis in enumerate(("z", "x")):
                codes.append(4 * where + 2 * group + side_of(lax.axis_index(axis), where, 0))
        codes = jnp.stack(codes).astype(jnp.int32).reshape(1, 4)
        *wide, small = widen([over_z, over_x, *near], codes, width, small_count)
        start = mem_count
        vectors = [small[start + row] for row in range(8)]
        bin_rows = w_in.shape[1] // width
        vectors.append(small[start + 8 : start + 8 + bin_rows].reshape(-1))
        vectors.append(small[:mem_count])
        far, wide, vectors = lax.optimization_barrier((far, wide, vectors))
        far = [*far, core_swap(far[0]), core_swap(far[1])]
        wide = widen(far, codes ^ 1, width, small_count, wide)
        return *wide, *vectors, *pieces

    def nothing(operands):
        text_zero = jnp.zeros(tokens.shape, BF16)
        mem_zero = jnp.zeros(memory.shape, BF16)
        line = jnp.zeros((width,), F32)
        return (
            jnp.zeros(w_qkv.shape, F32),
            jnp.zeros(w_out.shape, F32),
            *[line] * 8,
            jnp.zeros(b_in.shape, F32),
            jnp.zeros(mem_init.shape, F32),
            text_zero,
            mem_zero,
            text_zero,
            mem_zero,
        )

    (
        grad_wqkv,
        grad_wout,
        grad_bquery,
        grad_bvalue,
        grad_gain1,
        grad_bias1,
        grad_bout,
        grad_gain2,
        grad_bias2,
        grad_bdown,
        grad_bin,
        grad_init,
        output,
        mem_output,
        grad_tokens,
        grad_memory,
    ) = lax.cond(
        reset_flags[0] >= 0, attention_back, nothing, (result, g_two, g_inner, sums_two, sums_in)
    )
    grad_down, grad_in = widen_feed(grad_down, grad_in)
    return (
        output,
        mem_output,
        grad_tokens,
        grad_memory,
        grad_init,
        grad_wqkv,
        grad_bquery,
        grad_bvalue,
        grad_wout,
        grad_bout,
        grad_gain1,
        grad_bias1,
        grad_in,
        grad_bin,
        grad_down,
        grad_bdown,
        grad_gain2,
        grad_bias2,
    )


def solution(mesh):
    chips = Mesh(mesh.devices.reshape(4, 4, 4, 2), ALL)
    placed = (
        P(SEG, BLK, None),
        P(SEG, None, None),
        P(),
        P(SEG),
        P(SEG, None),
        *([P()] * 13),
        P(SEG, BLK, None),
        P(SEG, None, None),
    )
    return jax.shard_map(
        local,
        mesh=chips,
        in_specs=placed,
        out_specs=(
            P(SEG, BLK, None),
            P(SEG, None, None),
            P(SEG, BLK, None),
            P(SEG, None, None),
            *([P()] * 14),
        ),
        check_vma=False,
    )
```
